32 devices in a mesh: wide: 16 (over z, y, core), narrow: 2 (over x).
Axes of the slice: x: 2, y: 2, z: 4, core: 2. Of those that a mesh axis runs over, the one named last changes fastest.
Arguments:
- text_in: bfloat16 [32, 64, 768], P(('wide', 'narrow')), may hold values from -6 to 6
- image_in: bfloat16 [32, 144, 1024], P(('wide', 'narrow')), may hold values from -6 to 6
- text_segments: int32 [32, 64], P(('wide', 'narrow')), may hold values from 0 to 1, as said below
- text_co_in: bfloat16 [1, 768, 3072], P(None, ('wide', 'narrow')), may hold values from -0.21875 to 0.21875
- text_co_out: bfloat16 [1, 1024, 768], P(None, ('wide', 'narrow')), may hold values from -1.5 to 1.5
- image_co_in: bfloat16 [1, 1024, 3072], P(None, ('wide', 'narrow')), may hold values from -0.1875 to 0.1875
- image_co_out: bfloat16 [1, 1024, 1024], P(None, ('wide', 'narrow')), may hold values from -1 to 1
- text_self_in: bfloat16 [1, 768, 2304], P(None, ('wide', 'narrow')), may hold values from -0.21875 to 0.21875
- text_self_out: bfloat16 [1, 768, 768], P(None, ('wide', 'narrow')), may hold values from -1.25 to 1.25
- image_self_in: bfloat16 [1, 1024, 3072], P(None, ('wide', 'narrow')), may hold values from -0.1875 to 0.1875
- image_self_out: bfloat16 [1, 1024, 1024], P(None, ('wide', 'narrow')), may hold values from -1.5 to 1.5
- text_up: bfloat16 [1, 2, 768, 3072], P(None, None, ('wide', 'narrow')), may hold values from -0.21875 to 0.21875
- text_down: bfloat16 [1, 2, 3072, 768], P(None, None, ('wide', 'narrow')), may hold values from -0.109375 to 0.109375
- image_up: bfloat16 [1, 2, 1024, 1024], P(None, None, ('wide', 'narrow')), may hold values from -0.1875 to 0.1875
- image_down: bfloat16 [1, 2, 1024, 1024], P(None, None, ('wide', 'narrow')), may hold values from -0.1875 to 0.1875
- text_gains: bfloat16 [1, 4, 768], P(None, None, ('wide', 'narrow')), may hold values from 0.5 to 1.5
- text_shifts: bfloat16 [1, 4, 768], P(None, None, ('wide', 'narrow')), may hold values from -1.1953125 to 1.1953125
- image_gains: bfloat16 [1, 4, 1024], P(None, None, ('wide', 'narrow')), may hold values from 0.5 to 1.5
- image_shifts: bfloat16 [1, 4, 1024], P(None, None, ('wide', 'narrow')), may hold values from -1.1953125 to 1.1953125
- grad_text_out: bfloat16 [32, 64, 768], P(('wide', 'narrow')), may hold values from -6 to 6
- grad_image_out: bfloat16 [32, 144, 1024], P(('wide', 'narrow')), may hold values from -6 to 6
Outputs:
- text_out: bfloat16 [32, 64, 768], P(('wide', 'narrow'))
- image_out: bfloat16 [32, 144, 1024], P(('wide', 'narrow'))
- text_in_grad: float32 [32, 64, 768], P(('wide', 'narrow'))
- image_in_grad: float32 [32, 144, 1024], P(('wide', 'narrow'))
- grad_text_co_in: float32 [1, 768, 3072], P(None, ('wide', 'narrow'))
- grad_text_co_out: float32 [1, 1024, 768], P(None, ('wide', 'narrow'))
- grad_image_co_in: float32 [1, 1024, 3072], P(None, ('wide', 'narrow'))
- grad_image_co_out: float32 [1, 1024, 1024], P(None, ('wide', 'narrow'))
- grad_text_self_in: float32 [1, 768, 2304], P(None, ('wide', 'narrow'))
- grad_text_self_out: float32 [1, 768, 768], P(None, ('wide', 'narrow'))
- grad_image_self_in: float32 [1, 1024, 3072], P(None, ('wide', 'narrow'))
- grad_image_self_out: float32 [1, 1024, 1024], P(None, ('wide', 'narrow'))
- grad_text_up: float32 [1, 2, 768, 3072], P(None, None, ('wide', 'narrow'))
- grad_text_down: float32 [1, 2, 3072, 768], P(None, None, ('wide', 'narrow'))
- grad_image_up: float32 [1, 2, 1024, 1024], P(None, None, ('wide', 'narrow'))
- grad_image_down: float32 [1, 2, 1024, 1024], P(None, None, ('wide', 'narrow'))
- grad_text_gains: float32 [1, 4, 768], P(None, None, ('wide', 'narrow'))
- grad_text_shifts: float32 [1, 4, 768], P(None, None, ('wide', 'narrow'))
- grad_image_gains: float32 [1, 4, 1024], P(None, None, ('wide', 'narrow'))
- grad_image_shifts: float32 [1, 4, 1024], P(None, None, ('wide', 'narrow'))
The draws below stay inside these ranges and needn't reach their ends.
Inputs may be any that keep to these rules, and one draw needn't show every extreme that they name: `text_segments`: in each row the text slots hold caption 0 and then caption 1, each of 8 slots or more.
All inputs are finite; a program needn't handle non-finite values.
Results may differ from the reference program's by a relative error of at most 0.024.
Values may be sent and summed in bfloat16 or wider, within the bound.
No kernel may reach another device: no remote copies, remote signals or barrier semaphores. Data moves between devices by JAX's collectives and lax.ppermute only.
A program may use at most 320 MiB of HBM per device.

```python
import jax
import jax.numpy as jnp
from jax import lax

DT = 768
DI = 1024
DC = 1024
HT = 12
HI = 8
HC = 8
FT = 3072
FI = 1024
LAYERS = 1
LT = 64
REGIONS = 36
LI = 144
ROWS = 32


def draw_text_segments(key, part):
    key = jax.random.fold_in(key, 7)
    boundary = jax.random.randint(key, (ROWS, 1), LT // 8, LT - LT // 8 + 1)
    position = jnp.arange(LT, dtype=jnp.int32)[None, :]
    return (position >= boundary).astype(jnp.int32)


def level_of(rng, shape, cuts, least, largest):
    factor_of = 1.0
    for dim, blocks in cuts:
        heights = jax.random.uniform(jax.random.fold_in(jax.random.fold_in(rng, 6), dim), (blocks,), jnp.float32, least / len(cuts), largest / len(cuts))
        factor_of = factor_of * jnp.repeat(jnp.exp(heights), shape[dim] // blocks).reshape((-1,) + (1,) * (len(shape) - 1 - dim))
    return factor_of


def scatter_about(rng, shape, width, reach, cuts=(), kind=jnp.bfloat16):
    result = jax.random.normal(rng, shape, jnp.float32) * width
    if len(cuts) > 0:
        result = level_of(rng, shape, cuts, -0.22, 0.18) * result
    return jnp.clip(result, min=-reach, max=reach).astype(kind)


def setup_inputs(seed: int = 0) -> dict:
    seeds = jax.random.split(jax.random.key(seed), 22)
    return {
        "text_in": scatter_about(seeds[0], (ROWS, LT, DT), 1.0, 6.0, ((0, 32),)),
        "image_in": scatter_about(seeds[1], (ROWS, LI, DI), 1.0, 6.0, ((0, 32),)),
        "text_segments": draw_text_segments(jax.random.fold_in(seeds[21], 71), 0),
        "text_co_in": scatter_about(seeds[3], (LAYERS, DT, 3 * DC), DT ** -0.5, 0.21875, ((1, 32),)),
        "text_co_out": scatter_about(seeds[4], (LAYERS, DC, DT), (max(1, DC // (2 * REGIONS))) ** -0.5, 1.5, ((1, 32),)),
        "image_co_in": scatter_about(seeds[5], (LAYERS, DI, 3 * DC), DI ** -0.5, 0.1875, ((1, 32),)),
        "image_co_out": scatter_about(seeds[6], (LAYERS, DC, DI), (max(1, DC // (LT // 2))) ** -0.5, 1.0, ((1, 32),)),
        "text_self_in": scatter_about(seeds[7], (LAYERS, DT, 3 * DT), DT ** -0.5, 0.21875, ((1, 32),)),
        "text_self_out": scatter_about(seeds[8], (LAYERS, DT, DT), (max(1, DT // (LT // 2))) ** -0.5, 1.25, ((1, 32),)),
        "image_self_in": scatter_about(seeds[9], (LAYERS, DI, 3 * DI), DI ** -0.5, 0.1875, ((1, 32),)),
        "image_self_out": scatter_about(seeds[10], (LAYERS, DI, DI), (max(1, DI // (2 * REGIONS))) ** -0.5, 1.5, ((1, 32),)),
        "text_up": scatter_about(seeds[11], (LAYERS, 2, DT, FT), DT ** -0.5, 0.21875, ((2, 32),)),
        "text_down": scatter_about(seeds[12], (LAYERS, 2, FT, DT), FT ** -0.5, 0.109375, ((2, 32),)),
        "image_up": scatter_about(seeds[13], (LAYERS, 2, DI, FI), DI ** -0.5, 0.1875, ((2, 32),)),
        "image_down": scatter_about(seeds[14], (LAYERS, 2, FI, DI), FI ** -0.5, 0.1875, ((2, 32),)),
        "text_gains": jnp.clip(1.0 + 0.1 * jax.random.normal(seeds[15], (LAYERS, 4, DT), jnp.float32), 0.5, 1.5).astype(jnp.bfloat16),
        "text_shifts": scatter_about(seeds[16], (LAYERS, 4, DT), 0.2, 1.1953125, ((2, 32),)),
        "image_gains": jnp.clip(1.0 + 0.1 * jax.random.normal(seeds[17], (LAYERS, 4, DI), jnp.float32), 0.5, 1.5).astype(jnp.bfloat16),
        "image_shifts": scatter_about(seeds[18], (LAYERS, 4, DI), 0.2, 1.1953125, ((2, 32),)),
        "grad_text_out": scatter_about(seeds[19], (ROWS, LT, DT), 1.0, 6.0, ((0, 32),)),
        "grad_image_out": scatter_about(seeds[20], (ROWS, LI, DI), 1.0, 6.0, ((0, 32),)),
    }


@jax.custom_vjp
def low(v):
    return lax.optimization_barrier(v.astype(jnp.bfloat16)).astype(jnp.float32)

@jax.custom_vjp
def low_back(v):
    return v

def low_keep(v):
    return (low(v), None)

def low_pass(kept, grad):
    return (grad,)

def back_keep(v):
    return (v, None)

def back_low(kept, grad):
    return (low(grad),)
low.defvjp(low_keep, low_pass)
low_back.defvjp(back_keep, back_low)
epsilon = 1e-06
precise = lax.Precision.HIGHEST

def matmul(values, weights):
    return jnp.einsum('rlk,km->rlm', values, weights, precision=precise)

def normalize(values, gains_row, offset):
    average = lax.optimization_barrier(jnp.mean(values, -1, keepdims=True))
    centred = values - average
    spread = lax.optimization_barrier(jnp.mean(centred * centred, -1, keepdims=True))
    return centred * lax.rsqrt(spread + epsilon) * gains_row + offset

def attend(queries, keys_in, values_in, allowed, head_count):
    row_count, length_q, width_all = queries.shape
    head_size = width_all // head_count
    query_heads = queries.reshape(row_count, length_q, head_count, head_size)
    key_heads = keys_in.reshape(row_count, keys_in.shape[1], head_count, head_size)
    value_heads = values_in.reshape(row_count, values_in.shape[1], head_count, head_size)
    scores = jnp.einsum('rqhd,rkhd->rhqk', query_heads, key_heads, precision=precise) * head_size ** (-0.5)
    scores = low_back(scores)
    scores = jnp.where(allowed[:, None], scores, -1e+30)
    probabilities = low(jax.nn.softmax(scores, axis=-1))
    context = jnp.einsum('rhqk,rkhd->rqhd', probabilities, value_heads, precision=precise)
    return low(low_back(context.reshape(row_count, length_q, width_all)))

def feed_forward(values, w_up, w_down, gains_row, offset):
    before = low_back(matmul(low(values), w_up))
    hidden = low(jax.nn.gelu(before, approximate=False))
    return normalize(values + low_back(matmul(hidden, w_down)), gains_row, offset)

def self_block(values, allowed, w_in, w_out, w_up, w_down, gains_rows, offsets, head_count):
    mixture = low(low_back(matmul(low(values), w_in)))
    queries, keys_in, values_in = jnp.split(mixture, 3, axis=-1)
    context = attend(queries, keys_in, values_in, allowed, head_count)
    middle = normalize(values + low_back(matmul(context, w_out)), gains_rows[0], offsets[0])
    return feed_forward(middle, w_up, w_down, gains_rows[1], offsets[1])

def co_block(text_state, image_state, cross, weights):
    text_in_w, text_out_w, image_in_w, image_out_w, text_up_w, text_down_w, image_up_w, image_down_w, text_gain, text_offset, image_gain, image_offset = weights
    text_mix = low(low_back(matmul(low(text_state), text_in_w)))
    image_mix = low(low_back(matmul(low(image_state), image_in_w)))
    text_query, text_keys, text_vals = jnp.split(text_mix, 3, axis=-1)
    image_query, image_keys, image_vals = jnp.split(image_mix, 3, axis=-1)
    text_ctx = attend(text_query, image_keys, image_vals, cross, HC)
    image_ctx = attend(image_query, text_keys, text_vals, jnp.swapaxes(cross, 1, 2), HC)
    text_mid = normalize(text_state + low_back(matmul(text_ctx, text_out_w)), text_gain[0], text_offset[0])
    image_mid = normalize(image_state + low_back(matmul(image_ctx, image_out_w)), image_gain[0], image_offset[0])
    text_top = feed_forward(text_mid, text_up_w, text_down_w, text_gain[1], text_offset[1])
    image_top = feed_forward(image_mid, image_up_w, image_down_w, image_gain[1], image_offset[1])
    return (text_top, image_top)

def forward_pass(text_state, image_state, segments, params):
    text_co_in, text_co_out, image_co_in, image_co_out, text_self_in, text_self_out, image_self_in, image_self_out, text_up, text_down, image_up, image_down, text_gains, text_shifts, image_gains, image_shifts = params
    image_ids = jnp.arange(LI, dtype=jnp.int32) // (2 * REGIONS)
    cross = segments[:, :, None] == image_ids[None, None, :]
    text_allowed = segments[:, :, None] == segments[:, None, :]
    image_allowed = (image_ids[:, None] == image_ids[None, :])[None]
    for layer_no in range(LAYERS):
        co_weights = (text_co_in[layer_no], text_co_out[layer_no], image_co_in[layer_no], image_co_out[layer_no], text_up[layer_no, 0], text_down[layer_no, 0], image_up[layer_no, 0], image_down[layer_no, 0], text_gains[layer_no, 0:2], text_shifts[layer_no, 0:2], image_gains[layer_no, 0:2], image_shifts[layer_no, 0:2])
        text_state, image_state = co_block(text_state, image_state, cross, co_weights)
        text_state = self_block(text_state, text_allowed, text_self_in[layer_no], text_self_out[layer_no], text_up[layer_no, 1], text_down[layer_no, 1], text_gains[layer_no, 2:4], text_shifts[layer_no, 2:4], HT)
        image_state = self_block(image_state, image_allowed, image_self_in[layer_no], image_self_out[layer_no], image_up[layer_no, 1], image_down[layer_no, 1], image_gains[layer_no, 2:4], image_shifts[layer_no, 2:4], HI)
    return (text_state, image_state)

def reference(text_in, image_in, text_segments, text_co_in, text_co_out, image_co_in, image_co_out, text_self_in, text_self_out, image_self_in, image_self_out, text_up, text_down, image_up, image_down, text_gains, text_shifts, image_gains, image_shifts, grad_text_out, grad_image_out):
    params = tuple((weight_in.astype(jnp.float32) for weight_in in (text_co_in, text_co_out, image_co_in, image_co_out, text_self_in, text_self_out, image_self_in, image_self_out, text_up, text_down, image_up, image_down, text_gains, text_shifts, image_gains, image_shifts)))
    groups = ROWS // 16

    def regroup(array):
        return array.reshape((groups, 16) + array.shape[1:])
    batches = (regroup(text_in.astype(jnp.float32)), regroup(image_in.astype(jnp.float32)), regroup(text_segments), regroup(grad_text_out.astype(jnp.float32)), regroup(grad_image_out.astype(jnp.float32)))

    def one_group(totals, batch):
        text_part, image_part, segment_part, text_cot, image_cot = batch
        outputs, pull_back = jax.vjp(lambda text_arg, image_arg, param_arg: forward_pass(text_arg, image_arg, segment_part, param_arg), text_part, image_part, params)
        text_grad, image_grad, param_grads = pull_back((text_cot, image_cot))
        totals = jax.tree.map(lambda left, right: left + right, totals, param_grads)
        return (totals, (outputs[0], outputs[1], text_grad, image_grad))
    zeros_init = jax.tree.map(jnp.zeros_like, params)
    totals, (text_top, image_top, text_grad, image_grad) = lax.scan(one_group, zeros_init, batches)

    def flatten(array):
        return array.reshape((ROWS,) + array.shape[2:])
    return (flatten(text_top).astype(jnp.bfloat16), flatten(image_top).astype(jnp.bfloat16), flatten(text_grad), flatten(image_grad), totals[0], totals[1], totals[2], totals[3], totals[4], totals[5], totals[6], totals[7], totals[8], totals[9], totals[10], totals[11], totals[12], totals[13], totals[14], totals[15])
```

```python
from functools import partial

import jax
import jax.numpy as jnp
from jax import lax
from jax.sharding import PartitionSpec as P

HT = 12
HI = 8
HC = 8
REGIONS = 36
AXES = ("wide", "narrow")
EPS = 1e-06
F32 = jnp.float32
BF16 = jnp.bfloat16


class Grid:
    def __init__(self, wide, narrow):
        self.depth = wide // 4
        self.narrow = narrow
        self.count = wide * narrow
        w = lax.axis_index("wide")
        self.x = lax.axis_index("narrow")
        self.core = w % 2
        self.y = (w // 2) % 2
        self.z = w // 4

    def split(self, i):
        x = i % self.narrow
        i = i // self.narrow
        return i // 4, (i // 2) % 2, i % 2, x

    def join(self, z, y, c, x):
        return ((z * 2 + y) * 2 + c) * self.narrow + x

    def move(self, value, to):
        pairs = [(i, self.join(*to(*self.split(i)))) for i in range(self.count)]
        return lax.ppermute(value, AXES, pairs)

    def to_core(self, value):
        return self.move(value, lambda z, y, c, x: (z, y, 1 - c, x))

    def to_x(self, value):
        return self.move(value, lambda z, y, c, x: (z, y, c, 1 - x))

    def to_y(self, value):
        return self.move(value, lambda z, y, c, x: (z, 1 - y, c, x))

    def to_z(self, value, step):
        return self.move(value, lambda z, y, c, x: ((z + step) % self.depth, y, c, x))

    def swap_half(self, value):
        half = self.depth // 2
        return self.move(value, lambda z, y, c, x: (c * half + z % half, y, z // half, x))


def pick(value, index, axis):
    return lax.dynamic_index_in_dim(value, index, axis, keepdims=False)


def paired(own, other, index, axis):
    low = jnp.expand_dims(jnp.where(index == 0, own, other), axis)
    high = jnp.expand_dims(jnp.where(index == 0, other, own), axis)
    return jnp.concatenate([low, high], axis)


def halves(width, groups):
    return groups, 2, width // groups // 2


def chunk_in(grid, w, groups):
    r, n = w.shape
    parts = w.reshape((r,) + halves(n, groups))
    keep = pick(parts, grid.core, 2).reshape(r, n // 2)
    give = pick(parts, 1 - grid.core, 2).reshape(r, n // 2)
    return paired(keep, grid.to_core(give), grid.core, 0)


def chunk_out(grid, mats):
    joined = jnp.concatenate(mats, 0) if len(mats) > 1 else mats[0]
    return grid.swap_half(joined)[None]


def gather_z(grid, chunk):
    got = [chunk] + [grid.to_z(chunk, k) for k in range(1, grid.depth)]
    places = []
    for place in range(grid.depth):
        value = got[0]
        for k in range(1, grid.depth):
            value = jnp.where((grid.z - place) % grid.depth == k, got[k], value)
        places.append(value)
    return jnp.stack(places)


def gather_plane(grid, block, order):
    if order == "xy":
        both = paired(block, grid.to_x(block), grid.x, 2)
        return paired(both, grid.to_y(both), grid.y, 1)
    both = paired(block, grid.to_y(block), grid.y, 1)
    return paired(both, grid.to_x(both), grid.x, 3)


def finish_in(full):
    return full.reshape(-1, full.shape[-1])


def finish_out(grid, full, rows):
    z, _, p, _, r, c = full.shape
    full = full.reshape(2, z // 2, 2, 2, r, c).transpose(1, 2, 0, 3, 4, 5)
    out, at = [], 0
    for count in rows:
        out.append(full[..., at : at + count, :].reshape(-1, c))
        at += count
    return out


def add_low(a, b):
    return (a.astype(F32) + b.astype(F32)).astype(BF16)


def reduce_plane(grid, view, order):
    if order == "xy":
        got = grid.to_y(pick(view, 1 - grid.y, 1))
        both = add_low(pick(view, grid.y, 1), got)
        got = grid.to_x(pick(both, 1 - grid.x, 2))
        return add_low(pick(both, grid.x, 2), got)
    got = grid.to_x(pick(view, 1 - grid.x, 3))
    both = add_low(pick(view, grid.x, 3), got)
    got = grid.to_y(pick(both, 1 - grid.y, 1))
    return add_low(pick(both, grid.y, 1), got)


def reduce_z(grid, block):
    total = pick(block, grid.z, 0).astype(F32)
    for k in range(1, grid.depth):
        give = pick(block, (grid.z + k) % grid.depth, 0)
        total = total + grid.to_z(give, k).astype(F32)
    return total


def return_in(grid, grad, groups, order):
    k, c = grad.shape
    view = grad.reshape(grid.depth, 2, 2, 2, k // grid.count, c)
    total = reduce_z(grid, reduce_plane(grid, view, order))
    keep = pick(total, grid.core, 0)
    got = grid.to_core(pick(total, 1 - grid.core, 0).astype(BF16)).astype(F32)
    r = keep.shape[0]
    shape = (r, groups, c // groups)
    return paired(keep.reshape(shape), got.reshape(shape), grid.core, 2).reshape(r, 2 * c)


def return_out(grid, grads, order):
    half = grid.depth // 2
    views = []
    for grad in grads:
        k, c = grad.shape
        view = grad.reshape(half, 2, 2, 2, 2 * k // grid.count, c).transpose(2, 0, 1, 3, 4, 5)
        views.append(view.reshape(grid.depth, 2, 1, 2, 2 * k // grid.count, c))
    view = jnp.concatenate(views, 4) if len(views) > 1 else views[0]
    total = reduce_z(grid, reduce_plane(grid, view, order))[0]
    total = grid.swap_half(total.astype(BF16)).astype(F32)
    out, at = [], 0
    for view in views:
        out.append(total[at : at + view.shape[4]])
        at += view.shape[4]
    return out


def gather_norms(grid, packed):
    both = paired(packed[None], grid.to_core(packed[None]), grid.core, 0)
    full = gather_plane(grid, gather_z(grid, both), "xy")
    return full.reshape(grid.count, packed.shape[0])


def reduce_norms(grid, packed):
    view = packed.reshape(grid.depth, 2, 2, 2, 1, packed.shape[1])
    view = pick(view, grid.core, 2) + grid.to_core(pick(view, 1 - grid.core, 2))
    view = pick(view, grid.y, 1) + grid.to_y(pick(view, 1 - grid.y, 1))
    view = pick(view, grid.x, 1) + grid.to_x(pick(view, 1 - grid.x, 1))
    return reduce_z(grid, view)[0]


def dot(a, b):
    return jnp.einsum("rlk,km->rlm", a, b, preferred_element_type=F32)


def dot_back(a, b):
    return jnp.einsum("rlm,km->rlk", a, b, preferred_element_type=F32)


def dot_weight(a, b):
    return jnp.einsum("rlk,rlm->km", a, b, preferred_element_type=F32).astype(BF16)


def layer_norm(values, gain, shift):
    average = jnp.mean(values, -1, keepdims=True)
    centred = values - average
    inverse = lax.rsqrt(jnp.mean(centred * centred, -1, keepdims=True) + EPS)
    normed = centred * inverse
    return normed * gain + shift, (normed, inverse)


def norm_back(upstream, stored, gain):
    normed, inverse = stored
    scaled = upstream * gain
    grad = inverse * (
        scaled
        - jnp.mean(scaled, -1, keepdims=True)
        - normed * jnp.mean(scaled * normed, -1, keepdims=True)
    )
    return grad, jnp.sum(upstream * normed, axis=0), jnp.sum(upstream, axis=0)


def heads_of(array, count):
    return array.reshape(array.shape[0], array.shape[1], count, array.shape[2] // count)


def attend(q, k, v, allowed, count):
    rows, length, width = q.shape
    factor = (width // count) ** (-0.5)
    qh, kh, vh = heads_of(q, count), heads_of(k, count), heads_of(v, count)
    scores = jnp.einsum("rqhd,rkhd->rhqk", qh, kh, preferred_element_type=F32) * factor
    scores = jnp.where(allowed[:, None], scores, -1e30)
    exponent = jnp.exp(scores - jnp.max(scores, -1, keepdims=True))
    probs = exponent / jnp.sum(exponent, -1, keepdims=True)
    context = jnp.einsum("rhqk,rkhd->rqhd", probs.astype(BF16), vh, preferred_element_type=F32)
    return context.reshape(rows, length, width).astype(BF16), probs


def attend_back(grad, q, k, v, probs, count):
    rows, length, width = q.shape
    factor = (width // count) ** (-0.5)
    qh, kh, vh, gh = (heads_of(a, count) for a in (q, k, v, grad))
    dv = jnp.einsum("rhqk,rqhd->rkhd", probs.astype(BF16), gh, preferred_element_type=F32)
    dp = jnp.einsum("rqhd,rkhd->rhqk", gh, vh, preferred_element_type=F32)
    ds = (probs * (dp - jnp.sum(dp * probs, -1, keepdims=True))).astype(BF16)
    dq = jnp.einsum("rhqk,rkhd->rqhd", ds, kh, preferred_element_type=F32) * factor
    dk = jnp.einsum("rhqk,rqhd->rkhd", ds, qh, preferred_element_type=F32) * factor
    flat = lambda a: a.reshape(a.shape[0], a.shape[1], width).astype(BF16)
    return flat(dq), flat(dk), flat(dv)


def share(grid, own):
    return jnp.stack([own, grid.to_core(own)])


def settle(grid, partial_sums):
    return partial_sums[0] + grid.to_core(partial_sums[1])


def project(low, w):
    return jnp.split(dot(low, w).astype(BF16), 3, axis=-1)


def attn_out(grid, values, context, w, gain, shift):
    result, stored = layer_norm(values + settle(grid, dot(context, w)), gain, shift)
    return result, stored


def feed_forward(grid, values, up, down, gain, shift):
    low = share(grid, values.astype(BF16))
    before = dot(low, up)
    hidden = jax.nn.gelu(before, approximate=False).astype(BF16)
    result, stored = layer_norm(values + settle(grid, dot(hidden, down)), gain, shift)
    return result, (low, before, hidden, stored)


def feed_back(grid, upstream, saved, up, down, gain):
    low, before, hidden, stored = saved
    summed, dgain, dshift = norm_back(upstream, stored, gain)
    out = share(grid, summed.astype(BF16))
    hidden_grad = dot_back(out, down)
    _, pull = jax.vjp(partial(jax.nn.gelu, approximate=False), before)
    before_grad = pull(hidden_grad)[0].astype(BF16)
    entry = settle(grid, dot_back(before_grad, up))
    ddown = dot_weight(hidden, out)
    dup = dot_weight(low, before_grad)
    return summed + entry, dup, ddown, dgain, dshift


def attn_out_back(grid, upstream, context, stored, w, gain):
    summed, dgain, dshift = norm_back(upstream, stored, gain)
    out = share(grid, summed.astype(BF16))
    context_grad = dot_back(out, w).astype(BF16)
    return summed, context_grad, dot_weight(context, out), dgain, dshift


def project_back(grid, low, grads, w):
    joined = jnp.concatenate(grads, axis=-1)
    return settle(grid, dot_back(joined, w)), dot_weight(low, joined)


def pack_norms(text_gains, text_shifts, image_gains, image_shifts):
    return jnp.concatenate([a.reshape(-1) for a in (text_gains, text_shifts, image_gains, image_shifts)])


def unpack_norms(full, tw, iw):
    out, at = [], 0
    for width in (tw, tw, iw, iw):
        part = full[:, at : at + 4 * width].reshape(-1, 4, width)
        out.append(part.transpose(1, 0, 2).reshape(4, -1).astype(F32))
        at += 4 * width
    return out


def shards(
    wide,
    narrow,
    text_in,
    image_in,
    text_segments,
    text_co_in,
    text_co_out,
    image_co_in,
    image_co_out,
    text_self_in,
    text_self_out,
    image_self_in,
    image_self_out,
    text_up,
    text_down,
    image_up,
    image_down,
    text_gains,
    text_shifts,
    image_gains,
    image_shifts,
    grad_text_out,
    grad_image_out,
):
    grid = Grid(wide, narrow)
    tw, iw = text_gains.shape[2], image_gains.shape[2]

    norms = gather_norms(
        grid, pack_norms(text_gains[0], text_shifts[0], image_gains[0], image_shifts[0])
    )
    gain_t, shift_t, gain_i, shift_i = unpack_norms(norms, tw, iw)

    specs = [
        ("tci", "in", [text_co_in[0]], 3, "xy"),
        ("ici", "in", [image_co_in[0]], 3, "yx"),
        ("to0", "out", [text_co_out[0], text_down[0, 0]], 1, "xy"),
        ("tu0", "in", [text_up[0, 0]], 1, "yx"),
        ("io0", "out", [image_co_out[0], image_down[0, 0]], 1, "xy"),
        ("iu0", "in", [image_up[0, 0]], 1, "yx"),
        ("tsi", "in", [text_self_in[0]], 3, "yx"),
        ("isi", "in", [image_self_in[0]], 3, "xy"),
        ("to1", "out", [text_self_out[0], text_down[0, 1]], 1, "yx"),
        ("tu1", "in", [text_up[0, 1]], 1, "xy"),
        ("io1", "out", [image_self_out[0], image_down[0, 1]], 1, "yx"),
        ("iu1", "in", [image_up[0, 1]], 1, "xy"),
    ]
    full = {}
    order_of = {}
    blocks = []
    for name, kind, mats, groups, order in specs:
        chunk = chunk_in(grid, mats[0], groups) if kind == "in" else chunk_out(grid, mats)
        if len(blocks) >= 2:
            chunk, _ = lax.optimization_barrier((chunk, blocks[-2]))
        block = gather_z(grid, chunk)
        blocks.append(block)
        whole = gather_plane(grid, block, order)
        order_of[name] = order
        if kind == "in":
            full[name] = finish_in(whole)
        else:
            full[name] = finish_out(grid, whole, [m.shape[0] for m in mats])
    tco, td0 = full["to0"]
    ico, id0 = full["io0"]
    tso, td1 = full["to1"]
    iso, id1 = full["io1"]

    segments = share(grid, text_segments[0].astype(F32))
    image_ids = (jnp.arange(image_in.shape[1], dtype=jnp.int32) // (2 * REGIONS)).astype(F32)
    cross = segments[:, :, None] == image_ids[None, None, :]
    cross_back = jnp.swapaxes(cross, 1, 2)
    text_allowed = segments[:, :, None] == segments[:, None, :]
    image_allowed = (image_ids[:, None] == image_ids[None, :])[None]

    hc, ht, hi = HC // 2, HT // 2, HI // 2
    xt, xi = text_in[0].astype(F32), image_in[0].astype(F32)
    low_t, low_i = share(grid, text_in[0]), share(grid, image_in[0])
    qt, kt, vt = project(low_t, full["tci"])
    qi, ki, vi = project(low_i, full["ici"])
    ct, pt = attend(qt, ki, vi, cross, hc)
    ci, pi = attend(qi, kt, vt, cross_back, hc)
    yt, yt_saved = attn_out(grid, xt, ct, tco, gain_t[0], shift_t[0])
    yi, yi_saved = attn_out(grid, xi, ci, ico, gain_i[0], shift_i[0])
    zt, zt_saved = feed_forward(grid, yt, full["tu0"], td0, gain_t[1], shift_t[1])
    zi, zi_saved = feed_forward(grid, yi, full["iu0"], id0, gain_i[1], shift_i[1])

    def self_forward(values, w_in, w_out, up, down, allowed, count, gain, shift):
        low = share(grid, values.astype(BF16))
        q, k, v = project(low, w_in)
        context, probs = attend(q, k, v, allowed, count)
        middle, mid_saved = attn_out(grid, values, context, w_out, gain[2], shift[2])
        top, top_saved = feed_forward(grid, middle, up, down, gain[3], shift[3])
        return top, (low, q, k, v, context, probs, mid_saved, top_saved)

    ot, ot_saved = self_forward(
        zt, full["tsi"], tso, full["tu1"], td1, text_allowed, ht, gain_t, shift_t
    )
    oi, oi_saved = self_forward(
        zi, full["isi"], iso, full["iu1"], id1, image_allowed, hi, gain_i, shift_i
    )

    grads = {}

    def self_backward(upstream, saved, w_in, w_out, up, down, count, gain):
        low, q, k, v, context, probs, mid_saved, top_saved = saved
        middle, dup, ddown, dg3, db3 = feed_back(grid, upstream, top_saved, up, down, gain[3])
        residual, context_grad, dout, dg2, db2 = attn_out_back(
            grid, middle, context, mid_saved, w_out, gain[2]
        )
        joined = attend_back(context_grad, q, k, v, probs, count)
        entry, din = project_back(grid, low, joined, w_in)
        return residual + entry, din, dout, dup, ddown, (dg2, dg3), (db2, db3)

    gt, d_tsi, d_tso, d_tu1, d_td1, dgt_top, dbt_top = self_backward(
        grad_text_out[0].astype(F32), ot_saved, full["tsi"], tso, full["tu1"], td1, ht, gain_t
    )
    gi, d_isi, d_iso, d_iu1, d_id1, dgi_top, dbi_top = self_backward(
        grad_image_out[0].astype(F32), oi_saved, full["isi"], iso, full["iu1"], id1, hi, gain_i
    )

    gt, d_tu0, d_td0, dgt1, dbt1 = feed_back(grid, gt, zt_saved, full["tu0"], td0, gain_t[1])
    gi, d_iu0, d_id0, dgi1, dbi1 = feed_back(grid, gi, zi_saved, full["iu0"], id0, gain_i[1])
    rt, ct_grad, d_tco, dgt0, dbt0 = attn_out_back(grid, gt, ct, yt_saved, tco, gain_t[0])
    ri, ci_grad, d_ico, dgi0, dbi0 = attn_out_back(grid, gi, ci, yi_saved, ico, gain_i[0])
    dqt, dki, dvi = attend_back(ct_grad, qt, ki, vi, pt, hc)
    dqi, dkt, dvt = attend_back(ci_grad, qi, kt, vt, pi, hc)
    et, d_tci = project_back(grid, low_t, (dqt, dkt, dvt), full["tci"])
    ei, d_ici = project_back(grid, low_i, (dqi, dki, dvi), full["ici"])

    groups_of = {name: groups for name, _, _, groups, _ in specs}

    def give_in(name, grad):
        return return_in(grid, grad, groups_of[name], order_of[name])

    g_tu1 = give_in("tu1", d_tu1)
    g_iu1 = give_in("iu1", d_iu1)
    g_tso, g_td1 = return_out(grid, [d_tso, d_td1], order_of["to1"])
    g_iso, g_id1 = return_out(grid, [d_iso, d_id1], order_of["io1"])
    g_tsi = give_in("tsi", d_tsi)
    g_isi = give_in("isi", d_isi)
    g_tu0 = give_in("tu0", d_tu0)
    g_iu0 = give_in("iu0", d_iu0)
    g_tco, g_td0 = return_out(grid, [d_tco, d_td0], order_of["to0"])
    g_ico, g_id0 = return_out(grid, [d_ico, d_id0], order_of["io0"])
    g_tci = give_in("tci", d_tci)
    g_ici = give_in("ici", d_ici)

    def by_device(rows, width):
        return jnp.stack(rows).reshape(4, grid.count, width).transpose(1, 0, 2).reshape(grid.count, 4 * width)

    sums = jnp.concatenate(
        [
            by_device([dgt0, dgt1, *dgt_top], tw),
            by_device([dbt0, dbt1, *dbt_top], tw),
            by_device([dgi0, dgi1, *dgi_top], iw),
            by_device([dbi0, dbi1, *dbi_top], iw),
        ],
        1,
    )
    own = reduce_norms(grid, sums)
    norm_grads, at = [], 0
    for width in (tw, tw, iw, iw):
        norm_grads.append(own[at : at + 4 * width].reshape(1, 4, width))
        at += 4 * width

    return (
        ot.astype(BF16)[None],
        oi.astype(BF16)[None],
        (rt + et)[None],
        (ri + ei)[None],
        g_tci[None],
        g_tco[None],
        g_ici[None],
        g_ico[None],
        g_tsi[None],
        g_tso[None],
        g_isi[None],
        g_iso[None],
        jnp.stack([g_tu0, g_tu1])[None],
        jnp.stack([g_td0, g_td1])[None],
        jnp.stack([g_iu0, g_iu1])[None],
        jnp.stack([g_id0, g_id1])[None],
        *norm_grads,
    )


def solution(mesh):
    rows = P(AXES, None, None)
    weight = P(None, AXES, None)
    pair = P(None, None, AXES, None)
    norm = P(None, None, AXES)
    return jax.shard_map(
        partial(shards, mesh.shape["wide"], mesh.shape["narrow"]),
        mesh=mesh,
        in_specs=(rows, rows, P(AXES, None), *[weight] * 8, *[pair] * 4, *[norm] * 4, rows, rows),
        out_specs=(rows, rows, rows, rows, *[weight] * 8, *[pair] * 4, *[norm] * 4),
        check_vma=False,
    )
```

```python
from functools import partial

import jax
import jax.numpy as jnp
from jax import lax
from jax.sharding import Mesh, PartitionSpec as P

HT = 12
HI = 8
HC = 8
REGIONS = 36
EPS = 1e-06
F32 = jnp.float32
BF16 = jnp.bfloat16
ALL = ("z", "y", "core", "x")
TEAM = 4
FLIP = ((0, 1), (1, 0))


class Grid:
    def __init__(self, depth):
        self.depth = depth
        self.low = depth // TEAM
        self.z, self.y, self.core, self.x = (lax.axis_index(name) for name in ALL)

    def to_core(self, value):
        return lax.ppermute(value, "core", FLIP)

    def to_x(self, value):
        return lax.ppermute(value, "x", FLIP)

    def to_y(self, value):
        return lax.ppermute(value, "y", FLIP)

    def to_z(self, value, step):
        return lax.ppermute(value, "z", [(z, (z + step) % self.depth) for z in range(self.depth)])

    def swap_team(self, value):
        pairs = []
        for high in range(TEAM):
            for low in range(self.low):
                for y in range(2):
                    for place in range(TEAM):
                        here = ((high * self.low + low) * 2 + y) * TEAM + place
                        there = ((place * self.low + low) * 2 + y) * TEAM + high
                        pairs.append((here, there))
        return lax.ppermute(value, ALL, pairs)


def pick(value, index, axis):
    return lax.dynamic_index_in_dim(value, index, axis, keepdims=False)


def paired(own, other, index, axis):
    own, other = jnp.expand_dims(own, axis), jnp.expand_dims(other, axis)
    shape = list(own.shape)
    shape[axis] = 2
    place = lax.broadcasted_iota(jnp.int32, shape, axis)
    return jnp.where(place == index, own, other)


def quarter(w, groups):
    r, n = w.shape
    parts = w.reshape(r, groups, TEAM, n // groups // TEAM)
    return parts.transpose(2, 0, 1, 3).reshape(2, 2, r, n // TEAM)


def unquarter(parts, groups):
    _, _, r, c = parts.shape
    parts = parts.reshape(TEAM, r, groups, c // groups)
    return parts.transpose(1, 2, 0, 3).reshape(r, TEAM * c)


def team_trade(grid, parts):
    got = grid.to_x(pick(parts, 1 - grid.x, 1))
    parts = paired(pick(parts, grid.x, 1), got, grid.x, 1)
    got = grid.to_core(pick(parts, 1 - grid.core, 0))
    return paired(pick(parts, grid.core, 0), got, grid.core, 0)


def widen(value, width):
    lack = width - value.shape[-1]
    if lack == 0:
        return value
    return jnp.pad(value, [(0, 0)] * (value.ndim - 1) + [(0, lack)])


class Bundle:
    def __init__(self, width, ins, outs, z_by, extra=0):
        self.width, self.ins, self.outs, self.z_by, self.extra = width, ins, outs, z_by, extra

    def flat(self, parts):
        c = parts.shape[-1]
        if c * TEAM == self.width:
            return jnp.concatenate([parts[..., k, :, :] for k in range(TEAM)], -1)
        parts = widen(parts, self.width)
        return parts.reshape(parts.shape[:-3] + (TEAM * parts.shape[-2], self.width))

    def unflat(self, rows, c):
        if c * TEAM == self.width:
            return jnp.stack([rows[..., k * c : (k + 1) * c] for k in range(TEAM)], -3)
        rows = rows.reshape(rows.shape[:-2] + (TEAM, rows.shape[-2] // TEAM, self.width))
        return rows[..., :c]


def gather(grid, bundle, weights, extra=None, after=None):
    pieces = []
    if bundle.ins:
        parts = [quarter(weights[name], groups) for name, groups in bundle.ins]
        kinds = {}
        for i, part in enumerate(parts):
            kinds.setdefault(part.shape[-1], []).append(i)
        traded = [None] * len(parts)
        for members in kinds.values():
            joined = jnp.concatenate([parts[i] for i in members], 2) if len(members) > 1 else parts[members[0]]
            joined = team_trade(grid, joined)
            at = 0
            for i in members:
                r = parts[i].shape[2]
                traded[i] = joined[:, :, at : at + r].reshape(TEAM, r, parts[i].shape[3])
                at += r
        pieces += [bundle.flat(t) for t in traded]
    if bundle.outs:
        outs = [weights[name] for name in bundle.outs]
        pieces.append(grid.swap_team(jnp.concatenate(outs, 0) if len(outs) > 1 else outs[0]))
    if extra is not None:
        lines = team_trade(grid, jnp.broadcast_to(extra, (2, 2) + extra.shape)).reshape(TEAM, -1)
        lines = jnp.pad(lines, ((0, bundle.extra - TEAM), (0, bundle.width - lines.shape[1])))
        pieces.append(lines)
    chunk = jnp.concatenate(pieces, 0) if len(pieces) > 1 else pieces[0]
    if after is not None:
        chunk, _ = lax.optimization_barrier((chunk, after))

    if bundle.z_by == "gather":
        block = lax.all_gather(chunk, "z", axis=0, tiled=False)
    else:
        got = [chunk] + [grid.to_z(chunk, k) for k in range(1, grid.depth)]
        places = []
        for place in range(grid.depth):
            value = got[0]
            for k in range(1, grid.depth):
                value = jnp.where((grid.z - place) % grid.depth == k, got[k], value)
            places.append(value)
        block = jnp.stack(places)
    other = grid.to_y(block)

    full, at = {}, 0
    for name, groups in bundle.ins:
        r, n = weights[name].shape
        c = n // TEAM
        rows = r if c * TEAM == bundle.width else r * TEAM
        own, got = block[:, at : at + rows], other[:, at : at + rows]
        own, got = bundle.unflat(own, c), bundle.unflat(got, c)
        full[name] = paired(own, got, grid.y, 1).reshape(-1, c)
        at += rows
    for name in bundle.outs:
        r, n = weights[name].shape

        def ordered(part):
            part = part[:, at : at + r].reshape(TEAM, grid.low, r, n)
            return part.transpose(1, 0, 2, 3)

        full[name] = paired(ordered(block), ordered(other), grid.y, 1).reshape(-1, n)
        at += r
    if extra is not None:
        own, got = block[:, at : at + TEAM], other[:, at : at + TEAM]
        full["extra"] = paired(own, got, grid.y, 1).reshape(-1, bundle.width)[:, : extra.shape[0]]
    return full, block


def give(grid, bundle, grads, extra=None):
    views, spans = [], []
    for name, groups in bundle.ins:
        k, c = grads[name].shape
        r = k // (grid.depth * 2 * TEAM)
        views.append(bundle.flat(grads[name].reshape(grid.depth, 2, TEAM, r, c)))
    for name in bundle.outs:
        k, n = grads[name].shape
        r = k // (grid.low * 2 * TEAM)
        view = grads[name].reshape(grid.low, 2, TEAM, r, n).transpose(2, 0, 1, 3, 4)
        views.append(view.reshape(grid.depth, 2, r, n))
    if extra is not None:
        view = extra.astype(BF16).reshape(grid.depth, 2, TEAM, -1)
        lack = (bundle.extra - TEAM, bundle.width - view.shape[-1])
        views.append(jnp.pad(view, ((0, 0), (0, 0), (0, lack[0]), (0, lack[1]))))

    away = [pick(v, 1 - grid.y, 1) for v in views]
    home = [pick(v, grid.y, 1) for v in views]
    away = jnp.concatenate(away, 1) if len(away) > 1 else away[0]
    home = jnp.concatenate(home, 1) if len(home) > 1 else home[0]
    block = (home.astype(F32) + grid.to_y(away).astype(F32)).astype(BF16)
    if bundle.z_by == "gather":
        total = lax.psum_scatter(block, "z", scatter_dimension=0, tiled=False).astype(F32)
    else:
        total = pick(block, grid.z, 0).astype(F32)
        for k in range(1, grid.depth):
            total = total + grid.to_z(pick(block, (grid.z + k) % grid.depth, 0), k).astype(F32)
    total = total.astype(BF16)

    done, at = {}, 0
    kinds, parts = {}, {}
    for (name, groups), view in zip(bundle.ins, views):
        rows, c = view.shape[2], grads[name].shape[1]
        parts[name] = bundle.unflat(total[at : at + rows], c)
        kinds.setdefault(c, []).append((name, groups))
        at += rows
    for members in kinds.values():
        joined = jnp.concatenate([parts[name] for name, _ in members], 1) if len(members) > 1 else parts[members[0][0]]
        joined = team_trade(grid, joined.reshape((2, 2) + joined.shape[1:]))
        start = 0
        for name, groups in members:
            r = parts[name].shape[1]
            done[name] = unquarter(joined[:, :, start : start + r], groups).astype(F32)
            start += r
    if bundle.outs:
        rows = sum(v.shape[2] for v in views[len(bundle.ins) : len(bundle.ins) + len(bundle.outs)])
        mine = grid.swap_team(total[at : at + rows]).astype(F32)
        start = 0
        for name, view in zip(bundle.outs, views[len(bundle.ins) :]):
            r = view.shape[2]
            done[name] = mine[start : start + r]
            start += r
        at += rows
    if extra is not None:
        lines = total[at : at + TEAM].reshape(2, 2, -1)
        lines = pick(lines, grid.x, 1).astype(F32) + grid.to_x(pick(lines, 1 - grid.x, 1)).astype(F32)
        lines = pick(lines, grid.core, 0) + grid.to_core(pick(lines, 1 - grid.core, 0))
        done["extra"] = lines[: extra.shape[1]]
    return done


def dot(a, b):
    return jnp.einsum("rlk,km->rlm", a, b, preferred_element_type=F32)


def dot_back(a, b):
    return jnp.einsum("rlm,km->rlk", a, b, preferred_element_type=F32)


def dot_weight(a, b):
    return jnp.einsum("rlk,rlm->km", a, b, preferred_element_type=F32).astype(BF16)


def layer_norm(values, gain, shift):
    average = jnp.mean(values, -1, keepdims=True)
    centred = values - average
    inverse = lax.rsqrt(jnp.mean(centred * centred, -1, keepdims=True) + EPS)
    normed = centred * inverse
    return normed * gain + shift, (normed, inverse)


def norm_back(upstream, stored, gain):
    normed, inverse = stored
    scaled = upstream * gain
    grad = inverse * (
        scaled
        - jnp.mean(scaled, -1, keepdims=True)
        - normed * jnp.mean(scaled * normed, -1, keepdims=True)
    )
    return grad, jnp.sum(upstream * normed, axis=0), jnp.sum(upstream, axis=0)


def heads_of(array, count):
    return array.reshape(array.shape[0], array.shape[1], count, array.shape[2] // count)


def attend(q, k, v, allowed, count):
    rows, length, width = q.shape
    factor = (width // count) ** (-0.5)
    qh, kh, vh = heads_of(q, count), heads_of(k, count), heads_of(v, count)
    scores = jnp.einsum("rqhd,rkhd->rhqk", qh, kh, preferred_element_type=F32) * factor
    scores = jnp.where(allowed[:, None], scores, -1e30)
    exponent = jnp.exp(scores - jnp.max(scores, -1, keepdims=True))
    probs = exponent / jnp.sum(exponent, -1, keepdims=True)
    context = jnp.einsum("rhqk,rkhd->rqhd", probs.astype(BF16), vh, preferred_element_type=F32)
    return context.reshape(rows, length, width).astype(BF16), probs


def attend_back(grad, q, k, v, probs, count):
    rows, length, width = q.shape
    factor = (width // count) ** (-0.5)
    qh, kh, vh, gh = (heads_of(a, count) for a in (q, k, v, grad))
    dv = jnp.einsum("rhqk,rqhd->rkhd", probs.astype(BF16), gh, preferred_element_type=F32)
    dp = jnp.einsum("rqhd,rkhd->rhqk", gh, vh, preferred_element_type=F32)
    ds = (probs * (dp - jnp.sum(dp * probs, -1, keepdims=True))).astype(BF16)
    dq = jnp.einsum("rhqk,rkhd->rqhd", ds, kh, preferred_element_type=F32) * factor
    dk = jnp.einsum("rhqk,rqhd->rkhd", ds, qh, preferred_element_type=F32) * factor
    flat = lambda a: a.reshape(a.shape[0], a.shape[1], width).astype(BF16)
    return flat(dq), flat(dk), flat(dv)


def share(grid, own):
    both = jnp.stack([own, grid.to_x(own)])
    return jnp.concatenate([both, grid.to_core(both)])


def settle(grid, sums):
    both = sums[:2] + grid.to_core(sums[2:].astype(BF16)).astype(F32)
    return both[0] + grid.to_x(both[1].astype(BF16)).astype(F32)


def project(low, w):
    return jnp.split(dot(low, w).astype(BF16), 3, axis=-1)


def attn_out(grid, values, context, w, gain, shift):
    return layer_norm(values + settle(grid, dot(context, w)), gain, shift)


def feed_forward(grid, values, up, down, gain, shift):
    low = share(grid, values.astype(BF16))
    before = dot(low, up)
    hidden = jax.nn.gelu(before, approximate=False).astype(BF16)
    result, stored = layer_norm(values + settle(grid, dot(hidden, down)), gain, shift)
    return result, (low, before, hidden, stored)


def feed_back(grid, upstream, saved, up, down, gain):
    low, before, hidden, stored = saved
    summed, dgain, dshift = norm_back(upstream, stored, gain)
    out = share(grid, summed.astype(BF16))
    hidden_grad = dot_back(out, down)
    _, pull = jax.vjp(partial(jax.nn.gelu, approximate=False), before)
    before_grad = pull(hidden_grad)[0].astype(BF16)
    entry = settle(grid, dot_back(before_grad, up))
    ddown = dot_weight(hidden, out)
    dup = dot_weight(low, before_grad)
    return summed + entry, dup, ddown, dgain, dshift


def attn_out_back(grid, upstream, context, stored, w, gain):
    summed, dgain, dshift = norm_back(upstream, stored, gain)
    out = share(grid, summed.astype(BF16))
    context_grad = dot_back(out, w).astype(BF16)
    return summed, context_grad, dot_weight(context, out), dgain, dshift


def project_back(grid, low, grads, w):
    joined = jnp.concatenate(grads, axis=-1)
    return settle(grid, dot_back(joined, w)), dot_weight(low, joined)


def unpack_norms(full, tw, iw):
    out, at = [], 0
    for width in (tw, tw, iw, iw):
        part = full[:, at : at + 4 * width].reshape(-1, 4, width)
        out.append(part.transpose(1, 0, 2).reshape(4, -1).astype(F32))
        at += 4 * width
    return out


FETCH = (
    Bundle(768, [("tci", 3), ("ici", 3)], [], "permute", extra=16),
    Bundle(768, [("tu0", 1)], ["tco", "td0"], "gather"),
    Bundle(1024, [("iu0", 1)], ["ico", "id0"], "permute"),
    Bundle(768, [("tsi", 3), ("isi", 3)], [], "gather"),
    Bundle(768, [("tu1", 1)], ["tso", "td1"], "gather"),
    Bundle(1024, [("iu1", 1)], ["iso", "id1"], "permute"),
)
RETURN = (
    Bundle(768, [("tu1", 1)], ["td1"], "gather"),
    Bundle(1024, [("iu1", 1)], ["id1"], "permute"),
    Bundle(768, [("tsi", 3), ("isi", 3)], ["tso"], "gather"),
    Bundle(768, [("tu0", 1)], ["td0"], "gather"),
    Bundle(1024, [("iu0", 1)], ["iso", "id0", "ico"], "permute"),
    Bundle(768, [("tci", 3), ("ici", 3)], ["tco"], "permute", extra=16),
)


def shards(
    text_in,
    image_in,
    text_segments,
    text_co_in,
    text_co_out,
    image_co_in,
    image_co_out,
    text_self_in,
    text_self_out,
    image_self_in,
    image_self_out,
    text_up,
    text_down,
    image_up,
    image_down,
    text_gains,
    text_shifts,
    image_gains,
    image_shifts,
    grad_text_out,
    grad_image_out,
    depth,
):
    grid = Grid(depth)
    tw, iw = text_gains.shape[2], image_gains.shape[2]
    weights = {
        "tci": text_co_in[0],
        "tco": text_co_out[0],
        "ici": image_co_in[0],
        "ico": image_co_out[0],
        "tsi": text_self_in[0],
        "tso": text_self_out[0],
        "isi": image_self_in[0],
        "iso": image_self_out[0],
        "tu0": text_up[0, 0],
        "tu1": text_up[0, 1],
        "td0": text_down[0, 0],
        "td1": text_down[0, 1],
        "iu0": image_up[0, 0],
        "iu1": image_up[0, 1],
        "id0": image_down[0, 0],
        "id1": image_down[0, 1],
    }

    norms = jnp.concatenate(
        [a[0].reshape(-1) for a in (text_gains, text_shifts, image_gains, image_shifts)]
    )
    full, blocks = {}, []
    for bundle in FETCH:
        after = blocks[-2] if len(blocks) >= 2 and bundle.z_by == "permute" else None
        got, block = gather(grid, bundle, weights, norms if bundle.extra else None, after)
        full.update(got)
        blocks.append(block)
    gain_t, shift_t, gain_i, shift_i = unpack_norms(full["extra"], tw, iw)

    segments = share(grid, text_segments[0].astype(F32))
    image_ids = (jnp.arange(image_in.shape[1], dtype=jnp.int32) // (2 * REGIONS)).astype(F32)
    cross = segments[:, :, None] == image_ids[None, None, :]
    cross_back = jnp.swapaxes(cross, 1, 2)
    text_allowed = segments[:, :, None] == segments[:, None, :]
    image_allowed = (image_ids[:, None] == image_ids[None, :])[None]

    hc, ht, hi = HC // TEAM, HT // TEAM, HI // TEAM
    xt, xi = text_in[0].astype(F32), image_in[0].astype(F32)
    low_t, low_i = share(grid, text_in[0]), share(grid, image_in[0])
    qt, kt, vt = project(low_t, full["tci"])
    qi, ki, vi = project(low_i, full["ici"])
    ct, pt = attend(qt, ki, vi, cross, hc)
    ci, pi = attend(qi, kt, vt, cross_back, hc)
    yt, yt_saved = attn_out(grid, xt, ct, full["tco"], gain_t[0], shift_t[0])
    yi, yi_saved = attn_out(grid, xi, ci, full["ico"], gain_i[0], shift_i[0])
    zt, zt_saved = feed_forward(grid, yt, full["tu0"], full["td0"], gain_t[1], shift_t[1])
    zi, zi_saved = feed_forward(grid, yi, full["iu0"], full["id0"], gain_i[1], shift_i[1])

    def self_forward(values, w_in, w_out, up, down, allowed, count, gain, shift):
        low = share(grid, values.astype(BF16))
        q, k, v = project(low, w_in)
        context, probs = attend(q, k, v, allowed, count)
        middle, mid_saved = attn_out(grid, values, context, w_out, gain[2], shift[2])
        top, top_saved = feed_forward(grid, middle, up, down, gain[3], shift[3])
        return top, (low, q, k, v, context, probs, mid_saved, top_saved)

    ot, ot_saved = self_forward(
        zt, full["tsi"], full["tso"], full["tu1"], full["td1"], text_allowed, ht, gain_t, shift_t
    )
    oi, oi_saved = self_forward(
        zi, full["isi"], full["iso"], full["iu1"], full["id1"], image_allowed, hi, gain_i, shift_i
    )

    def self_backward(upstream, saved, w_in, w_out, up, down, count, gain):
        low, q, k, v, context, probs, mid_saved, top_saved = saved
        middle, dup, ddown, dg3, db3 = feed_back(grid, upstream, top_saved, up, down, gain[3])
        residual, context_grad, dout, dg2, db2 = attn_out_back(
            grid, middle, context, mid_saved, w_out, gain[2]
        )
        joined = attend_back(context_grad, q, k, v, probs, count)
        entry, din = project_back(grid, low, joined, w_in)
        return residual + entry, din, dout, dup, ddown, (dg2, dg3), (db2, db3)

    grads = {}
    gt, grads["tsi"], grads["tso"], grads["tu1"], grads["td1"], dgt_top, dbt_top = self_backward(
        grad_text_out[0].astype(F32),
        ot_saved,
        full["tsi"],
        full["tso"],
        full["tu1"],
        full["td1"],
        ht,
        gain_t,
    )
    gi, grads["isi"], grads["iso"], grads["iu1"], grads["id1"], dgi_top, dbi_top = self_backward(
        grad_image_out[0].astype(F32),
        oi_saved,
        full["isi"],
        full["iso"],
        full["iu1"],
        full["id1"],
        hi,
        gain_i,
    )

    gt, grads["tu0"], grads["td0"], dgt1, dbt1 = feed_back(
        grid, gt, zt_saved, full["tu0"], full["td0"], gain_t[1]
    )
    gi, grads["iu0"], grads["id0"], dgi1, dbi1 = feed_back(
        grid, gi, zi_saved, full["iu0"], full["id0"], gain_i[1]
    )
    rt, ct_grad, grads["tco"], dgt0, dbt0 = attn_out_back(
        grid, gt, ct, yt_saved, full["tco"], gain_t[0]
    )
    ri, ci_grad, grads["ico"], dgi0, dbi0 = attn_out_back(
        grid, gi, ci, yi_saved, full["ico"], gain_i[0]
    )
    dqt, dki, dvi = attend_back(ct_grad, qt, ki, vi, pt, hc)
    dqi, dkt, dvt = attend_back(ci_grad, qi, kt, vt, pi, hc)
    et, grads["tci"] = project_back(grid, low_t, (dqt, dkt, dvt), full["tci"])
    ei, grads["ici"] = project_back(grid, low_i, (dqi, dki, dvi), full["ici"])

    count = depth * 2 * TEAM

    def by_device(rows, width):
        lines = jnp.stack(rows).reshape(4, count, width)
        return lines.transpose(1, 0, 2).reshape(count, 4 * width)

    sums = jnp.concatenate(
        [
            by_device([dgt0, dgt1, *dgt_top], tw),
            by_device([dbt0, dbt1, *dbt_top], tw),
            by_device([dgi0, dgi1, *dgi_top], iw),
            by_device([dbi0, dbi1, *dbi_top], iw),
        ],
        1,
    )
    done = {}
    for bundle in RETURN:
        done.update(give(grid, bundle, grads, sums if bundle.extra else None))
    norm_grads, at = [], 0
    for width in (tw, tw, iw, iw):
        norm_grads.append(done["extra"][at : at + 4 * width].reshape(1, 4, width))
        at += 4 * width

    def both(first, second):
        return jnp.stack([done[first], done[second]])[None]

    return (
        ot.astype(BF16)[None],
        oi.astype(BF16)[None],
        (rt + et)[None],
        (ri + ei)[None],
        *(done[n][None] for n in ("tci", "tco", "ici", "ico", "tsi", "tso", "isi", "iso")),
        both("tu0", "tu1"),
        both("td0", "td1"),
        both("iu0", "iu1"),
        both("id0", "id1"),
        *norm_grads,
    )


def solution(mesh):
    depth = mesh.shape["wide"] // 4
    fine = Mesh(mesh.devices.reshape(depth, 2, 2, mesh.shape["narrow"]), ALL)
    rows = P(ALL, None, None)
    weight = P(None, ALL, None)
    pair = P(None, None, ALL, None)
    norm = P(None, None, ALL)
    return jax.shard_map(
        partial(shards, depth=depth),
        mesh=fine,
        in_specs=(rows, rows, P(ALL, None), *[weight] * 8, *[pair] * 4, *[norm] * 4, rows, rows),
        out_specs=(rows, rows, rows, rows, *[weight] * 8, *[pair] * 4, *[norm] * 4),
        check_vma=False,
    )
```

```python
from functools import partial

import jax
import jax.numpy as jnp
from jax import lax
from jax.experimental import pallas as pl
from jax.experimental.pallas import tpu as pltpu
from jax.sharding import Mesh, PartitionSpec as P

HT = 12
HI = 8
HC = 8
REGIONS = 36
EPS = 1e-06
F32 = jnp.float32
BF16 = jnp.bfloat16
ALL = ("z", "y", "core", "x")
FLIP = ((0, 1), (1, 0))
TEAM = 4
PIECE = 8


class Grid:
    def __init__(self, depth):
        self.depth, self.rest = depth, depth // 4
        self.y, self.core, self.x = (lax.axis_index(name) for name in ALL[1:])
        z = lax.axis_index("z")
        self.near = z // self.rest % 2
        self.column = z // (2 * self.rest) * self.rest + z % self.rest

    def split(self, z):
        return z // (2 * self.rest), z // self.rest % 2, z % self.rest

    def join(self, far, near, low):
        return (far * 2 + near) * self.rest + low

    def to_core(self, value):
        return lax.ppermute(value, "core", FLIP)

    def to_x(self, value):
        return lax.ppermute(value, "x", FLIP)

    def to_y(self, value):
        return lax.ppermute(value, "y", FLIP)

    def to_near(self, value):
        pairs = []
        for z in range(self.depth):
            far, near, low = self.split(z)
            pairs.append((z, self.join(far, 1 - near, low)))
        return lax.ppermute(value, "z", pairs)

    def to_column(self, value, step):
        pairs = []
        for z in range(self.depth):
            far, near, low = self.split(z)
            column = (far * self.rest + low + step) % (2 * self.rest)
            pairs.append((z, self.join(column // self.rest, near, column % self.rest)))
        return lax.ppermute(value, "z", pairs)

    def swap_far(self, value):
        pairs = []
        for z in range(self.depth):
            far, near, low = self.split(z)
            for y in range(2):
                for core in range(2):
                    for x in range(2):
                        there = ((self.join(core, near, low) * 2 + y) * 2 + far) * 2 + x
                        pairs.append((((z * 2 + y) * 2 + core) * 2 + x, there))
        return lax.ppermute(value, ALL, pairs)


def pick(value, index, axis):
    return lax.dynamic_index_in_dim(value, index, axis, keepdims=False)


def paired(own, other, index, axis):
    own, other = jnp.expand_dims(own, axis), jnp.expand_dims(other, axis)
    shape = list(own.shape)
    shape[axis] = 2
    place = lax.broadcasted_iota(jnp.int32, shape, axis)
    return jnp.where(place == index, own, other)


def joined(values, axis):
    return jnp.concatenate(values, axis) if len(values) > 1 else values[0]


def widen(value, width):
    lack = width - value.shape[-1]
    return jnp.pad(value, [(0, 0)] * (value.ndim - 1) + [(0, lack)]) if lack else value


GROUPS = {"tci": 3, "ici": 3, "tsi": 3, "isi": 3, "tu0": 1, "tu1": 1, "iu0": 1, "iu1": 1}
WIDE = 256


def quarters(w, groups):
    r, n = w.shape
    wide = n // groups // TEAM
    parts = widen(w.reshape(r, groups, TEAM, wide), -(-wide // WIDE) * WIDE)
    return parts.transpose(2, 0, 1, 3).reshape(2, 2, r, groups * parts.shape[3])


def from_quarters(parts, groups, n):
    _, _, r, c = parts.shape
    parts = parts.reshape(TEAM, r, groups, c // groups)[..., : n // groups // TEAM]
    return parts.transpose(1, 2, 0, 3).reshape(r, n)


def team_trade(grid, parts):
    got = grid.to_near(pick(parts, 1 - grid.near, 1))
    parts = paired(pick(parts, grid.near, 1), got, grid.near, 1)
    got = grid.to_core(pick(parts, 1 - grid.core, 0))
    return paired(pick(parts, grid.core, 0), got, grid.core, 0)


def trade_ins(grid, parts):
    width = max(p.shape[3] for p in parts)
    lines = team_trade(grid, joined([widen(p, width) for p in parts], 2))
    out, at = [], 0
    for p in parts:
        r, c = p.shape[2:]
        out.append(lines[:, :, at : at + r, :c])
        at += r
    return out


class Bundle:
    def __init__(self, names, width):
        self.names, self.width = names, width

    def flat(self, value):
        p, r, c = value.shape[-3:]
        lead = value.shape[:-3]
        if p * c == self.width and p > 1:
            value = jnp.concatenate([value[..., k, :, :] for k in range(p)], -1)
        else:
            value = value.reshape(lead + (p * r, c))
        lack = -value.shape[-2] % PIECE
        if lack:
            value = jnp.pad(value, [(0, 0)] * len(lead) + [(0, lack), (0, 0)])
        return value.reshape(lead + (-1, PIECE, self.width))

    def count(self, shape):
        p, r, c = shape
        return -(-(r if p * c == self.width else p * r) // PIECE)

    def unflat(self, lines, shape):
        p, r, c = shape
        lead = lines.shape[:-3]
        lines = lines.reshape(lead + (-1, self.width))
        if p * c == self.width and p > 1:
            return jnp.stack([lines[..., :r, k * c : (k + 1) * c] for k in range(p)], -3)
        return lines[..., : p * r, :].reshape(lead + (p, r, c))


class Gather:
    def __init__(self, grid, bundles, parts):
        self.grid, self.bundles, self.parts = grid, bundles, parts
        self.blocks, self.sides, self.corners = {}, {}, {}
        self.gate = ()

    def chunk(self, i):
        bundle = self.bundles[i]
        return joined([bundle.flat(self.parts[n]) for n in bundle.names], 0)

    def round(self, moves, also=()):
        grid, columns = self.grid, 2 * self.grid.rest
        sends = []
        for kind, i in moves:
            if kind == "z":
                sends.append(self.chunk(i))
            elif kind == "xy":
                sends.append(self.blocks[i])
            else:
                by_x, by_y = self.sides[i]
                cut = by_x.shape[1] // 2
                sends.append((by_x[:, :cut], by_y[:, cut:]))
        if self.gate or also:
            sends, _ = lax.optimization_barrier((sends, (self.gate, also)))
        self.gate = ()
        for (kind, i), value in zip(moves, sends):
            if kind == "c":
                got = self.corners[i] = (grid.to_y(value[0]), grid.to_x(value[1]))
            elif kind == "xy":
                self.blocks[i] = value
                got = self.sides[i] = (grid.to_x(value), grid.to_y(value))
            else:
                got = tuple(grid.to_column(value, k) for k in range(1, columns))
                order = (value, *got)
                places = []
                for place in range(columns):
                    here = order[0]
                    for k in range(1, columns):
                        here = jnp.where((grid.column - place) % columns == k, order[k], here)
                    places.append(here)
                self.blocks[i] = jnp.stack(places)
            self.gate += got

    def full(self, i):
        grid, bundle, parts = self.grid, self.bundles[i], self.parts
        corner = jnp.concatenate(self.corners[i], 1)
        full, at = {}, 0
        for name in bundle.names:
            shape = parts[name].shape
            p, r, c = shape
            n = bundle.count(shape)
            cut = [bundle.unflat(b[:, at : at + n], shape) for b in (self.blocks[i], *self.sides[i], corner)]
            at += n
            if p == TEAM:
                cut = [b.reshape(2, grid.rest, 2, 2, r, c).transpose(0, 3, 1, 2, 4, 5) for b in cut]
                cut = [b[:, :, :, None, :, None] for b in cut]
                place = (3, 5)
            else:
                cut = [b.reshape(2, grid.rest, r, c).swapaxes(0, 1)[:, None, :, None] for b in cut]
                place = (1, 3)
            size = list(cut[0].shape)
            size[place[0]] = size[place[1]] = 2
            here_y = lax.broadcasted_iota(jnp.int32, size, place[0]) == grid.y
            here_x = lax.broadcasted_iota(jnp.int32, size, place[1]) == grid.x
            own, ox, oy, oxy = cut
            value = jnp.where(here_y, jnp.where(here_x, own, ox), jnp.where(here_x, oy, oxy))
            full[name] = lax.optimization_barrier(value).reshape(-1, c)
        return full


def plus(a, *more):
    total = a.astype(F32)
    for b in more:
        total = total + b.astype(F32)
    return total.astype(BF16)


def after(gate, value):
    return lax.optimization_barrier((value, gate))[0]


class Give:
    def __init__(self, grid, bundle, grads, widths):
        self.grid, self.bundle, self.widths, self.step = grid, bundle, widths, 0
        rest = grid.rest
        self.views, self.shapes = [], []
        for name in bundle.names:
            k, c = grads[name].shape
            if name in GROUPS:
                r = k // (rest * 32)
                self.views.append(grads[name].reshape(2, 2, rest, 2, 2, 2, r, c))
                self.shapes.append((TEAM, r, c))
            else:
                r = k // (rest * 8)
                self.views.append(grads[name].reshape(rest, 2, 2, 2, r, c))
                self.shapes.append((1, r, c))
        self.next()

    def block(self, y, x):
        pieces = []
        for view, (p, r, c) in zip(self.views, self.shapes):
            if p == TEAM:
                value = pick(pick(view, x, 5), y, 3).transpose(0, 2, 3, 1, 4, 5)
            else:
                value = pick(pick(view, x, 3), y, 1).swapaxes(0, 1)
            pieces.append(self.bundle.flat(value.reshape(2 * self.grid.rest, p, r, c)))
        return joined(pieces, 1)

    def next(self, gate=None):
        if gate is not None:
            self.got = after(gate, self.got)
        step, self.step = self.step, self.step + 1
        (self.corner, self.side, self.column, self.team, self.core, self.finish)[step]()

    def corner(self):
        grid = self.grid
        corner = self.block(1 - grid.y, 1 - grid.x)
        self.cut = corner.shape[1] // 2
        self.got = grid.to_y(corner[:, : self.cut]), grid.to_x(corner[:, self.cut :])

    def side(self):
        grid, cut, (by_y, by_x) = self.grid, self.cut, self.got
        x = self.block(grid.y, 1 - grid.x)
        y = self.block(1 - grid.y, grid.x)
        x = jnp.concatenate([plus(x[:, :cut], by_y), x[:, cut:]], 1)
        y = jnp.concatenate([y[:, :cut], plus(y[:, cut:], by_x)], 1)
        self.got = grid.to_x(x), grid.to_y(y)

    def column(self):
        grid, columns = self.grid, 2 * self.grid.rest
        chunk = plus(self.block(grid.y, grid.x), *self.got)
        mine = pick(chunk, grid.column, 0)
        sent = [grid.to_column(pick(chunk, (grid.column + k) % columns, 0), k) for k in range(1, columns)]
        self.got = mine, *sent

    def team(self):
        grid, bundle = self.grid, self.bundle
        total = plus(*self.got)
        self.quads, outs, at = [], [], 0
        for name, shape in zip(bundle.names, self.shapes):
            n = bundle.count(shape)
            part = bundle.unflat(total[at : at + n], shape)
            if name in GROUPS:
                self.quads.append((name, part.reshape((2, 2) + part.shape[1:])))
            else:
                outs.append(part[0])
            at += n
        self.got = ()
        if self.quads:
            width = max(q.shape[3] for _, q in self.quads)
            lines = joined([widen(q, width) for _, q in self.quads], 2)
            self.got += (pick(lines, grid.near, 1), grid.to_near(pick(lines, 1 - grid.near, 1)))
        if outs:
            self.got += (grid.swap_far(joined(outs, 0)),)

    def core(self):
        grid = self.grid
        if self.quads:
            mine, came, *outs = self.got
            lines = paired(mine, came, grid.near, 1)
            self.got = (pick(lines, grid.core, 0), grid.to_core(pick(lines, 1 - grid.core, 0)), *outs)

    def finish(self):
        grid, outs, self.done = self.grid, self.got, {}
        if self.quads:
            mine, came, *outs = self.got
            lines, at = paired(mine, came, grid.core, 0), 0
            for name, quad in self.quads:
                r, c = quad.shape[2:]
                part = lines[:, :, at : at + r, :c]
                self.done[name] = from_quarters(part, GROUPS[name], self.widths[name]).astype(F32)
                at += r
        at = 0
        for name, (p, r, c) in zip(self.bundle.names, self.shapes):
            if p == 1:
                self.done[name] = outs[0][at : at + r].astype(F32)
                at += r

    def end(self):
        while self.step < 6:
            self.next()
        return self.done


class Sizes:
    def __init__(self, lt, kt, li, ki):
        self.lt, self.kt, self.li, self.ki = lt, kt, li, ki
        self.third, self.tall, self.left = kt // 3, lt * 3 // 4, lt // 4
        self.rows = li + 2 * self.tall
        self.wide_rows = self.rows + li

    def text(self, ref, r, base=None):
        base = (self.li if base is None else base) + r * self.tall
        top = ref[pl.ds(base, self.tall), : self.kt]
        last = [ref[pl.ds(base + j * self.left, self.left), self.kt :] for j in range(3)]
        return jnp.concatenate([top, jnp.concatenate(last, 1)], 0)

    def put_text(self, ref, r, text):
        base = self.li + r * self.tall
        text = text.astype(ref.dtype)
        ref[pl.ds(base, self.tall), : self.kt] = text[: self.tall]
        for j in range(3):
            block = text[self.tall :, j * self.third : (j + 1) * self.third]
            ref[pl.ds(base + j * self.left, self.left), self.kt :] = block

    def image(self, ref, r=0):
        return ref[pl.ds(r * self.rows, self.li), :]

    def put_image(self, ref, image, r=0):
        ref[pl.ds(r * self.rows, self.li), :] = image.astype(ref.dtype)

    def pack_rows(self, text, image):
        last = text[self.tall :]
        last = [last[:, j * self.third : (j + 1) * self.third] for j in range(3)]
        return jnp.concatenate([image, jnp.concatenate([text[: self.tall], jnp.concatenate(last, 0)], 1)], 0)

    def unpack_text(self, rows):
        rows = rows[self.li : self.li + self.tall]
        last = [rows[j * self.left : (j + 1) * self.left, self.kt :] for j in range(3)]
        return jnp.concatenate([rows[:, : self.kt], jnp.concatenate(last, 1)], 0)

    def both(self, near, far, wide=False):
        text = [self.text(ref, r) for ref in (near, far) for r in range(2)]
        image = [self.image(ref, r) for ref in (near, far) for r in range(2 if wide else 1)]
        return jnp.concatenate(text, 0), jnp.concatenate(image, 0)

    def put_sums(self, home, away, text, image):
        for r in range(TEAM):
            self.put_text((home, away)[r // 2], r % 2, text[r * self.lt : (r + 1) * self.lt])
        count = image.shape[0] // self.li
        for r in range(count):
            part = image[r * self.li : (r + 1) * self.li]
            self.put_image((home, away)[r * 2 // count], part, r % (count // 2))

    def sums(self, wide=False):
        shape = (self.wide_rows if wide else self.rows, self.ki)
        return [(shape, F32), (shape, BF16)]


def kernel(body, outs, args, flops, scratch=()):
    outs = [jax.ShapeDtypeStruct(shape, kind) for shape, kind in outs]
    size = sum(a.size * a.dtype.itemsize for a in (*args, *outs))
    return pl.pallas_call(
        body,
        out_shape=outs,
        scratch_shapes=[pltpu.VMEM(shape, kind) for shape, kind in scratch],
        compiler_params=pltpu.CompilerParams(vmem_limit_bytes=int(1.25 * size) + (14 << 20)),
        cost_estimate=pl.CostEstimate(flops=flops, bytes_accessed=size, transcendentals=0),
    )(*args)


def mm(a, b):
    return jnp.dot(a, b, preferred_element_type=F32)


def mm_bt(a, b):
    return lax.dot_general(a, b, (((1,), (1,)), ((), ())), preferred_element_type=F32)


def mm_at(a, b):
    return lax.dot_general(a, b, (((0,), (0,)), ((), ())), preferred_element_type=F32)


def gelu(v):
    return 0.5 * v * (1.0 + lax.erf(v * (0.5**0.5)))


def gelu_slope(v):
    return 0.5 * (1.0 + lax.erf(v * (0.5**0.5))) + v * jnp.exp(-0.5 * v * v) * (0.5 / jnp.pi) ** 0.5


def ffn_kernel(near, far, ut, dt, ui, di, uj, dj, before_t, hidden_t, before_i, hidden_i, home, away, *, s):
    text, image = s.both(near, far)
    pre = mm(text, ut[...])
    before_t[...] = pre
    act = gelu(pre).astype(BF16)
    hidden_t[...] = act
    text_sums, image_sums = mm(act, dt[...]), 0.0
    f = ui.shape[1]
    for part, (up, down) in enumerate(((ui, di), (uj, dj))):
        at = pl.ds(part * f, f)
        pre = mm(image, up[...])
        before_i[:, at] = pre
        act = gelu(pre).astype(BF16)
        hidden_i[:, at] = act
        image_sums = image_sums + mm(act, down[...])
    s.put_sums(home, away, text_sums, image_sums)


def ffn(s, low, ut, dt, *image_w):
    ft, fi = ut.shape[1], 2 * image_w[0].shape[1]
    outs = []
    for length, f in ((TEAM * s.lt, ft), (2 * s.li, fi)):
        outs += [((length, f), F32), ((length, f), BF16)]
    flops = 16 * (s.lt * s.kt * ft + s.li * s.ki * fi)
    return kernel(partial(ffn_kernel, s=s), outs + s.sums(), (*low, ut, dt, *image_w), flops)


def ffn_back_kernel(near, far, before_t, before_i, ut, dt, ui, di, uj, dj, bg_t, bg_i, home, away, *, s):
    text, image = s.both(near, far)
    grad = (mm_bt(text, dt[...]) * gelu_slope(before_t[...])).astype(BF16)
    bg_t[...] = grad
    text_sums, image_sums = mm_bt(grad, ut[...]), 0.0
    f = ui.shape[1]
    for part, (up, down) in enumerate(((ui, di), (uj, dj))):
        at = pl.ds(part * f, f)
        grad = (mm_bt(image, down[...]) * gelu_slope(before_i[:, at])).astype(BF16)
        bg_i[:, at] = grad
        image_sums = image_sums + mm_bt(grad, up[...])
    s.put_sums(home, away, text_sums, image_sums)


def ffn_back(s, out, before_t, before_i, ut, dt, *image_w):
    ft, fi = ut.shape[1], 2 * image_w[0].shape[1]
    outs = [((TEAM * s.lt, ft), BF16), ((2 * s.li, fi), BF16)] + s.sums()
    flops = 16 * (s.lt * s.kt * ft + s.li * s.ki * fi)
    args = (*out, before_t, before_i, ut, dt, *image_w)
    return kernel(partial(ffn_back_kernel, s=s), outs, args, flops)


def softmax_of(q, k, allowed, factor):
    scores = jnp.where(allowed, mm_bt(q, k) * factor, -1e30)
    exponent = jnp.exp(scores - jnp.max(scores, -1, keepdims=True))
    return exponent / jnp.sum(exponent, -1, keepdims=True)


def head_back(q, k, v, grad, allowed, factor):
    probs = softmax_of(q, k, allowed, factor)
    dv = mm_at(probs.astype(BF16), grad)
    dp = mm_bt(grad, v)
    ds = (probs * (dp - jnp.sum(dp * probs, -1, keepdims=True))).astype(BF16)
    return mm(ds, k) * factor, mm_at(ds, q) * factor, dv


LANES = 128


def lane_part(size, sub):
    lane = lax.broadcasted_iota(jnp.int32, (1, LANES), 1)
    return jnp.logical_and(lane >= sub * size, lane < (sub + 1) * size)


def half_ids(length):
    col = lax.broadcasted_iota(jnp.int32, (length, 1), 0) >= length // 2
    row = lax.broadcasted_iota(jnp.int32, (1, length), 1) >= length // 2
    return col, row


def thirds(tile, wide):
    return [pl.ds(i * wide + tile * LANES, LANES) for i in range(3)]


def image_places(s):
    for r in range(TEAM):
        yield pl.ds(r * s.li, s.li)


def self_kernel(near, far, wt, wot, wi, woi, col, row, qkv_t, ctx_t, qkv_i, ctx_i, home, away, *, s, size, heads):
    text, image = s.both(near, far, True)
    qkv_t[...] = mm(text, wt[...]).astype(BF16)
    qkv_i[...] = mm(image, wi[...]).astype(BF16)
    wide = ctx_t.shape[1]
    allowed = col[...] == row[...]
    for tile in range(wide // LANES):
        q, k, v = (qkv_t[:, at] for at in thirds(tile, wide))
        total = jnp.zeros(q.shape, F32)
        for sub in range(min(LANES // size, heads - tile * (LANES // size))):
            lanes = lane_part(size, sub)
            probs = softmax_of(jnp.where(lanes, q, 0), k, allowed, size**-0.5)
            total = total + jnp.where(lanes, mm(probs.astype(BF16), v), 0.0)
        ctx_t[:, pl.ds(tile * LANES, LANES)] = total.astype(BF16)
    wide = ctx_i.shape[1]
    own, other = half_ids(s.li)
    for at in image_places(s):
        for tile in range(wide // LANES):
            q, k, v = (qkv_i[at, lanes] for lanes in thirds(tile, wide))
            probs = softmax_of(q, k, own == other, LANES**-0.5)
            ctx_i[at, pl.ds(tile * LANES, LANES)] = mm(probs.astype(BF16), v).astype(BF16)
    s.put_sums(home, away, mm(ctx_t[...], wot[...]), mm(ctx_i[...], woi[...]))


def attention_outs(s, wt, wi):
    outs = []
    for length, n in ((s.lt, wt.shape[1]), (s.li, wi.shape[1])):
        outs += [((TEAM * length, n), BF16), ((TEAM * length, n // 3), BF16)]
    return outs


def attention_flops(s, wt, wi):
    return 12 * (s.lt * s.kt * wt.shape[1] + s.li * s.ki * wi.shape[1])


def self_attention(s, low, wt, wot, wi, woi, col, row, size, heads):
    outs = attention_outs(s, wt, wi) + s.sums(True)
    args = (*low, wt, wot, wi, woi, col, row)
    return kernel(partial(self_kernel, s=s, size=size, heads=heads), outs, args, attention_flops(s, wt, wi))


def self_back_kernel(
    near, far, wt, wot, wi, woi, col, row, qkv_t, qkv_i, dqkv_t, dqkv_i, home, away, dctx_t, dctx_i, *, s, size, heads
):
    text, image = s.both(near, far, True)
    dctx_t[...] = mm_bt(text, wot[...]).astype(BF16)
    dctx_i[...] = mm_bt(image, woi[...]).astype(BF16)
    wide = dctx_t.shape[1]
    allowed = col[...] == row[...]
    for tile in range(wide // LANES):
        q, k, v = (qkv_t[:, at] for at in thirds(tile, wide))
        grad = dctx_t[:, pl.ds(tile * LANES, LANES)]
        totals = [jnp.zeros(q.shape, F32) for _ in range(3)]
        for sub in range(min(LANES // size, heads - tile * (LANES // size))):
            lanes = lane_part(size, sub)
            dq, dk, dv = head_back(
                jnp.where(lanes, q, 0), k, v, jnp.where(lanes, grad, 0), allowed, size**-0.5
            )
            totals = [totals[0] + jnp.where(lanes, dq, 0.0), totals[1] + dk, totals[2] + dv]
        for at, total in zip(thirds(tile, wide), totals):
            dqkv_t[:, at] = total.astype(BF16)
    wide = dctx_i.shape[1]
    own, other = half_ids(s.li)
    for at in image_places(s):
        for tile in range(wide // LANES):
            columns = thirds(tile, wide)
            q, k, v = (qkv_i[at, lanes] for lanes in columns)
            grad = dctx_i[at, pl.ds(tile * LANES, LANES)]
            grads = head_back(q, k, v, grad, own == other, LANES**-0.5)
            for lanes, value in zip(columns, grads):
                dqkv_i[at, lanes] = value.astype(BF16)
    s.put_sums(home, away, mm_bt(dqkv_t[...], wt[...]), mm_bt(dqkv_i[...], wi[...]))


def back_outs(s, wt, wi):
    outs = [((TEAM * s.lt, wt.shape[1]), BF16), ((TEAM * s.li, wi.shape[1]), BF16)] + s.sums(True)
    scratch = [((TEAM * s.lt, wt.shape[1] // 3), BF16), ((TEAM * s.li, wi.shape[1] // 3), BF16)]
    return outs, scratch


def self_back(s, out, wt, wot, wi, woi, col, row, qkv_t, qkv_i, size, heads):
    outs, scratch = back_outs(s, wt, wi)
    args = (*out, wt, wot, wi, woi, col, row, qkv_t, qkv_i)
    body = partial(self_back_kernel, s=s, size=size, heads=heads)
    return kernel(body, outs, args, attention_flops(s, wt, wi), scratch)


def co_places(s, seg_col, seg_row):
    col, row = half_ids(s.li)
    for r in range(TEAM):
        text, image = pl.ds(r * s.lt, s.lt), pl.ds(r * s.li, s.li)
        text_col = seg_col[text, :] > 0.5
        text_row = seg_row[pl.ds(r, 1), :] > 0.5
        yield text, image, text_col == row, col == text_row


def co_kernel(
    near, far, wt, wot, wi, woi, seg_col, seg_row, qkv_t, ctx_t, qkv_i, ctx_i, home, away, *, s
):
    text, image = s.both(near, far, True)
    qkv_t[...] = mm(text, wt[...]).astype(BF16)
    qkv_i[...] = mm(image, wi[...]).astype(BF16)
    wide = ctx_t.shape[1]
    for text, image, cross, back in co_places(s, seg_col, seg_row):
        for tile in range(wide // LANES):
            q, k, v = thirds(tile, wide)
            probs = softmax_of(qkv_t[text, q], qkv_i[image, k], cross, LANES**-0.5)
            ctx_t[text, q] = mm(probs.astype(BF16), qkv_i[image, v]).astype(BF16)
            probs = softmax_of(qkv_i[image, q], qkv_t[text, k], back, LANES**-0.5)
            ctx_i[image, q] = mm(probs.astype(BF16), qkv_t[text, v]).astype(BF16)
    s.put_sums(home, away, mm(ctx_t[...], wot[...]), mm(ctx_i[...], woi[...]))


def co_attention(s, low, wt, wot, wi, woi, seg_col, seg_row):
    outs = attention_outs(s, wt, wi) + s.sums(True)
    args = (*low, wt, wot, wi, woi, seg_col, seg_row)
    return kernel(partial(co_kernel, s=s), outs, args, attention_flops(s, wt, wi))


def co_back_kernel(
    near, far, wt, wot, wi, woi, seg_col, seg_row, qkv_t, qkv_i, dqkv_t, dqkv_i, home, away, dctx_t, dctx_i, *, s
):
    text, image = s.both(near, far, True)
    dctx_t[...] = mm_bt(text, wot[...]).astype(BF16)
    dctx_i[...] = mm_bt(image, woi[...]).astype(BF16)
    wide = dctx_t.shape[1]
    for text, image, cross, back in co_places(s, seg_col, seg_row):
        for tile in range(wide // LANES):
            q, k, v = thirds(tile, wide)
            dq, dk, dv = head_back(
                qkv_t[text, q], qkv_i[image, k], qkv_i[image, v], dctx_t[text, q], cross, LANES**-0.5
            )
            dqkv_t[text, q] = dq.astype(BF16)
            dqkv_i[image, k] = dk.astype(BF16)
            dqkv_i[image, v] = dv.astype(BF16)
            dq, dk, dv = head_back(
                qkv_i[image, q], qkv_t[text, k], qkv_t[text, v], dctx_i[image, q], back, LANES**-0.5
            )
            dqkv_i[image, q] = dq.astype(BF16)
            dqkv_t[text, k] = dk.astype(BF16)
            dqkv_t[text, v] = dv.astype(BF16)
    s.put_sums(home, away, mm_bt(dqkv_t[...], wt[...]), mm_bt(dqkv_i[...], wi[...]))


def co_back(s, out, wt, wot, wi, woi, seg_col, seg_row, qkv_t, qkv_i):
    outs, scratch = back_outs(s, wt, wi)
    args = (*out, wt, wot, wi, woi, seg_col, seg_row, qkv_t, qkv_i)
    return kernel(partial(co_back_kernel, s=s), outs, args, attention_flops(s, wt, wi), scratch)


def weight_kernel(near, far, out_near, out_far, mid_t, grad_t, mid_i, grad_i, *outs, s, wide, parts):
    text, image = s.both(near, far, wide)
    text_out, image_out = s.both(out_near, out_far, wide)
    outs[0][...] = mm_at(text, grad_t[...]).astype(BF16)
    outs[1][...] = mm_at(mid_t[...], text_out).astype(BF16)
    grad, mid = grad_i.shape[1] // parts, mid_i.shape[1] // parts
    for part in range(parts):
        at = grad_i[:, pl.ds(part * grad, grad)]
        outs[2 + 2 * part][...] = mm_at(image, at).astype(BF16)
        at = mid_i[:, pl.ds(part * mid, mid)]
        outs[3 + 2 * part][...] = mm_at(at, image_out).astype(BF16)


def weight_grads(s, low, out, mid_t, grad_t, mid_i, grad_i, parts):
    outs = [((s.kt, grad_t.shape[1]), BF16), ((mid_t.shape[1], s.kt), BF16)]
    for _ in range(parts):
        outs += [((s.ki, grad_i.shape[1] // parts), BF16), ((mid_i.shape[1] // parts, s.ki), BF16)]
    flops = sum(8 * s.lt * shape[0] * shape[1] for shape, _ in outs)
    args = (*low, *out, mid_t, grad_t, mid_i, grad_i)
    return kernel(partial(weight_kernel, s=s, wide=parts == 1, parts=parts), outs, args, flops)


def fold_kernel(home, got, out, *, s):
    text = pl.ds(s.li, 2 * s.tall)
    sums = (home[text, :] + got[text, :].astype(F32)).astype(BF16)
    if out.shape[0] == 2 * s.tall:
        out[...] = sums
    else:
        out[pl.ds(0, s.li), :] = (s.image(home, 1) + s.image(got, 1).astype(F32)).astype(BF16)
        out[text, :] = sums


def fold(s, home, got):
    rows = s.rows if home.shape[0] > s.rows else 2 * s.tall
    body = partial(fold_kernel, s=s)
    return kernel(body, [((rows, s.ki), BF16)], (home, got), home.size)[0]


def settled_text(s, base, home, got, other, r):
    start = s.li if other.shape[0] == s.rows else 0
    value = s.text(base, r).astype(F32) + s.text(home, r) + s.text(got, r).astype(F32)
    return value + s.text(other, 1 - r, start).astype(F32)


def settled_image(s, base, home, got, other):
    value = s.image(base).astype(F32) + s.image(home) + s.image(got).astype(F32)
    return value + s.image(other).astype(F32) if other.shape[0] == s.rows else value


def norm_kernel(values, home, got, other, params, out, low, normed, inverse, *, s, i):
    def one(v, gain, shift, start):
        centred = v - jnp.mean(v, -1, keepdims=True)
        inv = lax.rsqrt(jnp.mean(centred * centred, -1, keepdims=True) + EPS)
        n = centred * inv
        inverse[pl.ds(start, v.shape[0]), :] = inv
        return n, n * gain + shift

    param = lambda k, width: params[pl.ds(4 * k + i, 1), :width]
    for r in range(2):
        v = settled_text(s, values, home, got, other, r)
        n, y = one(v, param(0, s.kt), param(1, s.kt), s.li + r * s.lt)
        for ref, value in ((normed, n), (out, y), (low, y)):
            s.put_text(ref, r, value)
    v = settled_image(s, values, home, got, other)
    n, y = one(v, param(2, s.ki), param(3, s.ki), 0)
    for ref, value in ((normed, n), (out, y), (low, y)):
        s.put_image(ref, value)


def norm(s, values, sums, params, i):
    pack = (s.rows, s.ki)
    outs = [(pack, F32), (pack, BF16), (pack, F32), ((s.li + 2 * s.lt, 1), F32)]
    y, low, *stored = kernel(partial(norm_kernel, s=s, i=i), outs, (values, *sums, params), 32 * s.rows * s.ki)
    return y, low, stored


def norm_back_kernel(*refs, s, i, first):
    if first:
        up, normed, inverse, params, grad, low, sums = refs
    else:
        up, home, got, other, normed, inverse, params, grad, low, sums = refs

    def one(u, n, gain, start):
        scaled = u * gain
        return inverse[pl.ds(start, u.shape[0]), :] * (
            scaled - jnp.mean(scaled, -1, keepdims=True) - n * jnp.mean(scaled * n, -1, keepdims=True)
        )

    def keep(k, u, n):
        width = u.shape[1]
        sums[pl.ds(k, 1), :width] = jnp.sum(u * n, axis=0, keepdims=True)
        sums[pl.ds(k + 1, 1), :width] = jnp.sum(u, axis=0, keepdims=True)

    sums[...] = jnp.zeros(sums.shape, F32)
    for r in range(2):
        u = s.text(up, r).astype(F32) if first else settled_text(s, up, home, got, other, r)
        n = s.text(normed, r)
        value = one(u, n, params[pl.ds(i, 1), : s.kt], s.li + r * s.lt)
        s.put_text(grad, r, value)
        s.put_text(low, r, value)
        if r == 0:
            keep(0, u, n)
    u = s.image(up).astype(F32) if first else settled_image(s, up, home, got, other)
    n = s.image(normed)
    value = one(u, n, params[pl.ds(8 + i, 1), :], 0)
    s.put_image(grad, value)
    s.put_image(low, value)
    keep(2, u, n)


def norm_back(s, upstream, sums, stored, params, i):
    pack = (s.rows, s.ki)
    outs = [(pack, F32), (pack, BF16), ((4, s.ki), F32)]
    body = partial(norm_back_kernel, s=s, i=i, first=sums is None)
    return kernel(body, outs, (upstream, *(sums or ()), *stored, params), 32 * s.rows * s.ki)


def sum_all(grid, value):
    value = value + grid.to_core(value)
    value = value + grid.to_x(value)
    value = value + grid.to_y(value)
    value = value + grid.to_near(value)
    return sum((grid.to_column(value, k) for k in range(1, 2 * grid.rest)), value)


FETCH = (
    Bundle(["tci", "ici", "tco", "icoa", "icob"], 768),
    Bundle(["id0", "iu0", "iso"], 1024),
    Bundle(["tu0", "td0"], 768),
    Bundle(["tsi", "isi", "tso"], 768),
    Bundle(["id1", "iu1"], 1024),
    Bundle(["tu1", "td1"], 768),
)


def shards(
    text_in,
    image_in,
    text_segments,
    text_co_in,
    text_co_out,
    image_co_in,
    image_co_out,
    text_self_in,
    text_self_out,
    image_self_in,
    image_self_out,
    text_up,
    text_down,
    image_up,
    image_down,
    text_gains,
    text_shifts,
    image_gains,
    image_shifts,
    grad_text_out,
    grad_image_out,
    depth,
):
    grid = Grid(depth)
    tw, iw = text_gains.shape[2], image_gains.shape[2]
    s = Sizes(*text_in.shape[1:], *image_in.shape[1:])
    weights = {
        "tci": text_co_in[0],
        "tco": text_co_out[0],
        "ici": image_co_in[0],
        "ico": image_co_out[0],
        "tsi": text_self_in[0],
        "tso": text_self_out[0],
        "isi": image_self_in[0],
        "iso": image_self_out[0],
        "tu0": text_up[0, 0],
        "tu1": text_up[0, 1],
        "td0": text_down[0, 0],
        "td1": text_down[0, 1],
        "iu0": image_up[0, 0],
        "iu1": image_up[0, 1],
        "id0": image_down[0, 0],
        "id1": image_down[0, 1],
    }

    weights["icoa"] = image_co_out[0][:, : FETCH[0].width]
    weights["icob"] = widen(image_co_out[0][:, FETCH[0].width :], FETCH[0].width)
    place = ((lax.axis_index("z") * 2 + grid.y) * 2 + grid.core) * 2 + grid.x
    params = jnp.zeros((16, s.ki), F32)
    for at, k, kinds in ((0, tw, (text_gains, text_shifts)), (8, iw, (image_gains, image_shifts))):
        own = jnp.concatenate([a[0] for a in kinds]).astype(F32)
        params = lax.dynamic_update_slice(params, own, (at, place * k))
    width = FETCH[0].width
    widths = {name: weights[name].shape[1] for name in GROUPS}
    quads = {name: quarters(weights[name], groups) for name, groups in GROUPS.items()}
    early = ("tci", "ici")
    late = ("tu0", "tsi", "isi", "tu1", "iu0", "iu1")
    parts = {}

    def trade(names):
        for n, q in zip(names, trade_ins(grid, [quads[n] for n in names])):
            parts[n] = q.reshape((TEAM,) + q.shape[2:])

    def swap(names):
        swapped, at = grid.swap_far(joined([weights[n] for n in names], 0)), 0
        for n in names:
            r = weights[n].shape[0]
            parts[n] = swapped[at : at + r][None]
            at += r

    trade(early)
    swap(("tco", "icoa", "icob"))
    fetch = Gather(grid, FETCH, parts)
    fetch.round([("z", 0)])
    names = ("td0", "tso", "td1", "id0", "iso", "id1")
    inputs = (text_in, image_in, text_segments, grad_text_out, grad_image_out, params)
    later = {n: quads[n] for n in late}, {n: weights[n] for n in names}, inputs
    quarters_later, weights_later, inputs = after(parts["ici"], later)
    quads.update(quarters_later)
    weights.update(weights_later)
    text_in, image_in, text_segments, grad_text_out, grad_image_out, params = inputs
    trade(late)
    swap(("id0", "iso", "id1"))
    swap(("td0", "tso", "td1"))
    fetch.round([("xy", 0)])
    params = sum_all(grid, params)

    def pair(own):
        return own, grid.to_core(own)

    segments = text_segments.astype(F32)
    segments = jnp.concatenate(pair(jnp.concatenate([segments, grid.to_near(segments)])))
    seg_col = segments.reshape(-1, 1)
    ids = segments + 2.0 * jnp.arange(TEAM, dtype=F32)[:, None]
    id_col, id_row = ids.reshape(-1, 1), ids.reshape(1, -1)
    size, heads = s.kt // HT, HT // TEAM
    own = s.pack_rows(text_in[0], image_in[0])
    got = grid.to_near(own)
    values = jnp.concatenate([own, got[s.li :], got[: s.li]])
    low0 = pair(values)
    own = s.pack_rows(grad_text_out[0], grad_image_out[0])
    upstream = jnp.concatenate([own, grid.to_near(own[s.li :])])

    def settle(home, away):
        got = grid.to_core(away)
        return home, got, grid.to_near(fold(s, home, got))

    def normal(values, sums, i):
        return norm(s, values, sums, params, i)

    def widened(low):
        return jnp.concatenate([low, grid.to_near(low[: s.li])])

    def near_pairs(*names):
        for name in names:
            yield full[name]
        for name in names:
            yield grid.to_near(full[name])

    fetch.round([("c", 0), ("z", 1)])
    full = fetch.full(0)
    full["ico"] = jnp.concatenate([full["icoa"], full["icob"][:, : s.ki - width]], 1)
    co_w = [full[n] for n in ("tci", "tco", "ici", "ico")]
    fetch.round([("xy", 1), ("z", 2)])
    qkv_t, ctx_t, qkv_i, ctx_i, home, away = co_attention(s, low0, *co_w, seg_col, segments)
    fetch.round([("c", 1), ("xy", 2), ("z", 3)], away)
    full.update(fetch.full(1))
    sums = settle(home, away)
    y, low, stored0 = normal(values, sums, 0)
    low1 = pair(low)
    fetch.round([("c", 2), ("xy", 3), ("z", 4)], sums[1])
    full.update(fetch.full(2))
    ffn_w = [[full["tu0"], full["td0"], *near_pairs("iu0", "id0")]]
    fetch.round([("c", 3), ("xy", 4), ("z", 5)], low)
    full.update(fetch.full(3))
    full["tso"] = jnp.pad(full["tso"], ((0, full["tsi"].shape[1] // 3 - full["tso"].shape[0]), (0, 0)))
    self_w = [full[n] for n in ("tsi", "tso", "isi", "iso")]
    before_t0, hidden_t0, before_i0, hidden_i0, home, away = ffn(s, low1, *ffn_w[0])
    fetch.round([("c", 4), ("xy", 5)], away)
    full.update(fetch.full(4))
    y, low, stored1 = normal(y, settle(home, away), 1)
    fetch.round([("c", 5)], low)
    full.update(fetch.full(5))
    low2 = pair(widened(low))
    ffn_w.append([full["tu1"], full["td1"], *near_pairs("iu1", "id1")])
    sqkv_t, sctx_t, sqkv_i, sctx_i, home, away = self_attention(s, low2, *self_w, id_col, id_row, size, heads)
    y, low, stored2 = normal(y, settle(home, away), 2)
    low3 = pair(low)
    before_t1, hidden_t1, before_i1, hidden_i1, home, away = ffn(s, low3, *ffn_w[1])
    _, last, stored3 = normal(y, settle(home, away), 3)

    grads, norm_grads = {}, [None] * 4

    def normal_back(upstream, sums, stored, i):
        grad, low, norm_grads[i] = norm_back(s, upstream, sums, stored, params, i)
        return grad, low

    def weigh(names, home, away, low, out, *mids, parts=1):
        got = grid.to_core(away)
        folded = fold(s, home, got)
        low, out, mids = after(folded, (low, out, mids))
        values = weight_grads(s, low, out, *mids, parts)
        grads.update(zip(names, values))
        return (home, got, grid.to_near(folded)), folded, values[4:]

    def give(names, wide, *gate):
        return Give(grid, Bundle(names, wide), grads, widths)

    def join_near(names, values, gate):
        values = after(gate, values)
        for name, value in zip(names, values):
            grads[name] = plus(grads[name], grid.to_near(value))

    g, low = normal_back(upstream, None, stored3, 3)
    out = pair(low)
    bg_t, bg_i, home, away = ffn_back(s, out, before_t1, before_i1, *ffn_w[1])
    sums, folded, others = weigh(
        ("tu1", "td1", "iu1", "id1"), home, away, low3, out, hidden_t1, bg_t, hidden_i1, bg_i, parts=2
    )
    text3 = give(["tu1", "td1"], width)

    g, low = normal_back(g, sums, stored2, 2)
    out = pair(widened(low))
    text3.next(low)
    dqkv_t, dqkv_i, home, away = self_back(s, out, *self_w, id_col, id_row, sqkv_t, sqkv_i, size, heads)
    join_near(("iu1", "id1"), others, away)
    sums, folded, _ = weigh(
        ("tsi", "tso", "isi", "iso"), home, away, low2, out, sctx_t, dqkv_t, sctx_i, dqkv_i
    )
    text3.next(folded)
    grads["tso"] = grads["tso"][: size * heads]
    text2 = give(["tsi", "isi", "tso"], width)

    g, low = normal_back(g, sums, stored1, 1)
    out = pair(low)
    text2.next(low)
    text3.next(low)
    image3 = give(["id1", "iu1", "iso"], s.ki)
    bg_t, bg_i, home, away = ffn_back(s, out, before_t0, before_i0, *ffn_w[0])
    sums, folded, others = weigh(
        ("tu0", "td0", "iu0", "id0"), home, away, low1, out, hidden_t0, bg_t, hidden_i0, bg_i, parts=2
    )
    image3.next(folded)
    text2.next(folded)
    text3.next(folded)
    text1 = give(["tu0", "td0"], width)

    g, low = normal_back(g, sums, stored0, 0)
    out = pair(widened(low))
    text1.next(low)
    image3.next(low)
    text2.next(low)
    join_near(("iu0", "id0"), others, out[1])
    dqkv_t, dqkv_i, home, away = co_back(s, out, *co_w, seg_col, segments, qkv_t, qkv_i)
    image1 = give(["id0", "iu0"], s.ki)
    sums, folded, _ = weigh(
        ("tci", "tco", "ici", "ico"), home, away, low0, out, ctx_t, dqkv_t, ctx_i, dqkv_i
    )
    grads["icoa"] = grads["ico"][:, :width]
    grads["icob"] = widen(grads["ico"][:, width:], width)
    text0 = give(["tci", "ici", "tco", "icoa", "icob"], width)
    for each in (text1, image3, text2, image1):
        each.next(folded)
    norm_sums = sum_all(grid, after(folded, jnp.concatenate(norm_grads))).reshape(4, 4, s.ki)
    home, got, other = sums
    mine = slice(0, s.li + s.tall)
    sums = g[mine] + home[mine] + got[mine].astype(F32)
    sums = sums + jnp.concatenate([other[: s.li], other[s.li + s.tall :]]).astype(F32)

    done = {}
    for each in (text3, text2, image3, text1, image1, text0):
        done.update(each.end())
    done["ico"] = jnp.concatenate([done["icoa"], done["icob"][:, : s.ki - width]], 1)
    norm_outs = [
        lax.dynamic_slice(norm_sums[:, i], (0, place * k), (4, k))[None]
        for i, k in enumerate((tw, tw, iw, iw))
    ]

    def both(first, second):
        return jnp.stack([done[first], done[second]])[None]

    return (
        s.unpack_text(last)[None],
        last[: s.li][None],
        s.unpack_text(sums)[None],
        sums[: s.li][None],
        *(done[n][None] for n in ("tci", "tco", "ici", "ico", "tsi", "tso", "isi", "iso")),
        both("tu0", "tu1"),
        both("td0", "td1"),
        both("iu0", "iu1"),
        both("id0", "id1"),
        *norm_outs,
    )


def solution(mesh):
    depth = mesh.shape["wide"] // 4
    fine = Mesh(mesh.devices.reshape(depth, 2, 2, mesh.shape["narrow"]), ALL)
    rows = P(ALL, None, None)
    weight = P(None, ALL, None)
    pair = P(None, None, ALL, None)
    norm = P(None, None, ALL)
    return jax.shard_map(
        partial(shards, depth=depth),
        mesh=fine,
        in_specs=(rows, rows, P(ALL, None), *[weight] * 8, *[pair] * 4, *[norm] * 4, rows, rows),
        out_specs=(rows, rows, rows, rows, *[weight] * 8, *[pair] * 4, *[norm] * 4),
        check_vma=False,
    )
```

```python
from functools import partial

import jax
import jax.numpy as jnp
from jax import lax
from jax.experimental import pallas as pl
from jax.experimental.pallas import tpu as pltpu
from jax.sharding import Mesh, PartitionSpec as P

HT = 12
HI = 8
HC = 8
REGIONS = 36
EPS = 1e-06
F32 = jnp.float32
BF16 = jnp.bfloat16
ALL = ("z", "y", "core", "x")
FLIP = ((0, 1), (1, 0))
TEAM = 4
PIECE = 8


class Grid:
    def __init__(self, depth):
        self.depth, self.rest = depth, depth // 4
        self.y, self.core, self.x = (lax.axis_index(name) for name in ALL[1:])
        z = lax.axis_index("z")
        self.near = z // self.rest % 2
        self.column = z // (2 * self.rest) * self.rest + z % self.rest

    def split(self, z):
        return z // (2 * self.rest), z // self.rest % 2, z % self.rest

    def join(self, far, near, low):
        return (far * 2 + near) * self.rest + low

    def to_core(self, value):
        return lax.ppermute(value, "core", FLIP)

    def to_x(self, value):
        return lax.ppermute(value, "x", FLIP)

    def to_y(self, value):
        return lax.ppermute(value, "y", FLIP)

    def to_near(self, value):
        pairs = []
        for z in range(self.depth):
            far, near, low = self.split(z)
            pairs.append((z, self.join(far, 1 - near, low)))
        return lax.ppermute(value, "z", pairs)

    def to_column(self, value, step):
        pairs = []
        for z in range(self.depth):
            far, near, low = self.split(z)
            column = (far * self.rest + low + step) % (2 * self.rest)
            pairs.append((z, self.join(column // self.rest, near, column % self.rest)))
        return lax.ppermute(value, "z", pairs)

    def swap_far(self, value):
        pairs = []
        for z in range(self.depth):
            far, near, low = self.split(z)
            for y in range(2):
                for core in range(2):
                    for x in range(2):
                        there = ((self.join(core, near, low) * 2 + y) * 2 + far) * 2 + x
                        pairs.append((((z * 2 + y) * 2 + core) * 2 + x, there))
        return lax.ppermute(value, ALL, pairs)


def pick(value, index, axis):
    return lax.dynamic_index_in_dim(value, index, axis, keepdims=False)


def paired(own, other, index, axis):
    own, other = jnp.expand_dims(own, axis), jnp.expand_dims(other, axis)
    shape = list(own.shape)
    shape[axis] = 2
    place = lax.broadcasted_iota(jnp.int32, shape, axis)
    return jnp.where(place == index, own, other)


def joined(values, axis):
    return jnp.concatenate(values, axis) if len(values) > 1 else values[0]


def widen(value, width):
    lack = width - value.shape[-1]
    return jnp.pad(value, [(0, 0)] * (value.ndim - 1) + [(0, lack)]) if lack else value


GROUPS = {"tci": 3, "ici": 3, "tsi": 3, "isi": 3, "tu0": 1, "tu1": 1, "iu0": 1, "iu1": 1}
WIDE = 256


def quarters(w, groups):
    r, n = w.shape
    wide = n // groups // TEAM
    parts = widen(w.reshape(r, groups, TEAM, wide), -(-wide // WIDE) * WIDE)
    return parts.transpose(2, 0, 1, 3).reshape(2, 2, r, groups * parts.shape[3])


def from_quarters(parts, groups, n):
    _, _, r, c = parts.shape
    parts = parts.reshape(TEAM, r, groups, c // groups)[..., : n // groups // TEAM]
    return parts.transpose(1, 2, 0, 3).reshape(r, n)


def trade_ins(grid, parts):
    width = max(p.shape[3] for p in parts)
    lines = joined([widen(p, width) for p in parts], 2)
    got = grid.to_near(pick(lines, 1 - grid.near, 1))
    lines = paired(pick(lines, grid.near, 1), got, grid.near, 1)
    came = grid.to_core(pick(lines, 1 - grid.core, 0))
    lines = paired(pick(lines, grid.core, 0), came, grid.core, 0)
    out, at = [], 0
    for p in parts:
        r, c = p.shape[2:]
        out.append(lines[:, :, at : at + r, :c])
        at += r
    return out, (got, came)


class Bundle:
    def __init__(self, names, width, turn="both"):
        self.names, self.width, self.turn = names, width, turn

    def flat(self, value):
        p, r, c = value.shape[-3:]
        lead = value.shape[:-3]
        if p * c == self.width and p > 1:
            value = jnp.concatenate([value[..., k, :, :] for k in range(p)], -1)
        else:
            value = value.reshape(lead + (p * r, c))
        lack = -value.shape[-2] % PIECE
        if lack:
            value = jnp.pad(value, [(0, 0)] * len(lead) + [(0, lack), (0, 0)])
        return value.reshape(lead + (-1, PIECE, self.width))

    def count(self, shape):
        p, r, c = shape
        return -(-(r if p * c == self.width else p * r) // PIECE)

    def unflat(self, lines, shape):
        p, r, c = shape
        lead = lines.shape[:-3]
        lines = lines.reshape(lead + (-1, self.width))
        if p * c == self.width and p > 1:
            return jnp.stack([lines[..., :r, k * c : (k + 1) * c] for k in range(p)], -3)
        return lines[..., : p * r, :].reshape(lead + (p, r, c))


class Gather:
    def __init__(self, grid, bundles, parts):
        self.grid, self.bundles, self.parts = grid, bundles, parts
        self.blocks, self.sides, self.corners = {}, {}, {}
        self.gate = ()

    def chunk(self, i):
        bundle = self.bundles[i]
        return joined([bundle.flat(self.parts[n]) for n in bundle.names], 0)

    def cut(self, i, n):
        return {"both": n // 2, "x": n, "y": 0}[self.bundles[i].turn]

    def round(self, moves, also=()):
        grid, columns = self.grid, 2 * self.grid.rest
        sends = []
        for kind, i in moves:
            if kind == "z":
                sends.append(self.chunk(i))
            elif kind == "xy":
                sends.append(self.blocks[i])
            else:
                by_x, by_y = self.sides[i]
                cut = self.cut(i, by_x.shape[1])
                sends.append((by_x[:, :cut], by_y[:, cut:]))
        if self.gate or also:
            sends, _ = lax.optimization_barrier((sends, (self.gate, also)))
        self.gate = ()
        for (kind, i), value in zip(moves, sends):
            if kind == "c":
                got = ()
                if value[0].shape[1]:
                    got += (grid.to_y(value[0]),)
                if value[1].shape[1]:
                    got += (grid.to_x(value[1]),)
                self.corners[i] = got
            elif kind == "xy":
                self.blocks[i] = value
                got = self.sides[i] = (grid.to_x(value), grid.to_y(value))
            else:
                got = tuple(grid.to_column(value, k) for k in range(1, columns))
                order = (value, *got)
                places = []
                for place in range(columns):
                    here = order[0]
                    for k in range(1, columns):
                        here = jnp.where((grid.column - place) % columns == k, order[k], here)
                    places.append(here)
                self.blocks[i] = jnp.stack(places)
            self.gate += got

    def full(self, i):
        grid, bundle, parts = self.grid, self.bundles[i], self.parts
        corner = joined(self.corners[i], 1)
        full, at = {}, 0
        for name in bundle.names:
            shape = parts[name].shape
            p, r, c = shape
            n = bundle.count(shape)
            cut = [bundle.unflat(b[:, at : at + n], shape) for b in (self.blocks[i], *self.sides[i], corner)]
            at += n
            if p == TEAM:
                cut = [b.reshape(2, grid.rest, 2, 2, r, c).transpose(0, 3, 1, 2, 4, 5) for b in cut]
                cut = [b[:, :, :, None, :, None] for b in cut]
                place = (3, 5)
            else:
                cut = [b.reshape(2, grid.rest, r, c).swapaxes(0, 1)[:, None, :, None] for b in cut]
                place = (1, 3)
            size = list(cut[0].shape)
            size[place[0]] = size[place[1]] = 2
            here_y = lax.broadcasted_iota(jnp.int32, size, place[0]) == grid.y
            here_x = lax.broadcasted_iota(jnp.int32, size, place[1]) == grid.x
            own, ox, oy, oxy = cut
            value = jnp.where(here_y, jnp.where(here_x, own, ox), jnp.where(here_x, oy, oxy))
            full[name] = lax.optimization_barrier(value).reshape(-1, c)
        return full


def plus(a, *more):
    total = a.astype(F32)
    for b in more:
        total = total + b.astype(F32)
    return total.astype(BF16)


def lay_kernel(core, mine, came, *outs, shapes):
    first = core[0] == 0
    at = 0
    for (r, c, groups, n), out in zip(shapes, outs):
        wide = n // groups // TEAM
        step = c // groups
        for near in range(2):
            a = mine[near, pl.ds(at, r), :].astype(F32)
            b = came[near, pl.ds(at, r), :].astype(F32)
            for k, value in enumerate((jnp.where(first, a, b), jnp.where(first, b, a))):
                for g in range(groups):
                    to = g * (n // groups) + (2 * k + near) * wide
                    out[:, to : to + wide] = value[:, g * step : g * step + wide]
        at += r


def lay_out(core, mine, came, shapes):
    if any(r % 8 for r, _, _, _ in shapes):
        lines, at, outs = paired(mine, came, core, 0), 0, []
        for r, c, groups, n in shapes:
            outs.append(from_quarters(lines[:, :, at : at + r, :c], groups, n).astype(F32))
            at += r
        return outs
    size = 4 * mine.size + sum(4 * r * n for r, _, _, n in shapes)
    return pl.pallas_call(
        partial(lay_kernel, shapes=shapes),
        out_shape=[jax.ShapeDtypeStruct((r, n), F32) for r, _, _, n in shapes],
        in_specs=[pl.BlockSpec(memory_space=pltpu.SMEM)] + [pl.BlockSpec(memory_space=pltpu.VMEM)] * 2,
        compiler_params=pltpu.CompilerParams(vmem_limit_bytes=2 * size + (8 << 20)),
        cost_estimate=pl.CostEstimate(flops=size, bytes_accessed=size, transcendentals=0),
    )(core.astype(jnp.int32).reshape(1), mine, came)


def after(gate, value):
    return lax.optimization_barrier((value, gate))[0]


class Give:
    def __init__(self, grid, bundle, grads):
        self.grid, self.bundle, self.step = grid, bundle, 0
        rest = grid.rest
        self.views, self.shapes = [], []
        for name in bundle.names:
            k, c = grads[name].shape
            if name in GROUPS:
                r = k // (rest * 32)
                self.views.append(grads[name].reshape(2, 2, rest, 2, 2, 2, r, c))
                self.shapes.append((TEAM, r, c))
            else:
                r = k // (rest * 8)
                self.views.append(grads[name].reshape(rest, 2, 2, 2, r, c))
                self.shapes.append((1, r, c))
        self.next()

    def block(self, y, x):
        pieces = []
        for view, (p, r, c) in zip(self.views, self.shapes):
            if p == TEAM:
                value = pick(pick(view, x, 5), y, 3).transpose(0, 2, 3, 1, 4, 5)
            else:
                value = pick(pick(view, x, 3), y, 1).swapaxes(0, 1)
            pieces.append(self.bundle.flat(value.reshape(2 * self.grid.rest, p, r, c)))
        return joined(pieces, 1)

    def next(self, gate=None):
        if gate is not None:
            self.got = after(gate, self.got)
        step, self.step = self.step, self.step + 1
        (self.corner, self.side, self.column)[step]()

    def corner(self):
        grid = self.grid
        corner = self.block(1 - grid.y, 1 - grid.x)
        n = corner.shape[1]
        self.cut = {"both": n // 2, "x": 0, "y": n}[self.bundle.turn]
        self.got = ()
        if self.cut:
            self.got += (grid.to_y(corner[:, : self.cut]),)
        if self.cut < n:
            self.got += (grid.to_x(corner[:, self.cut :]),)

    def side(self):
        grid, cut, got = self.grid, self.cut, list(self.got)
        x = self.block(grid.y, 1 - grid.x)
        y = self.block(1 - grid.y, grid.x)
        n = x.shape[1]
        if cut == n:
            x = plus(x, got[0])
        elif cut == 0:
            y = plus(y, got[0])
        else:
            x = jnp.concatenate([plus(x[:, :cut], got[0]), x[:, cut:]], 1)
            y = jnp.concatenate([y[:, :cut], plus(y[:, cut:], got[1])], 1)
        self.got = grid.to_x(x), grid.to_y(y)

    def column(self):
        grid, columns = self.grid, 2 * self.grid.rest
        chunk = plus(self.block(grid.y, grid.x), *self.got)
        self.mine = pick(chunk, grid.column, 0)
        self.got = tuple(
            grid.to_column(pick(chunk, (grid.column + k) % columns, 0), k) for k in range(1, columns)
        )


class Deliver:
    def __init__(self, grid, gives, widths, gate=None):
        self.grid, self.widths = grid, widths
        self.quads, self.outs = [], []
        for give in gives:
            got = give.got if gate is None else after(gate, give.got)
            total, at = plus(give.mine, *got), 0
            for name, shape in zip(give.bundle.names, give.shapes):
                n = give.bundle.count(shape)
                part = give.bundle.unflat(total[at : at + n], shape)
                if name in GROUPS:
                    self.quads.append((name, part.reshape((2, 2) + part.shape[1:])))
                else:
                    self.outs.append((name, part[0]))
                at += n
        width = max(q.shape[3] for _, q in self.quads)
        lines = joined([widen(q, width) for _, q in self.quads], 2)
        self.mine, self.came = pick(lines, grid.near, 1), grid.to_near(pick(lines, 1 - grid.near, 1))
        width = max(o.shape[1] for _, o in self.outs)
        self.swapped = grid.swap_far(joined([widen(o, width) for _, o in self.outs], 0))
        self.got = self.came

    def core(self, gate=None):
        grid = self.grid
        came = self.came if gate is None else after(gate, self.came)
        lines = paired(self.mine, came, grid.near, 1)
        self.mine, self.came = pick(lines, grid.core, 0), grid.to_core(pick(lines, 1 - grid.core, 0))
        self.got = self.came

    def finish(self, gate=None):
        came, swapped = self.came, self.swapped
        if gate is not None:
            came, swapped = after(gate, (came, swapped))
        shapes = [(*quad.shape[2:], GROUPS[name], self.widths[name]) for name, quad in self.quads]
        done = dict(zip((n for n, _ in self.quads), lay_out(self.grid.core, self.mine, came, shapes)))
        at = 0
        for name, out in self.outs:
            r, c = out.shape
            done[name] = swapped[at : at + r, :c].astype(F32)
            at += r
        return done


class Sizes:
    def __init__(self, lt, kt, li, ki):
        self.lt, self.kt, self.li, self.ki = lt, kt, li, ki
        self.third, self.tall, self.left = kt // 3, lt * 3 // 4, lt // 4
        self.rows = li + 2 * self.tall
        self.wide_rows = self.rows + li

    def text(self, ref, r, base=None):
        base = (self.li if base is None else base) + r * self.tall
        top = ref[pl.ds(base, self.tall), : self.kt]
        last = [ref[pl.ds(base + j * self.left, self.left), self.kt :] for j in range(3)]
        return jnp.concatenate([top, jnp.concatenate(last, 1)], 0)

    def put_text(self, ref, r, text):
        base = self.li + r * self.tall
        text = text.astype(ref.dtype)
        ref[pl.ds(base, self.tall), : self.kt] = text[: self.tall]
        for j in range(3):
            block = text[self.tall :, j * self.third : (j + 1) * self.third]
            ref[pl.ds(base + j * self.left, self.left), self.kt :] = block

    def image(self, ref, r=0):
        return ref[pl.ds(r * self.rows, self.li), :]

    def put_image(self, ref, image, r=0):
        ref[pl.ds(r * self.rows, self.li), :] = image.astype(ref.dtype)

    def pack_rows(self, text, image):
        last = text[self.tall :]
        last = [last[:, j * self.third : (j + 1) * self.third] for j in range(3)]
        return jnp.concatenate([image, jnp.concatenate([text[: self.tall], jnp.concatenate(last, 0)], 1)], 0)

    def unpack_text(self, rows):
        rows = rows[self.li : self.li + self.tall]
        last = [rows[j * self.left : (j + 1) * self.left, self.kt :] for j in range(3)]
        return jnp.concatenate([rows[:, : self.kt], jnp.concatenate(last, 1)], 0)

    def both(self, near, far, wide=False):
        text = [self.text(ref, r) for ref in (near, far) for r in range(2)]
        image = [self.image(ref, r) for ref in (near, far) for r in range(2 if wide else 1)]
        return jnp.concatenate(text, 0), jnp.concatenate(image, 0)

    def put_sums(self, home, away, text, image):
        for r in range(TEAM):
            self.put_text((home, away)[r // 2], r % 2, text[r * self.lt : (r + 1) * self.lt])
        count = image.shape[0] // self.li
        for r in range(count):
            part = image[r * self.li : (r + 1) * self.li]
            self.put_image((home, away)[r * 2 // count], part, r % (count // 2))

    def sums(self, wide=False):
        shape = (self.wide_rows if wide else self.rows, self.ki)
        return [(shape, F32), (shape, BF16)]


def kernel(body, outs, args, flops, scratch=()):
    outs = [jax.ShapeDtypeStruct(shape, kind) for shape, kind in outs]
    size = sum(a.size * a.dtype.itemsize for a in (*args, *outs))
    return pl.pallas_call(
        body,
        out_shape=outs,
        scratch_shapes=[pltpu.VMEM(shape, kind) for shape, kind in scratch],
        compiler_params=pltpu.CompilerParams(vmem_limit_bytes=int(1.25 * size) + (14 << 20)),
        cost_estimate=pl.CostEstimate(flops=flops, bytes_accessed=size, transcendentals=0),
    )(*args)


def mm(a, b):
    return jnp.dot(a, b, preferred_element_type=F32)


def mm_bt(a, b):
    return lax.dot_general(a, b, (((1,), (1,)), ((), ())), preferred_element_type=F32)


def mm_at(a, b):
    return lax.dot_general(a, b, (((0,), (0,)), ((), ())), preferred_element_type=F32)


def gelu(v):
    return 0.5 * v * (1.0 + lax.erf(v * (0.5**0.5)))


def gelu_slope(v):
    return 0.5 * (1.0 + lax.erf(v * (0.5**0.5))) + v * jnp.exp(-0.5 * v * v) * (0.5 / jnp.pi) ** 0.5


def ffn_kernel(near, far, ut, dt, ui, di, uj, dj, before_t, hidden_t, before_i, hidden_i, home, away, *, s):
    text, image = s.both(near, far)
    pre = mm(text, ut[...])
    before_t[...] = pre
    act = gelu(pre).astype(BF16)
    hidden_t[...] = act
    text_sums, image_sums = mm(act, dt[...]), 0.0
    f = ui.shape[1]
    for part, (up, down) in enumerate(((ui, di), (uj, dj))):
        at = pl.ds(part * f, f)
        pre = mm(image, up[...])
        before_i[:, at] = pre
        act = gelu(pre).astype(BF16)
        hidden_i[:, at] = act
        image_sums = image_sums + mm(act, down[...])
    s.put_sums(home, away, text_sums, image_sums)


def ffn(s, low, ut, dt, *image_w):
    ft, fi = ut.shape[1], 2 * image_w[0].shape[1]
    outs = []
    for length, f in ((TEAM * s.lt, ft), (2 * s.li, fi)):
        outs += [((length, f), F32), ((length, f), BF16)]
    flops = 16 * (s.lt * s.kt * ft + s.li * s.ki * fi)
    return kernel(partial(ffn_kernel, s=s), outs + s.sums(), (*low, ut, dt, *image_w), flops)


def ffn_back_kernel(near, far, before_t, before_i, ut, dt, ui, di, uj, dj, bg_t, bg_i, home, away, *, s):
    text, image = s.both(near, far)
    grad = (mm_bt(text, dt[...]) * gelu_slope(before_t[...])).astype(BF16)
    bg_t[...] = grad
    text_sums, image_sums = mm_bt(grad, ut[...]), 0.0
    f = ui.shape[1]
    for part, (up, down) in enumerate(((ui, di), (uj, dj))):
        at = pl.ds(part * f, f)
        grad = (mm_bt(image, down[...]) * gelu_slope(before_i[:, at])).astype(BF16)
        bg_i[:, at] = grad
        image_sums = image_sums + mm_bt(grad, up[...])
    s.put_sums(home, away, text_sums, image_sums)


def ffn_back(s, out, before_t, before_i, ut, dt, *image_w):
    ft, fi = ut.shape[1], 2 * image_w[0].shape[1]
    outs = [((TEAM * s.lt, ft), BF16), ((2 * s.li, fi), BF16)] + s.sums()
    flops = 16 * (s.lt * s.kt * ft + s.li * s.ki * fi)
    args = (*out, before_t, before_i, ut, dt, *image_w)
    return kernel(partial(ffn_back_kernel, s=s), outs, args, flops)


def softmax_of(q, k, allowed, factor):
    scores = jnp.where(allowed, mm_bt(q, k) * factor, -1e30)
    exponent = jnp.exp(scores - jnp.max(scores, -1, keepdims=True))
    return exponent / jnp.sum(exponent, -1, keepdims=True)


def head_back(q, k, v, grad, allowed, factor):
    probs = softmax_of(q, k, allowed, factor)
    dv = mm_at(probs.astype(BF16), grad)
    dp = mm_bt(grad, v)
    ds = (probs * (dp - jnp.sum(dp * probs, -1, keepdims=True))).astype(BF16)
    return mm(ds, k) * factor, mm_at(ds, q) * factor, dv


LANES = 128


def lane_part(size, sub):
    lane = lax.broadcasted_iota(jnp.int32, (1, LANES), 1)
    return jnp.logical_and(lane >= sub * size, lane < (sub + 1) * size)


def half_ids(length):
    col = lax.broadcasted_iota(jnp.int32, (length, 1), 0) >= length // 2
    row = lax.broadcasted_iota(jnp.int32, (1, length), 1) >= length // 2
    return col, row


def thirds(tile, wide):
    return [pl.ds(i * wide + tile * LANES, LANES) for i in range(3)]


def image_places(s):
    for r in range(TEAM):
        yield pl.ds(r * s.li, s.li)


def self_kernel(near, far, wt, wot, wi, woi, col, row, qkv_t, ctx_t, qkv_i, ctx_i, home, away, *, s, size, heads):
    text, image = s.both(near, far, True)
    qkv_t[...] = mm(text, wt[...]).astype(BF16)
    qkv_i[...] = mm(image, wi[...]).astype(BF16)
    wide = ctx_t.shape[1]
    allowed = col[...] == row[...]
    for tile in range(wide // LANES):
        q, k, v = (qkv_t[:, at] for at in thirds(tile, wide))
        total = jnp.zeros(q.shape, F32)
        for sub in range(min(LANES // size, heads - tile * (LANES // size))):
            lanes = lane_part(size, sub)
            probs = softmax_of(jnp.where(lanes, q, 0), k, allowed, size**-0.5)
            total = total + jnp.where(lanes, mm(probs.astype(BF16), v), 0.0)
        ctx_t[:, pl.ds(tile * LANES, LANES)] = total.astype(BF16)
    wide = ctx_i.shape[1]
    own, other = half_ids(s.li)
    for at in image_places(s):
        for tile in range(wide // LANES):
            q, k, v = (qkv_i[at, lanes] for lanes in thirds(tile, wide))
            probs = softmax_of(q, k, own == other, LANES**-0.5)
            ctx_i[at, pl.ds(tile * LANES, LANES)] = mm(probs.astype(BF16), v).astype(BF16)
    s.put_sums(home, away, mm(ctx_t[...], wot[...]), mm(ctx_i[...], woi[...]))


def attention_outs(s, wt, wi):
    outs = []
    for length, n in ((s.lt, wt.shape[1]), (s.li, wi.shape[1])):
        outs += [((TEAM * length, n), BF16), ((TEAM * length, n // 3), BF16)]
    return outs


def attention_flops(s, wt, wi):
    return 12 * (s.lt * s.kt * wt.shape[1] + s.li * s.ki * wi.shape[1])


def self_attention(s, low, wt, wot, wi, woi, col, row, size, heads):
    outs = attention_outs(s, wt, wi) + s.sums(True)
    args = (*low, wt, wot, wi, woi, col, row)
    return kernel(partial(self_kernel, s=s, size=size, heads=heads), outs, args, attention_flops(s, wt, wi))


def self_back_kernel(
    near, far, wt, wot, wi, woi, col, row, qkv_t, qkv_i, dqkv_t, dqkv_i, home, away, dctx_t, dctx_i, *, s, size, heads
):
    text, image = s.both(near, far, True)
    dctx_t[...] = mm_bt(text, wot[...]).astype(BF16)
    dctx_i[...] = mm_bt(image, woi[...]).astype(BF16)
    wide = dctx_t.shape[1]
    allowed = col[...] == row[...]
    for tile in range(wide // LANES):
        q, k, v = (qkv_t[:, at] for at in thirds(tile, wide))
        grad = dctx_t[:, pl.ds(tile * LANES, LANES)]
        totals = [jnp.zeros(q.shape, F32) for _ in range(3)]
        for sub in range(min(LANES // size, heads - tile * (LANES // size))):
            lanes = lane_part(size, sub)
            dq, dk, dv = head_back(
                jnp.where(lanes, q, 0), k, v, jnp.where(lanes, grad, 0), allowed, size**-0.5
            )
            totals = [totals[0] + jnp.where(lanes, dq, 0.0), totals[1] + dk, totals[2] + dv]
        for at, total in zip(thirds(tile, wide), totals):
            dqkv_t[:, at] = total.astype(BF16)
    wide = dctx_i.shape[1]
    own, other = half_ids(s.li)
    for at in image_places(s):
        for tile in range(wide // LANES):
            columns = thirds(tile, wide)
            q, k, v = (qkv_i[at, lanes] for lanes in columns)
            grad = dctx_i[at, pl.ds(tile * LANES, LANES)]
            grads = head_back(q, k, v, grad, own == other, LANES**-0.5)
            for lanes, value in zip(columns, grads):
                dqkv_i[at, lanes] = value.astype(BF16)
    s.put_sums(home, away, mm_bt(dqkv_t[...], wt[...]), mm_bt(dqkv_i[...], wi[...]))


def back_outs(s, wt, wi):
    outs = [((TEAM * s.lt, wt.shape[1]), BF16), ((TEAM * s.li, wi.shape[1]), BF16)] + s.sums(True)
    scratch = [((TEAM * s.lt, wt.shape[1] // 3), BF16), ((TEAM * s.li, wi.shape[1] // 3), BF16)]
    return outs, scratch


def self_back(s, out, wt, wot, wi, woi, col, row, qkv_t, qkv_i, size, heads):
    outs, scratch = back_outs(s, wt, wi)
    args = (*out, wt, wot, wi, woi, col, row, qkv_t, qkv_i)
    body = partial(self_back_kernel, s=s, size=size, heads=heads)
    return kernel(body, outs, args, attention_flops(s, wt, wi), scratch)


def co_places(s, seg_col, seg_row):
    col, row = half_ids(s.li)
    for r in range(TEAM):
        text, image = pl.ds(r * s.lt, s.lt), pl.ds(r * s.li, s.li)
        text_col = seg_col[text, :] > 0.5
        text_row = seg_row[pl.ds(r, 1), :] > 0.5
        yield text, image, text_col == row, col == text_row


def co_kernel(
    near, far, wt, wot, wi, woi, seg_col, seg_row, qkv_t, ctx_t, qkv_i, ctx_i, home, away, *, s
):
    text, image = s.both(near, far, True)
    qkv_t[...] = mm(text, wt[...]).astype(BF16)
    qkv_i[...] = mm(image, wi[...]).astype(BF16)
    wide = ctx_t.shape[1]
    for text, image, cross, back in co_places(s, seg_col, seg_row):
        for tile in range(wide // LANES):
            q, k, v = thirds(tile, wide)
            probs = softmax_of(qkv_t[text, q], qkv_i[image, k], cross, LANES**-0.5)
            ctx_t[text, q] = mm(probs.astype(BF16), qkv_i[image, v]).astype(BF16)
            probs = softmax_of(qkv_i[image, q], qkv_t[text, k], back, LANES**-0.5)
            ctx_i[image, q] = mm(probs.astype(BF16), qkv_t[text, v]).astype(BF16)
    s.put_sums(home, away, mm(ctx_t[...], wot[...]), mm(ctx_i[...], woi[...]))


def co_attention(s, low, wt, wot, wi, woi, seg_col, seg_row):
    outs = attention_outs(s, wt, wi) + s.sums(True)
    args = (*low, wt, wot, wi, woi, seg_col, seg_row)
    return kernel(partial(co_kernel, s=s), outs, args, attention_flops(s, wt, wi))


def co_back_kernel(
    near, far, wt, wot, wi, woi, seg_col, seg_row, qkv_t, qkv_i, dqkv_t, dqkv_i, home, away, dctx_t, dctx_i, *, s
):
    text, image = s.both(near, far, True)
    dctx_t[...] = mm_bt(text, wot[...]).astype(BF16)
    dctx_i[...] = mm_bt(image, woi[...]).astype(BF16)
    wide = dctx_t.shape[1]
    for text, image, cross, back in co_places(s, seg_col, seg_row):
        for tile in range(wide // LANES):
            q, k, v = thirds(tile, wide)
            dq, dk, dv = head_back(
                qkv_t[text, q], qkv_i[image, k], qkv_i[image, v], dctx_t[text, q], cross, LANES**-0.5
            )
            dqkv_t[text, q] = dq.astype(BF16)
            dqkv_i[image, k] = dk.astype(BF16)
            dqkv_i[image, v] = dv.astype(BF16)
            dq, dk, dv = head_back(
                qkv_i[image, q], qkv_t[text, k], qkv_t[text, v], dctx_i[image, q], back, LANES**-0.5
            )
            dqkv_i[image, q] = dq.astype(BF16)
            dqkv_t[text, k] = dk.astype(BF16)
            dqkv_t[text, v] = dv.astype(BF16)
    s.put_sums(home, away, mm_bt(dqkv_t[...], wt[...]), mm_bt(dqkv_i[...], wi[...]))


def co_back(s, out, wt, wot, wi, woi, seg_col, seg_row, qkv_t, qkv_i):
    outs, scratch = back_outs(s, wt, wi)
    args = (*out, wt, wot, wi, woi, seg_col, seg_row, qkv_t, qkv_i)
    return kernel(partial(co_back_kernel, s=s), outs, args, attention_flops(s, wt, wi), scratch)


def weight_kernel(near, far, out_near, out_far, mid_t, grad_t, mid_i, grad_i, *outs, s, wide, parts):
    text, image = s.both(near, far, wide)
    text_out, image_out = s.both(out_near, out_far, wide)
    outs[0][...] = mm_at(text, grad_t[...]).astype(BF16)
    outs[1][...] = mm_at(mid_t[...], text_out).astype(BF16)
    grad, mid = grad_i.shape[1] // parts, mid_i.shape[1] // parts
    for part in range(parts):
        at = grad_i[:, pl.ds(part * grad, grad)]
        outs[2 + 2 * part][...] = mm_at(image, at).astype(BF16)
        at = mid_i[:, pl.ds(part * mid, mid)]
        outs[3 + 2 * part][...] = mm_at(at, image_out).astype(BF16)


def weight_grads(s, low, out, mid_t, grad_t, mid_i, grad_i, parts):
    outs = [((s.kt, grad_t.shape[1]), BF16), ((mid_t.shape[1], s.kt), BF16)]
    for _ in range(parts):
        outs += [((s.ki, grad_i.shape[1] // parts), BF16), ((mid_i.shape[1] // parts, s.ki), BF16)]
    flops = sum(8 * s.lt * shape[0] * shape[1] for shape, _ in outs)
    args = (*low, *out, mid_t, grad_t, mid_i, grad_i)
    return kernel(partial(weight_kernel, s=s, wide=parts == 1, parts=parts), outs, args, flops)


def fold_kernel(home, got, out, *, s):
    text = pl.ds(s.li, 2 * s.tall)
    sums = (home[text, :] + got[text, :].astype(F32)).astype(BF16)
    if out.shape[0] == 2 * s.tall:
        out[...] = sums
    else:
        out[pl.ds(0, s.li), :] = (s.image(home, 1) + s.image(got, 1).astype(F32)).astype(BF16)
        out[text, :] = sums


def fold(s, home, got):
    rows = s.rows if home.shape[0] > s.rows else 2 * s.tall
    body = partial(fold_kernel, s=s)
    return kernel(body, [((rows, s.ki), BF16)], (home, got), home.size)[0]


def settled_text(s, base, home, got, other, r):
    start = s.li if other.shape[0] == s.rows else 0
    value = s.text(base, r).astype(F32) + s.text(home, r) + s.text(got, r).astype(F32)
    return value + s.text(other, 1 - r, start).astype(F32)


def settled_image(s, base, home, got, other):
    value = s.image(base).astype(F32) + s.image(home) + s.image(got).astype(F32)
    return value + s.image(other).astype(F32) if other.shape[0] == s.rows else value


def norm_kernel(values, home, got, other, params, out, low, normed, inverse, *, s, i):
    def one(v, gain, shift, start):
        centred = v - jnp.mean(v, -1, keepdims=True)
        inv = lax.rsqrt(jnp.mean(centred * centred, -1, keepdims=True) + EPS)
        n = centred * inv
        inverse[pl.ds(start, v.shape[0]), :] = inv
        return n, n * gain + shift

    param = lambda k, width: params[pl.ds(4 * k + i, 1), :width]
    for r in range(2):
        v = settled_text(s, values, home, got, other, r)
        n, y = one(v, param(0, s.kt), param(1, s.kt), s.li + r * s.lt)
        for ref, value in ((normed, n), (out, y), (low, y)):
            s.put_text(ref, r, value)
    v = settled_image(s, values, home, got, other)
    n, y = one(v, param(2, s.ki), param(3, s.ki), 0)
    for ref, value in ((normed, n), (out, y), (low, y)):
        s.put_image(ref, value)


def norm(s, values, sums, params, i):
    pack = (s.rows, s.ki)
    outs = [(pack, F32), (pack, BF16), (pack, F32), ((s.li + 2 * s.lt, 1), F32)]
    y, low, *stored = kernel(partial(norm_kernel, s=s, i=i), outs, (values, *sums, params), 32 * s.rows * s.ki)
    return y, low, stored


def norm_back_kernel(*refs, s, i, first):
    if first:
        up, normed, inverse, params, grad, low, sums = refs
    else:
        up, home, got, other, normed, inverse, params, grad, low, sums = refs

    def one(u, n, gain, start):
        scaled = u * gain
        return inverse[pl.ds(start, u.shape[0]), :] * (
            scaled - jnp.mean(scaled, -1, keepdims=True) - n * jnp.mean(scaled * n, -1, keepdims=True)
        )

    def keep(k, u, n):
        width = u.shape[1]
        sums[pl.ds(k, 1), :width] = jnp.sum(u * n, axis=0, keepdims=True)
        sums[pl.ds(k + 1, 1), :width] = jnp.sum(u, axis=0, keepdims=True)

    sums[...] = jnp.zeros(sums.shape, F32)
    for r in range(2):
        u = s.text(up, r).astype(F32) if first else settled_text(s, up, home, got, other, r)
        n = s.text(normed, r)
        value = one(u, n, params[pl.ds(i, 1), : s.kt], s.li + r * s.lt)
        s.put_text(grad, r, value)
        s.put_text(low, r, value)
        if r == 0:
            keep(0, u, n)
    u = s.image(up).astype(F32) if first else settled_image(s, up, home, got, other)
    n = s.image(normed)
    value = one(u, n, params[pl.ds(8 + i, 1), :], 0)
    s.put_image(grad, value)
    s.put_image(low, value)
    keep(2, u, n)


def norm_back(s, upstream, sums, stored, params, i):
    pack = (s.rows, s.ki)
    outs = [(pack, F32), (pack, BF16), ((4, s.ki), F32)]
    body = partial(norm_back_kernel, s=s, i=i, first=sums is None)
    return kernel(body, outs, (upstream, *(sums or ()), *stored, params), 32 * s.rows * s.ki)


FETCH = (
    Bundle(["tci", "ici", "tco", "icoa", "icob"], 768),
    Bundle(["id0", "iu0", "iso"], 1024, "x"),
    Bundle(["tu0", "td0"], 768, "y"),
    Bundle(["tsi", "isi", "tso"], 768, "x"),
    Bundle(["id1", "iu1"], 1024, "y"),
    Bundle(["tu1", "td1"], 768, "y"),
)


def shards(
    text_in,
    image_in,
    text_segments,
    text_co_in,
    text_co_out,
    image_co_in,
    image_co_out,
    text_self_in,
    text_self_out,
    image_self_in,
    image_self_out,
    text_up,
    text_down,
    image_up,
    image_down,
    text_gains,
    text_shifts,
    image_gains,
    image_shifts,
    grad_text_out,
    grad_image_out,
    depth,
):
    grid = Grid(depth)
    rest = grid.rest
    tw, iw = text_gains.shape[2], image_gains.shape[2]
    s = Sizes(*text_in.shape[1:], *image_in.shape[1:])
    weights = {
        "tci": text_co_in[0],
        "tco": text_co_out[0],
        "ici": image_co_in[0],
        "ico": image_co_out[0],
        "tsi": text_self_in[0],
        "tso": text_self_out[0],
        "isi": image_self_in[0],
        "iso": image_self_out[0],
        "tu0": text_up[0, 0],
        "tu1": text_up[0, 1],
        "td0": text_down[0, 0],
        "td1": text_down[0, 1],
        "iu0": image_up[0, 0],
        "iu1": image_up[0, 1],
        "id0": image_down[0, 0],
        "id1": image_down[0, 1],
    }

    weights["icoa"] = image_co_out[0][:, : FETCH[0].width]
    weights["icob"] = widen(image_co_out[0][:, FETCH[0].width :], FETCH[0].width)
    place = ((lax.axis_index("z") * 2 + grid.y) * 2 + grid.core) * 2 + grid.x
    params = jnp.zeros((16, s.ki), F32)
    for at, k, kinds in ((0, tw, (text_gains, text_shifts)), (8, iw, (image_gains, image_shifts))):
        own = jnp.concatenate([a[0] for a in kinds]).astype(F32)
        params = lax.dynamic_update_slice(params, own, (at, place * k))
    width = FETCH[0].width
    widths = {name: weights[name].shape[1] for name in GROUPS}
    quads = {name: quarters(weights[name], groups) for name, groups in GROUPS.items()}
    early = ("tci", "ici")
    late = ("tu0", "tsi", "isi", "tu1", "iu0", "iu1")
    parts = {}

    def trade(names):
        got, arrived = trade_ins(grid, [quads[n] for n in names])
        for n, q in zip(names, got):
            parts[n] = q.reshape((TEAM,) + q.shape[2:])
        return arrived

    def swap(names):
        swapped, at = grid.swap_far(joined([weights[n] for n in names], 0)), 0
        for n in names:
            r = weights[n].shape[0]
            parts[n] = swapped[at : at + r][None]
            at += r

    trade(early)
    swap(("tco", "icoa", "icob"))
    fetch = Gather(grid, FETCH, parts)
    fetch.round([("z", 0)])
    names = ("td0", "tso", "td1", "id0", "iso", "id1")
    inputs = (text_in, image_in, text_segments, grad_text_out, grad_image_out, params)
    later = {n: quads[n] for n in late}, {n: weights[n] for n in names}, inputs
    quarters_later, weights_later, inputs = after(fetch.gate, later)
    quads.update(quarters_later)
    weights.update(weights_later)
    text_in, image_in, text_segments, grad_text_out, grad_image_out, params = inputs
    trade(late)
    swap(("id0", "iso", "id1"))
    swap(("td0", "tso", "td1"))
    fetch.round([("xy", 0)])
    moved = grid.to_core(params)

    def more(move):
        nonlocal params, moved
        params = params + after(fetch.gate, moved)
        moved = move(params)

    def pair(own):
        return own, grid.to_core(own)

    segments = text_segments.astype(F32)
    segments = jnp.concatenate(pair(jnp.concatenate([segments, grid.to_near(segments)])))
    seg_col = segments.reshape(-1, 1)
    ids = segments + 2.0 * jnp.arange(TEAM, dtype=F32)[:, None]
    id_col, id_row = ids.reshape(-1, 1), ids.reshape(1, -1)
    size, heads = s.kt // HT, HT // TEAM
    own = s.pack_rows(text_in[0], image_in[0])
    got = grid.to_near(own)
    values = jnp.concatenate([own, got[s.li :], got[: s.li]])
    low0 = pair(values)
    own = s.pack_rows(grad_text_out[0], grad_image_out[0])
    upstream = jnp.concatenate([own, grid.to_near(own[s.li :])])

    def settle(home, away):
        got = grid.to_core(away)
        return home, got, grid.to_near(fold(s, home, got))

    def normal(values, sums, i):
        return norm(s, values, sums, params, i)

    def widened(low):
        return jnp.concatenate([low, grid.to_near(low[: s.li])])

    def near_pairs(*names):
        for name in names:
            yield full[name]
        for name in names:
            yield grid.to_near(full[name])

    more(grid.to_x)
    fetch.round([("c", 0), ("z", 1)])
    full = fetch.full(0)
    full["ico"] = jnp.concatenate([full["icoa"], full["icob"][:, : s.ki - width]], 1)
    co_w = [full[n] for n in ("tci", "tco", "ici", "ico")]
    more(grid.to_y)
    fetch.round([("xy", 1), ("z", 2)])
    qkv_t, ctx_t, qkv_i, ctx_i, home, away = co_attention(s, low0, *co_w, seg_col, segments)
    more(grid.to_near)
    fetch.round([("c", 1), ("xy", 2), ("z", 3)], away)
    full.update(fetch.full(1))
    sums = settle(home, away)
    more(lambda value: sum((grid.to_column(value, k) for k in range(2, 2 * rest)), grid.to_column(value, 1)))
    params = params + moved
    y, low, stored0 = normal(values, sums, 0)
    low1 = pair(low)
    fetch.round([("c", 2), ("xy", 3), ("z", 4)], sums[1])
    full.update(fetch.full(2))
    ffn_w = [[full["tu0"], full["td0"], *near_pairs("iu0", "id0")]]
    fetch.round([("c", 3), ("xy", 4), ("z", 5)], low)
    full.update(fetch.full(3))
    full["tso"] = jnp.pad(full["tso"], ((0, full["tsi"].shape[1] // 3 - full["tso"].shape[0]), (0, 0)))
    self_w = [full[n] for n in ("tsi", "tso", "isi", "iso")]
    before_t0, hidden_t0, before_i0, hidden_i0, home, away = ffn(s, low1, *ffn_w[0])
    fetch.round([("c", 4), ("xy", 5)], away)
    full.update(fetch.full(4))
    y, low, stored1 = normal(y, settle(home, away), 1)
    fetch.round([("c", 5)], low)
    full.update(fetch.full(5))
    low2 = pair(widened(low))
    ffn_w.append([full["tu1"], full["td1"], *near_pairs("iu1", "id1")])
    sqkv_t, sctx_t, sqkv_i, sctx_i, home, away = self_attention(s, low2, *self_w, id_col, id_row, size, heads)
    y, low, stored2 = normal(y, settle(home, away), 2)
    low3 = pair(low)
    before_t1, hidden_t1, before_i1, hidden_i1, home, away = ffn(s, low3, *ffn_w[1])
    _, last, stored3 = normal(y, settle(home, away), 3)

    grads, norm_grads = {}, [None] * 4

    def normal_back(upstream, sums, stored, i, due=None):
        grad, low, norm_grads[i] = norm_back(s, upstream, sums, stored, params, i)
        return grad, low if due is None else after(due, low)

    def weigh(names, home, away, low, out, *mids, parts=1, due=None):
        got = grid.to_core(away)
        if due is not None:
            got = after(due, got)
        folded = fold(s, home, got)
        low, out, mids = after(folded, (low, out, mids))
        values = weight_grads(s, low, out, *mids, parts)
        grads.update(zip(names, values))
        return (home, got, grid.to_near(folded)), values[0], values[4:]

    def give(names, wide, turn="both"):
        return Give(grid, Bundle(names, wide, turn), grads)

    def send_near(values, gate):
        return [grid.to_near(v) for v in after(gate, values)]

    def join_near(names, came, gate):
        for name, value in zip(names, after(gate, came)):
            grads[name] = plus(grads[name], value)

    g, low = normal_back(upstream, None, stored3, 3)
    out = pair(low)
    bg_t, bg_i, home, away = ffn_back(s, out, before_t1, before_i1, *ffn_w[1])
    sums, weighed, others = weigh(
        ("tu1", "td1", "iu1", "id1"), home, away, low3, out, hidden_t1, bg_t, hidden_i1, bg_i, parts=2
    )
    text3 = give(["tu1", "td1"], width, "y")

    g, low = normal_back(g, sums, stored2, 2, weighed)
    across = grid.to_near(low[: s.li])
    came = send_near(others, across)
    out = pair(jnp.concatenate([low, across]))
    dqkv_t, dqkv_i, home, away = self_back(s, out, *self_w, id_col, id_row, sqkv_t, sqkv_i, size, heads)
    sums, weighed, _ = weigh(
        ("tsi", "tso", "isi", "iso"), home, away, low2, out, sctx_t, dqkv_t, sctx_i, dqkv_i, due=text3.got
    )
    text3.next(away)
    grads["tso"] = grads["tso"][: size * heads]
    text2 = give(["tsi", "isi", "tso"], width, "x")

    g, low = normal_back(g, sums, stored1, 1, (weighed, came))
    join_near(("iu1", "id1"), came, low)
    image3 = give(["id1", "iu1", "iso"], s.ki, "y")
    out = pair(low)
    bg_t, bg_i, home, away = ffn_back(s, out, before_t0, before_i0, *ffn_w[0])
    sums, weighed, others = weigh(
        ("tu0", "td0", "iu0", "id0"), home, away, low1, out, hidden_t0, bg_t, hidden_i0, bg_i,
        parts=2, due=(text3.got, text2.got),
    )
    text3.next(away)
    text2.next(away)
    text1 = give(["tu0", "td0"], width, "x")

    g, low = normal_back(g, sums, stored0, 0, (weighed, image3.got))
    across = grid.to_near(low[: s.li])
    came = send_near(others, across)
    out = pair(jnp.concatenate([low, across]))
    image3.next(low)
    norm_sums = jnp.concatenate(norm_grads)
    moved = grid.to_core(norm_sums)
    dqkv_t, dqkv_i, home, away = co_back(s, out, *co_w, seg_col, segments, qkv_t, qkv_i)
    norm_sums = norm_sums + after(away, moved)
    moved = grid.to_x(norm_sums)
    sums, weighed, _ = weigh(
        ("tci", "tco", "ici", "ico"), home, away, low0, out, ctx_t, dqkv_t, ctx_i, dqkv_i,
        due=(text2.got, text1.got, image3.got),
    )
    text0 = give(["tci", "ici", "tco"], width)
    text2.next(away)
    text1.next(away)
    image3.next(away)
    home, got, other = sums

    gate = text0.got
    text0.next()
    join_near(("iu0", "id0"), came, gate)
    image1 = give(["id0", "iu0", "ico"], s.ki)
    text1.next(gate)
    first = Deliver(grid, [text3, text2, image3], widths, gate)
    norm_sums = norm_sums + after(gate, moved)
    moved = grid.to_y(norm_sums)
    gate = text0.got
    text0.next()
    image1.next(gate)
    first.core(gate)
    norm_sums = norm_sums + after(gate, moved)
    moved = grid.to_near(norm_sums)
    mine = slice(0, s.li + s.tall)
    other = after(gate, other)
    sums = g[mine] + home[mine] + got[mine].astype(F32)
    sums = sums + jnp.concatenate([other[: s.li], other[s.li + s.tall :]]).astype(F32)
    gate = text0.got
    image1.next(gate)
    norm_sums = norm_sums + after(gate, moved)
    moved = [grid.to_column(norm_sums, k) for k in range(1, 2 * rest)]
    done = first.finish(gate)
    last_two = Deliver(grid, [text0, text1, image1], widths)
    norm_sums = sum(after(last_two.got, moved), norm_sums).reshape(4, 4, s.ki)
    last_two.core()
    done.update(last_two.finish())
    norm_outs = [
        lax.dynamic_slice(norm_sums[:, i], (0, place * k), (4, k))[None]
        for i, k in enumerate((tw, tw, iw, iw))
    ]

    def both(first, second):
        return jnp.stack([done[first], done[second]])[None]

    return (
        s.unpack_text(last)[None],
        last[: s.li][None],
        s.unpack_text(sums)[None],
        sums[: s.li][None],
        *(done[n][None] for n in ("tci", "tco", "ici", "ico", "tsi", "tso", "isi", "iso")),
        both("tu0", "tu1"),
        both("td0", "td1"),
        both("iu0", "iu1"),
        both("id0", "id1"),
        *norm_outs,
    )


def solution(mesh):
    depth = mesh.shape["wide"] // 4
    fine = Mesh(mesh.devices.reshape(depth, 2, 2, mesh.shape["narrow"]), ALL)
    rows = P(ALL, None, None)
    weight = P(None, ALL, None)
    pair = P(None, None, ALL, None)
    norm = P(None, None, ALL)
    return jax.shard_map(
        partial(shards, depth=depth),
        mesh=fine,
        in_specs=(rows, rows, P(ALL, None), *[weight] * 8, *[pair] * 4, *[norm] * 4, rows, rows),
        out_specs=(rows, rows, rows, rows, *[weight] * 8, *[pair] * 4, *[norm] * 4),
        check_vma=False,
    )
```

```python
from functools import partial

import jax
import jax.numpy as jnp
from jax import lax
from jax.experimental import pallas as pl
from jax.experimental.pallas import tpu as pltpu
from jax.sharding import Mesh, PartitionSpec as P

HT = 12
HI = 8
HC = 8
REGIONS = 36
EPS = 1e-06
F32 = jnp.float32
BF16 = jnp.bfloat16
ALL = ("far", "near", "low", "y", "core", "x")
FLIP = ((0, 1), (1, 0))
TEAM = 4
PIECE = 8


class Grid:
    def __init__(self, rest):
        self.rest = rest
        self.far, self.near, self.low, self.y, self.core, self.x = (lax.axis_index(name) for name in ALL)
        self.column = self.far * rest + self.low

    def to_core(self, value):
        return lax.ppermute(value, "core", FLIP)

    def to_x(self, value):
        return lax.ppermute(value, "x", FLIP)

    def to_y(self, value):
        return lax.ppermute(value, "y", FLIP)

    def to_near(self, value):
        return lax.ppermute(value, "near", FLIP)

    def to_column(self, value, step):
        columns = 2 * self.rest
        return lax.ppermute(value, ("far", "low"), [(c, (c + step) % columns) for c in range(columns)])

    def swap_far(self, value):
        return lax.ppermute(value, ("far", "core"), ((0, 0), (1, 2), (2, 1), (3, 3)))


def pick(value, index, axis):
    return lax.dynamic_index_in_dim(value, index, axis, keepdims=False)


def paired(own, other, index, axis):
    own, other = jnp.expand_dims(own, axis), jnp.expand_dims(other, axis)
    shape = list(own.shape)
    shape[axis] = 2
    place = lax.broadcasted_iota(jnp.int32, shape, axis)
    return jnp.where(place == index, own, other)


def joined(values, axis):
    return jnp.concatenate(values, axis) if len(values) > 1 else values[0]


def widen(value, width):
    lack = width - value.shape[-1]
    return jnp.pad(value, [(0, 0)] * (value.ndim - 1) + [(0, lack)]) if lack else value


GROUPS = {"tci": 3, "ici": 3, "tsi": 3, "isi": 3, "tu0": 1, "tu1": 1, "iu0": 1, "iu1": 1}
WIDE = 256


def quarters(w, groups):
    r, n = w.shape
    wide = n // groups // TEAM
    parts = widen(w.reshape(r, groups, TEAM, wide), -(-wide // WIDE) * WIDE)
    return parts.transpose(2, 0, 1, 3).reshape(2, 2, r, groups * parts.shape[3])


def from_quarters(parts, groups, n):
    _, _, r, c = parts.shape
    parts = parts.reshape(TEAM, r, groups, c // groups)[..., : n // groups // TEAM]
    return parts.transpose(1, 2, 0, 3).reshape(r, n)


def trade_ins(grid, parts):
    width = max(p.shape[3] for p in parts)
    lines = joined([widen(p, width) for p in parts], 2)
    got = grid.to_near(pick(lines, 1 - grid.near, 1))
    lines = paired(pick(lines, grid.near, 1), got, grid.near, 1)
    came = grid.to_core(pick(lines, 1 - grid.core, 0))
    lines = paired(pick(lines, grid.core, 0), came, grid.core, 0)
    out, at = [], 0
    for p in parts:
        r, c = p.shape[2:]
        out.append(lines[:, :, at : at + r, :c])
        at += r
    return out, (got, came)


class Bundle:
    def __init__(self, names, width, turn="both"):
        self.names, self.width, self.turn = names, width, turn

    def flat(self, value):
        p, r, c = value.shape[-3:]
        lead = value.shape[:-3]
        if p * c == self.width and p > 1:
            value = jnp.concatenate([value[..., k, :, :] for k in range(p)], -1)
        else:
            value = value.reshape(lead + (p * r, c))
        lack = -value.shape[-2] % PIECE
        if lack:
            value = jnp.pad(value, [(0, 0)] * len(lead) + [(0, lack), (0, 0)])
        return value.reshape(lead + (-1, PIECE, self.width))

    def count(self, shape):
        p, r, c = shape
        return -(-(r if p * c == self.width else p * r) // PIECE)

    def unflat(self, lines, shape):
        p, r, c = shape
        lead = lines.shape[:-3]
        lines = lines.reshape(lead + (-1, self.width))
        if p * c == self.width and p > 1:
            return jnp.stack([lines[..., :r, k * c : (k + 1) * c] for k in range(p)], -3)
        return lines[..., : p * r, :].reshape(lead + (p, r, c))


class Gather:
    def __init__(self, grid, bundles, parts):
        self.grid, self.bundles, self.parts = grid, bundles, parts
        self.blocks, self.sides, self.corners = {}, {}, {}
        self.gate = ()

    def chunk(self, i):
        bundle = self.bundles[i]
        return joined([bundle.flat(self.parts[n]) for n in bundle.names], 0)

    def cut(self, i, n):
        return {"both": n // 2, "x": n, "y": 0}[self.bundles[i].turn]

    def round(self, moves, also=()):
        grid, columns = self.grid, 2 * self.grid.rest
        sends = []
        for kind, i in moves:
            if kind == "z":
                sends.append(self.chunk(i))
            elif kind == "xy":
                sends.append(self.blocks[i])
            else:
                by_x, by_y = self.sides[i]
                cut = self.cut(i, by_x.shape[1])
                sends.append((by_x[:, :cut], by_y[:, cut:]))
        if self.gate or also:
            sends, _ = lax.optimization_barrier((sends, (self.gate, also)))
        self.gate = ()
        for (kind, i), value in zip(moves, sends):
            if kind == "c":
                got = ()
                if value[0].shape[1]:
                    got += (grid.to_y(value[0]),)
                if value[1].shape[1]:
                    got += (grid.to_x(value[1]),)
                self.corners[i] = got
            elif kind == "xy":
                self.blocks[i] = value
                got = self.sides[i] = (grid.to_x(value), grid.to_y(value))
            else:
                got = tuple(grid.to_column(value, k) for k in range(1, columns))
                order = (value, *got)
                places = []
                for place in range(columns):
                    here = order[0]
                    for k in range(1, columns):
                        here = jnp.where((grid.column - place) % columns == k, order[k], here)
                    places.append(here)
                self.blocks[i] = jnp.stack(places)
            self.gate += got

    def full(self, i, gate=None):
        grid, bundle, parts = self.grid, self.bundles[i], self.parts
        corner = joined(self.corners[i] if gate is None else after(gate, self.corners[i]), 1)
        full, at = {}, 0
        for name in bundle.names:
            shape = parts[name].shape
            p, r, c = shape
            n = bundle.count(shape)
            cut = [bundle.unflat(b[:, at : at + n], shape) for b in (self.blocks[i], *self.sides[i], corner)]
            at += n
            if p == TEAM:
                cut = [b.reshape(2, grid.rest, 2, 2, r, c).transpose(0, 3, 1, 2, 4, 5) for b in cut]
                cut = [b[:, :, :, None, :, None] for b in cut]
                place = (3, 5)
            else:
                cut = [b.reshape(2, grid.rest, r, c).swapaxes(0, 1)[:, None, :, None] for b in cut]
                place = (1, 3)
            size = list(cut[0].shape)
            size[place[0]] = size[place[1]] = 2
            here_y = lax.broadcasted_iota(jnp.int32, size, place[0]) == grid.y
            here_x = lax.broadcasted_iota(jnp.int32, size, place[1]) == grid.x
            own, ox, oy, oxy = cut
            value = jnp.where(here_y, jnp.where(here_x, own, ox), jnp.where(here_x, oy, oxy))
            full[name] = lax.optimization_barrier(value).reshape(-1, c)
        return full


def plus(a, *more):
    total = a.astype(F32)
    for b in more:
        total = total + b.astype(F32)
    return total.astype(BF16)


def lay_kernel(core, mine, came, *outs, shapes):
    first = core[0] == 0
    at = 0
    for (r, c, groups, n), out in zip(shapes, outs):
        wide = n // groups // TEAM
        step = c // groups
        for near in range(2):
            a = mine[near, pl.ds(at, r), :].astype(F32)
            b = came[near, pl.ds(at, r), :].astype(F32)
            for k, value in enumerate((jnp.where(first, a, b), jnp.where(first, b, a))):
                for g in range(groups):
                    to = g * (n // groups) + (2 * k + near) * wide
                    out[:, to : to + wide] = value[:, g * step : g * step + wide]
        at += r


def lay_out(core, mine, came, shapes):
    if any(r % 8 for r, _, _, _ in shapes):
        lines, at, outs = paired(mine, came, core, 0), 0, []
        for r, c, groups, n in shapes:
            outs.append(from_quarters(lines[:, :, at : at + r, :c], groups, n).astype(F32))
            at += r
        return outs
    size = 4 * mine.size + sum(4 * r * n for r, _, _, n in shapes)
    return pl.pallas_call(
        partial(lay_kernel, shapes=shapes),
        out_shape=[jax.ShapeDtypeStruct((r, n), F32) for r, _, _, n in shapes],
        in_specs=[pl.BlockSpec(memory_space=pltpu.SMEM)] + [pl.BlockSpec(memory_space=pltpu.VMEM)] * 2,
        compiler_params=pltpu.CompilerParams(vmem_limit_bytes=2 * size + (8 << 20)),
        cost_estimate=pl.CostEstimate(flops=size, bytes_accessed=size, transcendentals=0),
    )(core.astype(jnp.int32).reshape(1), mine, came)


def after(gate, value):
    return lax.optimization_barrier((value, gate))[0]


class Give:
    def __init__(self, grid, bundle, grads):
        self.grid, self.bundle, self.step = grid, bundle, 0
        rest = grid.rest
        self.views, self.shapes = [], []
        for name in bundle.names:
            k, c = grads[name].shape
            if name in GROUPS:
                r = k // (rest * 32)
                self.views.append(grads[name].reshape(2, 2, rest, 2, 2, 2, r, c))
                self.shapes.append((TEAM, r, c))
            else:
                r = k // (rest * 8)
                self.views.append(grads[name].reshape(rest, 2, 2, 2, r, c))
                self.shapes.append((1, r, c))
        self.names = list(bundle.names)

    def block(self, y, x):
        pieces = []
        for view, (p, r, c) in zip(self.views, self.shapes):
            if p == TEAM:
                value = pick(pick(view, x, 5), y, 3).transpose(0, 2, 3, 1, 4, 5)
            else:
                value = pick(pick(view, x, 3), y, 1).swapaxes(0, 1)
            pieces.append(self.bundle.flat(value.reshape(2 * self.grid.rest, p, r, c)))
        return joined(pieces, 1)

    def next(self, gate):
        if self.step:
            self.got = after(gate, self.got)
        else:
            self.views = after(gate, self.views)
        step, self.step = self.step, self.step + 1
        (self.corner, self.side, self.column)[step]()

    def corner(self):
        grid = self.grid
        corner = self.block(1 - grid.y, 1 - grid.x)
        n = corner.shape[1]
        self.cut = {"both": n // 2, "x": 0, "y": n}[self.bundle.turn]
        self.got = ()
        if self.cut:
            self.got += (grid.to_y(corner[:, : self.cut]),)
        if self.cut < n:
            self.got += (grid.to_x(corner[:, self.cut :]),)

    def side(self):
        grid, cut, got = self.grid, self.cut, list(self.got)
        x = self.block(grid.y, 1 - grid.x)
        y = self.block(1 - grid.y, grid.x)
        n = x.shape[1]
        if cut == n:
            x = plus(x, got[0])
        elif cut == 0:
            y = plus(y, got[0])
        else:
            x = jnp.concatenate([plus(x[:, :cut], got[0]), x[:, cut:]], 1)
            y = jnp.concatenate([y[:, :cut], plus(y[:, cut:], got[1])], 1)
        self.got = grid.to_x(x), grid.to_y(y)

    def column(self):
        grid, columns = self.grid, 2 * self.grid.rest
        chunk = plus(self.block(grid.y, grid.x), *self.got)
        self.mine = pick(chunk, grid.column, 0)
        self.got = tuple(
            grid.to_column(pick(chunk, (grid.column + k) % columns, 0), k) for k in range(1, columns)
        )


class Deliver:
    def __init__(self, grid, gives, widths, gate=None):
        self.grid, self.widths = grid, widths
        self.quads, self.outs = [], []
        for give in gives:
            got = give.got if gate is None else after(gate, give.got)
            total, at = plus(give.mine, *got), 0
            for name, shape in zip(give.names, give.shapes):
                n = give.bundle.count(shape)
                part = give.bundle.unflat(total[at : at + n], shape)
                if name in GROUPS:
                    self.quads.append((name, part.reshape((2, 2) + part.shape[1:])))
                else:
                    self.outs.append((name, part[0]))
                at += n
        width = max(q.shape[3] for _, q in self.quads)
        lines = joined([widen(q, width) for _, q in self.quads], 2)
        self.mine, self.came = pick(lines, grid.near, 1), grid.to_near(pick(lines, 1 - grid.near, 1))
        width = max(o.shape[1] for _, o in self.outs)
        self.swapped = grid.swap_far(joined([widen(o, width) for _, o in self.outs], 0))
        self.got = self.came

    def core(self, gate=None):
        grid = self.grid
        came = self.came if gate is None else after(gate, self.came)
        lines = paired(self.mine, came, grid.near, 1)
        self.mine, self.came = pick(lines, grid.core, 0), grid.to_core(pick(lines, 1 - grid.core, 0))
        self.got = self.came

    def finish(self, gate=None):
        came, swapped = self.came, self.swapped
        if gate is not None:
            came, swapped = after(gate, (came, swapped))
        shapes = [(*quad.shape[2:], GROUPS[name], self.widths[name]) for name, quad in self.quads]
        done = dict(zip((n for n, _ in self.quads), lay_out(self.grid.core, self.mine, came, shapes)))
        at = 0
        for name, out in self.outs:
            r, c = out.shape
            done[name] = swapped[at : at + r, :c].astype(F32)
            at += r
        return done


class Sizes:
    def __init__(self, lt, kt, li, ki):
        self.lt, self.kt, self.li, self.ki = lt, kt, li, ki
        self.third, self.tall, self.left = kt // 3, lt * 3 // 4, lt // 4
        self.below = li + 2 * self.tall
        self.rows = self.below + li

    def text(self, ref, r):
        base = self.li + r * self.tall
        top = ref[pl.ds(base, self.tall), : self.kt]
        last = [ref[pl.ds(base + j * self.left, self.left), self.kt :] for j in range(3)]
        return jnp.concatenate([top, jnp.concatenate(last, 1)], 0)

    def put_text(self, ref, r, text):
        base = self.li + r * self.tall
        text = text.astype(ref.dtype)
        ref[pl.ds(base, self.tall), : self.kt] = text[: self.tall]
        for j in range(3):
            block = text[self.tall :, j * self.third : (j + 1) * self.third]
            ref[pl.ds(base + j * self.left, self.left), self.kt :] = block

    def image(self, ref, r=0):
        return ref[pl.ds(r * self.below, self.li), :]

    def put_image(self, ref, image, r=0):
        ref[pl.ds(r * self.below, self.li), :] = image.astype(ref.dtype)

    def pack_rows(self, text, image):
        last = text[self.tall :]
        last = [last[:, j * self.third : (j + 1) * self.third] for j in range(3)]
        return jnp.concatenate([image, jnp.concatenate([text[: self.tall], jnp.concatenate(last, 0)], 1)], 0)

    def unpack_text(self, rows):
        rows = rows[self.li : self.li + self.tall]
        last = [rows[j * self.left : (j + 1) * self.left, self.kt :] for j in range(3)]
        return jnp.concatenate([rows[:, : self.kt], jnp.concatenate(last, 1)], 0)

    def both(self, near, far):
        text = [self.text(ref, r) for ref in (near, far) for r in range(2)]
        image = [self.image(ref, r) for ref in (near, far) for r in range(2)]
        return jnp.concatenate(text, 0), jnp.concatenate(image, 0)

    def put_sums(self, home, away, text, image):
        for r in range(TEAM):
            ref = (home, away)[r // 2]
            self.put_text(ref, r % 2, text[r * self.lt : (r + 1) * self.lt])
            self.put_image(ref, image[r * self.li : (r + 1) * self.li], r % 2)

    def sums(self):
        shape = (self.rows, self.ki)
        return [(shape, F32), (shape, BF16)]


def kernel(body, outs, args, flops, scratch=()):
    outs = [jax.ShapeDtypeStruct(shape, kind) for shape, kind in outs]
    size = sum(a.size * a.dtype.itemsize for a in (*args, *outs))
    return pl.pallas_call(
        body,
        out_shape=outs,
        scratch_shapes=[pltpu.VMEM(shape, kind) for shape, kind in scratch],
        compiler_params=pltpu.CompilerParams(vmem_limit_bytes=int(1.25 * size) + (14 << 20)),
        cost_estimate=pl.CostEstimate(flops=flops, bytes_accessed=size, transcendentals=0),
    )(*args)


def mm(a, b):
    return jnp.dot(a, b, preferred_element_type=F32)


def mm_bt(a, b):
    return lax.dot_general(a, b, (((1,), (1,)), ((), ())), preferred_element_type=F32)


def mm_at(a, b):
    return lax.dot_general(a, b, (((0,), (0,)), ((), ())), preferred_element_type=F32)


def gelu(v):
    return 0.5 * v * (1.0 + lax.erf(v * (0.5**0.5)))


def gelu_slope(v):
    return 0.5 * (1.0 + lax.erf(v * (0.5**0.5))) + v * jnp.exp(-0.5 * v * v) * (0.5 / jnp.pi) ** 0.5


def ffn_kernel(near, far, ut, dt, ui, di, before_t, hidden_t, before_i, hidden_i, home, away, *, s):
    text, image = s.both(near, far)
    sums = []
    for low, up, down, before, hidden in (
        (text, ut, dt, before_t, hidden_t),
        (image, ui, di, before_i, hidden_i),
    ):
        pre = mm(low, up[...])
        before[...] = pre
        act = gelu(pre).astype(BF16)
        hidden[...] = act
        sums.append(mm(act, down[...]))
    s.put_sums(home, away, *sums)


def ffn(s, low, ut, dt, ui, di):
    ft, fi = ut.shape[1], ui.shape[1]
    outs = []
    for length, f in ((TEAM * s.lt, ft), (TEAM * s.li, fi)):
        outs += [((length, f), F32), ((length, f), BF16)]
    flops = 16 * (s.lt * s.kt * ft + s.li * s.ki * fi)
    return kernel(partial(ffn_kernel, s=s), outs + s.sums(), (*low, ut, dt, ui, di), flops)


def ffn_back_kernel(near, far, before_t, before_i, ut, dt, ui, di, bg_t, bg_i, home, away, *, s):
    text, image = s.both(near, far)
    sums = []
    for out, before, up, down, bg in (
        (text, before_t, ut, dt, bg_t),
        (image, before_i, ui, di, bg_i),
    ):
        grad = (mm_bt(out, down[...]) * gelu_slope(before[...])).astype(BF16)
        bg[...] = grad
        sums.append(mm_bt(grad, up[...]))
    s.put_sums(home, away, *sums)


def ffn_back(s, out, before_t, before_i, ut, dt, ui, di):
    ft, fi = ut.shape[1], ui.shape[1]
    outs = [((TEAM * s.lt, ft), BF16), ((TEAM * s.li, fi), BF16)] + s.sums()
    flops = 16 * (s.lt * s.kt * ft + s.li * s.ki * fi)
    args = (*out, before_t, before_i, ut, dt, ui, di)
    return kernel(partial(ffn_back_kernel, s=s), outs, args, flops)


def softmax_of(q, k, allowed, factor):
    scores = jnp.where(allowed, mm_bt(q, k) * factor, -1e30)
    exponent = jnp.exp(scores - jnp.max(scores, -1, keepdims=True))
    return exponent / jnp.sum(exponent, -1, keepdims=True)


def head_back(q, k, v, grad, allowed, factor):
    probs = softmax_of(q, k, allowed, factor)
    dv = mm_at(probs.astype(BF16), grad)
    dp = mm_bt(grad, v)
    ds = (probs * (dp - jnp.sum(dp * probs, -1, keepdims=True))).astype(BF16)
    return mm(ds, k) * factor, mm_at(ds, q) * factor, dv


LANES = 128


def lane_part(size, sub):
    lane = lax.broadcasted_iota(jnp.int32, (1, LANES), 1)
    return jnp.logical_and(lane >= sub * size, lane < (sub + 1) * size)


def half_ids(length):
    col = lax.broadcasted_iota(jnp.int32, (length, 1), 0) >= length // 2
    row = lax.broadcasted_iota(jnp.int32, (1, length), 1) >= length // 2
    return col, row


def thirds(tile, wide):
    return [pl.ds(i * wide + tile * LANES, LANES) for i in range(3)]


def image_places(s):
    for r in range(TEAM):
        yield pl.ds(r * s.li, s.li)


def self_kernel(near, far, wt, wot, wi, woi, col, row, qkv_t, ctx_t, qkv_i, ctx_i, home, away, *, s, size, heads):
    text, image = s.both(near, far)
    qkv_t[...] = mm(text, wt[...]).astype(BF16)
    qkv_i[...] = mm(image, wi[...]).astype(BF16)
    wide = ctx_t.shape[1]
    allowed = col[...] == row[...]
    for tile in range(wide // LANES):
        q, k, v = (qkv_t[:, at] for at in thirds(tile, wide))
        total = jnp.zeros(q.shape, F32)
        for sub in range(min(LANES // size, heads - tile * (LANES // size))):
            lanes = lane_part(size, sub)
            probs = softmax_of(jnp.where(lanes, q, 0), k, allowed, size**-0.5)
            total = total + jnp.where(lanes, mm(probs.astype(BF16), v), 0.0)
        ctx_t[:, pl.ds(tile * LANES, LANES)] = total.astype(BF16)
    wide = ctx_i.shape[1]
    own, other = half_ids(s.li)
    for at in image_places(s):
        for tile in range(wide // LANES):
            q, k, v = (qkv_i[at, lanes] for lanes in thirds(tile, wide))
            probs = softmax_of(q, k, own == other, LANES**-0.5)
            ctx_i[at, pl.ds(tile * LANES, LANES)] = mm(probs.astype(BF16), v).astype(BF16)
    s.put_sums(home, away, mm(ctx_t[...], wot[...]), mm(ctx_i[...], woi[...]))


def attention_outs(s, wt, wi):
    outs = []
    for length, n in ((s.lt, wt.shape[1]), (s.li, wi.shape[1])):
        outs += [((TEAM * length, n), BF16), ((TEAM * length, n // 3), BF16)]
    return outs


def attention_flops(s, wt, wi):
    return 12 * (s.lt * s.kt * wt.shape[1] + s.li * s.ki * wi.shape[1])


def self_attention(s, low, wt, wot, wi, woi, col, row, size, heads):
    outs = attention_outs(s, wt, wi) + s.sums()
    args = (*low, wt, wot, wi, woi, col, row)
    return kernel(partial(self_kernel, s=s, size=size, heads=heads), outs, args, attention_flops(s, wt, wi))


def self_back_kernel(
    near, far, wt, wot, wi, woi, col, row, qkv_t, qkv_i, dqkv_t, dqkv_i, home, away, dctx_t, dctx_i, *, s, size, heads
):
    text, image = s.both(near, far)
    dctx_t[...] = mm_bt(text, wot[...]).astype(BF16)
    dctx_i[...] = mm_bt(image, woi[...]).astype(BF16)
    wide = dctx_t.shape[1]
    allowed = col[...] == row[...]
    for tile in range(wide // LANES):
        q, k, v = (qkv_t[:, at] for at in thirds(tile, wide))
        grad = dctx_t[:, pl.ds(tile * LANES, LANES)]
        totals = [jnp.zeros(q.shape, F32) for _ in range(3)]
        for sub in range(min(LANES // size, heads - tile * (LANES // size))):
            lanes = lane_part(size, sub)
            dq, dk, dv = head_back(
                jnp.where(lanes, q, 0), k, v, jnp.where(lanes, grad, 0), allowed, size**-0.5
            )
            totals = [totals[0] + jnp.where(lanes, dq, 0.0), totals[1] + dk, totals[2] + dv]
        for at, total in zip(thirds(tile, wide), totals):
            dqkv_t[:, at] = total.astype(BF16)
    wide = dctx_i.shape[1]
    own, other = half_ids(s.li)
    for at in image_places(s):
        for tile in range(wide // LANES):
            columns = thirds(tile, wide)
            q, k, v = (qkv_i[at, lanes] for lanes in columns)
            grad = dctx_i[at, pl.ds(tile * LANES, LANES)]
            grads = head_back(q, k, v, grad, own == other, LANES**-0.5)
            for lanes, value in zip(columns, grads):
                dqkv_i[at, lanes] = value.astype(BF16)
    s.put_sums(home, away, mm_bt(dqkv_t[...], wt[...]), mm_bt(dqkv_i[...], wi[...]))


def back_outs(s, wt, wi):
    outs = [((TEAM * s.lt, wt.shape[1]), BF16), ((TEAM * s.li, wi.shape[1]), BF16)] + s.sums()
    scratch = [((TEAM * s.lt, wt.shape[1] // 3), BF16), ((TEAM * s.li, wi.shape[1] // 3), BF16)]
    return outs, scratch


def self_back(s, out, wt, wot, wi, woi, col, row, qkv_t, qkv_i, size, heads):
    outs, scratch = back_outs(s, wt, wi)
    args = (*out, wt, wot, wi, woi, col, row, qkv_t, qkv_i)
    body = partial(self_back_kernel, s=s, size=size, heads=heads)
    return kernel(body, outs, args, attention_flops(s, wt, wi), scratch)


def co_places(s, seg_col, seg_row):
    col, row = half_ids(s.li)
    for r in range(TEAM):
        text, image = pl.ds(r * s.lt, s.lt), pl.ds(r * s.li, s.li)
        text_col = seg_col[text, :] > 0.5
        text_row = seg_row[pl.ds(r, 1), :] > 0.5
        yield text, image, text_col == row, col == text_row


def co_kernel(
    near, far, wt, wot, wi, woi, seg_col, seg_row, qkv_t, ctx_t, qkv_i, ctx_i, home, away, *, s
):
    text, image = s.both(near, far)
    qkv_t[...] = mm(text, wt[...]).astype(BF16)
    qkv_i[...] = mm(image, wi[...]).astype(BF16)
    wide = ctx_t.shape[1]
    for text, image, cross, back in co_places(s, seg_col, seg_row):
        for tile in range(wide // LANES):
            q, k, v = thirds(tile, wide)
            probs = softmax_of(qkv_t[text, q], qkv_i[image, k], cross, LANES**-0.5)
            ctx_t[text, q] = mm(probs.astype(BF16), qkv_i[image, v]).astype(BF16)
            probs = softmax_of(qkv_i[image, q], qkv_t[text, k], back, LANES**-0.5)
            ctx_i[image, q] = mm(probs.astype(BF16), qkv_t[text, v]).astype(BF16)
    s.put_sums(home, away, mm(ctx_t[...], wot[...]), mm(ctx_i[...], woi[...]))


def co_attention(s, low, wt, wot, wi, woi, seg_col, seg_row):
    outs = attention_outs(s, wt, wi) + s.sums()
    args = (*low, wt, wot, wi, woi, seg_col, seg_row)
    return kernel(partial(co_kernel, s=s), outs, args, attention_flops(s, wt, wi))


def co_back_kernel(
    near, far, wt, wot, wi, woi, seg_col, seg_row, qkv_t, qkv_i, dqkv_t, dqkv_i, home, away, dctx_t, dctx_i, *, s
):
    text, image = s.both(near, far)
    dctx_t[...] = mm_bt(text, wot[...]).astype(BF16)
    dctx_i[...] = mm_bt(image, woi[...]).astype(BF16)
    wide = dctx_t.shape[1]
    for text, image, cross, back in co_places(s, seg_col, seg_row):
        for tile in range(wide // LANES):
            q, k, v = thirds(tile, wide)
            dq, dk, dv = head_back(
                qkv_t[text, q], qkv_i[image, k], qkv_i[image, v], dctx_t[text, q], cross, LANES**-0.5
            )
            dqkv_t[text, q] = dq.astype(BF16)
            dqkv_i[image, k] = dk.astype(BF16)
            dqkv_i[image, v] = dv.astype(BF16)
            dq, dk, dv = head_back(
                qkv_i[image, q], qkv_t[text, k], qkv_t[text, v], dctx_i[image, q], back, LANES**-0.5
            )
            dqkv_i[image, q] = dq.astype(BF16)
            dqkv_t[text, k] = dk.astype(BF16)
            dqkv_t[text, v] = dv.astype(BF16)
    s.put_sums(home, away, mm_bt(dqkv_t[...], wt[...]), mm_bt(dqkv_i[...], wi[...]))


def co_back(s, out, wt, wot, wi, woi, seg_col, seg_row, qkv_t, qkv_i):
    outs, scratch = back_outs(s, wt, wi)
    args = (*out, wt, wot, wi, woi, seg_col, seg_row, qkv_t, qkv_i)
    return kernel(partial(co_back_kernel, s=s), outs, args, attention_flops(s, wt, wi), scratch)


def weight_kernel(near, far, out_near, out_far, mid_t, grad_t, mid_i, grad_i, in_t, out_t, in_i, out_i, *, s):
    text, image = s.both(near, far)
    in_t[...] = mm_at(text, grad_t[...]).astype(BF16)
    in_i[...] = mm_at(image, grad_i[...]).astype(BF16)
    text, image = s.both(out_near, out_far)
    out_t[...] = mm_at(mid_t[...], text).astype(BF16)
    out_i[...] = mm_at(mid_i[...], image).astype(BF16)


def weight_grads(s, low, out, mid_t, grad_t, mid_i, grad_i):
    outs = []
    for k, mid, grad in ((s.kt, mid_t, grad_t), (s.ki, mid_i, grad_i)):
        outs += [((k, grad.shape[1]), BF16), ((mid.shape[1], k), BF16)]
    flops = sum(8 * s.lt * shape[0] * shape[1] for shape, _ in outs)
    args = (*low, *out, mid_t, grad_t, mid_i, grad_i)
    return kernel(partial(weight_kernel, s=s), outs, args, flops)


def fold_kernel(home, got, out):
    out[...] = (home[...] + got[...].astype(F32)).astype(BF16)


def fold(s, home, got):
    return kernel(fold_kernel, [((s.rows, s.ki), BF16)], (home, got), home.size)[0]


def settled(read, base, home, got, other, r):
    return read(base, r).astype(F32) + read(home, r) + read(got, r).astype(F32) + read(other, 1 - r).astype(F32)


def streams(s, params, i, k):
    return (
        (s.text, lambda ref, r, v: s.put_text(ref, r, v), params[pl.ds(4 * k + i, 1), : s.kt], 2 * s.li, s.lt),
        (s.image, lambda ref, r, v: s.put_image(ref, v, r), params[pl.ds(8 + 4 * k + i, 1), :], 0, s.li),
    )


def norm_kernel(values, home, got, other, params, out, low, normed, inverse, *, s, i):
    for (read, put, gain, start, length), (_, _, shift, _, _) in zip(streams(s, params, i, 0), streams(s, params, i, 1)):
        for r in range(2):
            v = settled(read, values, home, got, other, r)
            centred = v - jnp.mean(v, -1, keepdims=True)
            inv = lax.rsqrt(jnp.mean(centred * centred, -1, keepdims=True) + EPS)
            n = centred * inv
            inverse[pl.ds(start + r * length, length), :] = inv
            y = n * gain + shift
            for ref, value in ((normed, n), (out, y), (low, y)):
                put(ref, r, value)


def norm(s, values, sums, params, i):
    pack = (s.rows, s.ki)
    outs = [(pack, F32), (pack, BF16), (pack, F32), ((2 * s.li + 2 * s.lt, 1), F32)]
    y, low, *stored = kernel(partial(norm_kernel, s=s, i=i), outs, (values, *sums, params), 32 * s.rows * s.ki)
    return y, low, stored


def norm_back_kernel(*refs, s, i, first):
    if first:
        up, normed, inverse, params, grad, low, sums = refs
    else:
        up, home, got, other, normed, inverse, params, grad, low, sums = refs
    sums[...] = jnp.zeros(sums.shape, F32)
    for stream, (read, put, gain, start, length) in enumerate(streams(s, params, i, 0)):
        for r in range(2):
            u = read(up, r).astype(F32) if first else settled(read, up, home, got, other, r)
            n = read(normed, r)
            scaled = u * gain
            value = inverse[pl.ds(start + r * length, length), :] * (
                scaled - jnp.mean(scaled, -1, keepdims=True) - n * jnp.mean(scaled * n, -1, keepdims=True)
            )
            put(grad, r, value)
            put(low, r, value)
            if r == 0:
                width = u.shape[1]
                sums[pl.ds(2 * stream, 1), :width] = jnp.sum(u * n, axis=0, keepdims=True)
                sums[pl.ds(2 * stream + 1, 1), :width] = jnp.sum(u, axis=0, keepdims=True)


def norm_back(s, upstream, sums, stored, params, i):
    pack = (s.rows, s.ki)
    outs = [(pack, F32), (pack, BF16), ((4, s.ki), F32)]
    body = partial(norm_back_kernel, s=s, i=i, first=sums is None)
    return kernel(body, outs, (upstream, *(sums or ()), *stored, params), 32 * s.rows * s.ki)


FETCH = (
    Bundle(["tci", "ici", "tco", "icoa", "icob"], 768),
    Bundle(["id0", "iu0", "iso"], 1024, "x"),
    Bundle(["tu0", "td0"], 768, "y"),
    Bundle(["tsi", "isi", "tso"], 768, "x"),
    Bundle(["id1", "iu1"], 1024, "y"),
    Bundle(["tu1", "td1"], 768, "y"),
)


def shards(
    text_in,
    image_in,
    text_segments,
    text_co_in,
    text_co_out,
    image_co_in,
    image_co_out,
    text_self_in,
    text_self_out,
    image_self_in,
    image_self_out,
    text_up,
    text_down,
    image_up,
    image_down,
    text_gains,
    text_shifts,
    image_gains,
    image_shifts,
    grad_text_out,
    grad_image_out,
    rest,
):
    grid = Grid(rest)
    tw, iw = text_gains.shape[2], image_gains.shape[2]
    s = Sizes(*text_in.shape[1:], *image_in.shape[1:])
    weights = {
        "tci": text_co_in[0],
        "tco": text_co_out[0],
        "ici": image_co_in[0],
        "ico": image_co_out[0],
        "tsi": text_self_in[0],
        "tso": text_self_out[0],
        "isi": image_self_in[0],
        "iso": image_self_out[0],
        "tu0": text_up[0, 0],
        "tu1": text_up[0, 1],
        "td0": text_down[0, 0],
        "td1": text_down[0, 1],
        "iu0": image_up[0, 0],
        "iu1": image_up[0, 1],
        "id0": image_down[0, 0],
        "id1": image_down[0, 1],
    }

    weights["icoa"] = image_co_out[0][:, : FETCH[0].width]
    weights["icob"] = widen(image_co_out[0][:, FETCH[0].width :], FETCH[0].width)
    place = ((((grid.far * 2 + grid.near) * rest + grid.low) * 2 + grid.y) * 2 + grid.core) * 2 + grid.x
    params = jnp.zeros((16, s.ki), BF16)
    for at, k, kinds in ((0, tw, (text_gains, text_shifts)), (8, iw, (image_gains, image_shifts))):
        own = jnp.concatenate([a[0] for a in kinds])
        params = lax.dynamic_update_slice(params, own, (at, place * k))
    width = FETCH[0].width
    widths = {name: weights[name].shape[1] for name in GROUPS}
    quads = {name: quarters(weights[name], groups) for name, groups in GROUPS.items()}
    parts = {}

    def trade(names):
        got, _ = trade_ins(grid, [quads[n] for n in names])
        for n, q in zip(names, got):
            parts[n] = q.reshape((TEAM,) + q.shape[2:])

    def swap(names):
        swapped, at = grid.swap_far(joined([weights[n] for n in names], 0)), 0
        for n in names:
            r = weights[n].shape[0]
            parts[n] = swapped[at : at + r][None]
            at += r

    def pair(own):
        return own, grid.to_core(own)

    trade(("tci", "ici"))
    swap(("tco", "icoa", "icob"))
    segments = text_segments.astype(F32)
    segments = jnp.concatenate(pair(jnp.concatenate([segments, grid.to_near(segments)])))
    params = params + grid.to_x(params)
    params = params + grid.to_y(params)
    params = params + grid.to_core(params)

    def more(move):
        nonlocal params, moved
        params = params + after(fetch.gate, moved)
        moved = move(params)

    fetch = Gather(grid, FETCH, parts)
    moved = grid.to_near(params)
    fetch.round([("z", 0)])

    def later(ins, outs, *inputs):
        new = {n: quads[n] for n in ins}, {n: weights[n] for n in sum(outs, ())}, inputs
        new_quads, new_weights, inputs = after(fetch.gate, new)
        quads.update(new_quads)
        weights.update(new_weights)
        trade(ins)
        for names in outs:
            swap(names)
        return inputs

    text_in, image_in = later(
        ("iu0", "tu0", "tsi", "isi", "iu1", "tu1"), (("id0", "iso", "id1"), ("td0", "tso", "td1")), text_in, image_in
    )
    own = s.pack_rows(text_in[0], image_in[0])
    got = grid.to_near(own)
    values = jnp.concatenate([own, got[s.li :], got[: s.li]])
    low0 = pair(values)
    fetch.round([("xy", 0)])

    seg_col = segments.reshape(-1, 1)
    ids = segments + 2.0 * jnp.arange(TEAM, dtype=F32)[:, None]
    id_col, id_row = ids.reshape(-1, 1), ids.reshape(1, -1)
    size, heads = s.kt // HT, HT // TEAM

    def settle(home, away):
        got = grid.to_core(away)
        return home, got, grid.to_near(fold(s, home, got))

    def normal(values, sums, i):
        return norm(s, values, sums, params, i)

    more(lambda value: sum((grid.to_column(value, k) for k in range(2, 2 * rest)), grid.to_column(value, 1)))
    fetch.round([("c", 0), ("z", 1)])
    params = (params + after(fetch.gate, moved)).astype(F32)
    grad_text_out, grad_image_out = after(fetch.gate, (grad_text_out, grad_image_out))
    own = s.pack_rows(grad_text_out[0], grad_image_out[0])
    got = grid.to_near(own)
    upstream = jnp.concatenate([own, got[s.li :], got[: s.li]])
    full = fetch.full(0)
    full["ico"] = jnp.concatenate([full["icoa"], full["icob"][:, : s.ki - width]], 1)
    co_w = [full[n] for n in ("tci", "tco", "ici", "ico")]
    fetch.round([("xy", 1), ("z", 2)])
    qkv_t, ctx_t, qkv_i, ctx_i, home, away = co_attention(s, low0, *co_w, seg_col, segments)
    fetch.round([("c", 1), ("xy", 2), ("z", 3)], away)
    sums = settle(home, away)
    full.update(fetch.full(1, sums[1]))
    y, low, stored0 = normal(values, sums, 0)
    low1 = pair(low)
    fetch.round([("c", 2), ("xy", 3), ("z", 4)], sums[1])
    full.update(fetch.full(2, low))
    ffn_w = [[full["tu0"], full["td0"], full["iu0"], full["id0"]]]
    before_t0, hidden_t0, before_i0, hidden_i0, home, away = ffn(s, low1, *ffn_w[0])
    fetch.round([("c", 3), ("xy", 4), ("z", 5)], low)
    full.update(fetch.full(3, away))
    full["tso"] = jnp.pad(full["tso"], ((0, full["tsi"].shape[1] // 3 - full["tso"].shape[0]), (0, 0)))
    self_w = [full[n] for n in ("tsi", "tso", "isi", "iso")]
    fetch.round([("c", 4), ("xy", 5)], away)
    y, low, stored1 = normal(y, settle(home, away), 1)
    low2 = pair(low)
    sqkv_t, sctx_t, sqkv_i, sctx_i, home, away = self_attention(s, low2, *self_w, id_col, id_row, size, heads)
    fetch.round([("c", 5)], low)
    full.update(fetch.full(4, away))
    sums = settle(home, away)
    full.update(fetch.full(5, sums[1]))
    ffn_w.append([full["tu1"], full["td1"], full["iu1"], full["id1"]])
    y, low, stored2 = normal(y, sums, 2)
    low3 = pair(low)
    before_t1, hidden_t1, before_i1, hidden_i1, home, away = ffn(s, low3, *ffn_w[1])
    _, last, stored3 = normal(y, settle(home, away), 3)

    grads, norm_grads = {}, [None] * 4

    def normal_back(upstream, sums, stored, i, due=None):
        grad, low, norm_grads[i] = norm_back(s, upstream, sums, stored, params, i)
        return grad, low if due is None else after(due, low)

    def weigh(names, home, away, low, out, *mids, due=None):
        got = grid.to_core(away)
        if due is not None:
            got = after(due, got)
        folded = fold(s, home, got)
        low, out, mids = after(folded, (low, out, mids))
        values = weight_grads(s, low, out, *mids)
        grads.update(zip(names, values))
        return home, got, folded, values[0]

    def give(names, wide, turn="both"):
        return Give(grid, Bundle(names, wide, turn), grads)

    arrived = ()

    def steps(*gives, also=()):
        nonlocal arrived
        gate = arrived, also
        for each in gives:
            each.next(gate)
        arrived = tuple(each.got for each in gives)

    g, low = normal_back(upstream, None, stored3, 3)
    out = pair(low)
    bg_t, bg_i, home, away = ffn_back(s, out, before_t1, before_i1, *ffn_w[1])
    home, got, folded, weighed = weigh(
        ("tu1", "td1", "iu1", "id1"), home, away, low3, out, hidden_t1, bg_t, hidden_i1, bg_i
    )
    other = grid.to_near(folded)

    text3 = give(["tu1", "td1"], width, "y")
    steps(text3, also=weighed)

    g, low = normal_back(g, (home, got, other), stored2, 2, (weighed, text3.got))
    out = pair(low)
    dqkv_t, dqkv_i, home, away = self_back(s, out, *self_w, id_col, id_row, sqkv_t, sqkv_i, size, heads)
    home, got, folded, weighed = weigh(
        ("tsi", "tso", "isi", "iso"), home, away, low2, out, sctx_t, dqkv_t, sctx_i, dqkv_i
    )
    other = grid.to_near(folded)
    grads["tso"] = grads["tso"][: size * heads]
    text2 = give(["tsi", "isi", "tso"], width, "x")
    text3.next(folded)
    text2.next(weighed)

    g, low = normal_back(g, (home, got, other), stored1, 1, (weighed, text3.got))
    image3 = give(["id1", "iu1", "iso"], s.ki, "y")
    text3.next(low)
    image3.next(low)
    out = pair(low)
    bg_t, bg_i, home, away = ffn_back(s, out, before_t0, before_i0, *ffn_w[0])
    home, got, folded, weighed = weigh(
        ("tu0", "td0", "iu0", "id0"), home, away, low1, out, hidden_t0, bg_t, hidden_i0, bg_i
    )
    other = grid.to_near(folded)
    text1 = give(["tu0", "td0"], width, "y")
    text1.next(weighed)

    g, low = normal_back(g, (home, got, other), stored0, 0, (weighed, text3.got, text2.got, image3.got, text1.got))
    steps(text2, image3, also=low)
    out = pair(low)
    norm_sums = jnp.concatenate(norm_grads)
    moved = grid.to_core(norm_sums)
    dqkv_t, dqkv_i, home, away = co_back(s, out, *co_w, seg_col, segments, qkv_t, qkv_i)
    norm_sums = norm_sums + after(away, moved)
    moved = grid.to_x(norm_sums)
    home, got, folded, weighed = weigh(
        ("tci", "tco", "ici", "ico"), home, away, low0, out, ctx_t, dqkv_t, ctx_i, dqkv_i
    )
    text0 = give(["tci", "ici", "tco"], width)
    image1 = give(["id0", "iu0", "ico"], s.ki, "y")

    other = grid.to_near(after(weighed, folded))
    steps(text0, text2, text1, image1, also=weighed)
    arrived = arrived, other
    norm_sums = norm_sums + after(arrived, moved)
    steps(text0, image1, image3, text1)
    moved = grid.to_y(after(arrived, norm_sums))
    first = Deliver(grid, [text3, text2, image3], widths, arrived)
    steps(text0, image1)
    first.core(arrived)
    norm_sums = norm_sums + after(arrived, moved)
    moved = grid.to_near(norm_sums)
    second = Deliver(grid, [text0, text1, image1], widths, arrived)
    done = first.finish(second.got)
    norm_sums = norm_sums + after(second.got, moved)
    moved = [grid.to_column(norm_sums, k) for k in range(1, 2 * rest)]
    other = after(second.got, other)
    mine = slice(0, s.li + s.tall)
    sums = g[mine] + home[mine] + got[mine].astype(F32)
    sums = sums + jnp.concatenate([other[s.below :], other[s.li + s.tall : s.below]]).astype(F32)
    second.core()
    norm_sums = sum(after(second.got, moved), norm_sums).reshape(4, 4, s.ki)
    done.update(second.finish())
    norm_outs = [
        lax.dynamic_slice(norm_sums[:, i], (0, place * k), (4, k))[None]
        for i, k in enumerate((tw, tw, iw, iw))
    ]

    def both(first, second):
        return jnp.stack([done[first], done[second]])[None]

    return (
        s.unpack_text(last)[None],
        last[: s.li][None],
        s.unpack_text(sums)[None],
        sums[: s.li][None],
        *(done[n][None] for n in ("tci", "tco", "ici", "ico", "tsi", "tso", "isi", "iso")),
        both("tu0", "tu1"),
        both("td0", "td1"),
        both("iu0", "iu1"),
        both("id0", "id1"),
        *norm_outs,
    )


def solution(mesh):
    rest = mesh.shape["wide"] // 16
    fine = Mesh(mesh.devices.reshape(2, 2, rest, 2, 2, mesh.shape["narrow"]), ALL)
    rows = P(ALL, None, None)
    weight = P(None, ALL, None)
    pair = P(None, None, ALL, None)
    norm = P(None, None, ALL)
    return jax.shard_map(
        partial(shards, rest=rest),
        mesh=fine,
        in_specs=(rows, rows, P(ALL, None), *[weight] * 8, *[pair] * 4, *[norm] * 4, rows, rows),
        out_specs=(rows, rows, rows, rows, *[weight] * 8, *[pair] * 4, *[norm] * 4),
        check_vma=False,
    )
```

```python
from functools import partial

import jax
import jax.numpy as jnp
from jax import lax
from jax.experimental import pallas as pl
from jax.experimental.pallas import tpu as pltpu
from jax.sharding import Mesh, PartitionSpec as P

HT = 12
HI = 8
HC = 8
REGIONS = 36
EPS = 1e-06
F32 = jnp.float32
BF16 = jnp.bfloat16
ALL = ("far", "near", "low", "y", "core", "x")
FLIP = ((0, 1), (1, 0))
TEAM = 4
PIECE = 8


class Grid:
    def __init__(self, rest):
        self.rest = rest
        self.far, self.near, self.low, self.y, self.core, self.x = (lax.axis_index(name) for name in ALL)
        self.column = self.far * rest + self.low

    def to_core(self, value):
        return lax.ppermute(value, "core", FLIP)

    def to_x(self, value):
        return lax.ppermute(value, "x", FLIP)

    def to_y(self, value):
        return lax.ppermute(value, "y", FLIP)

    def to_near(self, value):
        return lax.ppermute(value, "near", FLIP)

    def to_column(self, value, step):
        columns = 2 * self.rest
        return lax.ppermute(value, ("far", "low"), [(c, (c + step) % columns) for c in range(columns)])

    def swap_far(self, value):
        return lax.ppermute(value, ("far", "core"), ((0, 0), (1, 2), (2, 1), (3, 3)))


def pick(value, index, axis):
    return lax.dynamic_index_in_dim(value, index, axis, keepdims=False)


def paired(own, other, index, axis):
    own, other = jnp.expand_dims(own, axis), jnp.expand_dims(other, axis)
    shape = list(own.shape)
    shape[axis] = 2
    place = lax.broadcasted_iota(jnp.int32, shape, axis)
    return jnp.where(place == index, own, other)


def joined(values, axis):
    return jnp.concatenate(values, axis) if len(values) > 1 else values[0]


def widen(value, width):
    lack = width - value.shape[-1]
    return jnp.pad(value, [(0, 0)] * (value.ndim - 1) + [(0, lack)]) if lack else value


GROUPS = {"tci": 3, "ici": 3, "tsi": 3, "isi": 3, "tu0": 1, "tu1": 1, "iu0": 1, "iu1": 1}
WIDE = 256


def quarters(w, groups):
    r, n = w.shape
    wide = n // groups // TEAM
    parts = widen(w.reshape(r, groups, TEAM, wide), -(-wide // WIDE) * WIDE)
    return parts.transpose(2, 0, 1, 3).reshape(2, 2, r, groups * parts.shape[3])


def from_quarters(parts, groups, n):
    _, _, r, c = parts.shape
    parts = parts.reshape(TEAM, r, groups, c // groups)[..., : n // groups // TEAM]
    return parts.transpose(1, 2, 0, 3).reshape(r, n)


def trade_ins(grid, parts):
    width = max(p.shape[3] for p in parts)
    lines = joined([widen(p, width) for p in parts], 2)
    got = grid.to_near(pick(lines, 1 - grid.near, 1))
    lines = paired(pick(lines, grid.near, 1), got, grid.near, 1)
    came = grid.to_core(pick(lines, 1 - grid.core, 0))
    lines = paired(pick(lines, grid.core, 0), came, grid.core, 0)
    out, at = [], 0
    for p in parts:
        r, c = p.shape[2:]
        out.append(lines[:, :, at : at + r, :c])
        at += r
    return out, (got, came)


class Bundle:
    def __init__(self, names, width, turn="both"):
        self.names, self.width, self.turn = names, width, turn

    def flat(self, value):
        p, r, c = value.shape[-3:]
        lead = value.shape[:-3]
        if p * c == self.width and p > 1:
            value = jnp.concatenate([value[..., k, :, :] for k in range(p)], -1)
        else:
            value = value.reshape(lead + (p * r, c))
        lack = -value.shape[-2] % PIECE
        if lack:
            value = jnp.pad(value, [(0, 0)] * len(lead) + [(0, lack), (0, 0)])
        return value.reshape(lead + (-1, PIECE, self.width))

    def count(self, shape):
        p, r, c = shape
        return -(-(r if p * c == self.width else p * r) // PIECE)

    def unflat(self, lines, shape):
        p, r, c = shape
        lead = lines.shape[:-3]
        lines = lines.reshape(lead + (-1, self.width))
        if p * c == self.width and p > 1:
            return jnp.stack([lines[..., :r, k * c : (k + 1) * c] for k in range(p)], -3)
        return lines[..., : p * r, :].reshape(lead + (p, r, c))


class Gather:
    def __init__(self, grid, bundles, parts):
        self.grid, self.bundles, self.parts = grid, bundles, parts
        self.blocks, self.sides, self.corners = {}, {}, {}
        self.gate = ()

    def chunk(self, i):
        bundle = self.bundles[i]
        return joined([bundle.flat(self.parts[n]) for n in bundle.names], 0)

    def cut(self, i, n):
        return {"both": n // 2, "x": n, "y": 0}[self.bundles[i].turn]

    def round(self, moves, also=()):
        grid, columns = self.grid, 2 * self.grid.rest
        sends = []
        for kind, i in moves:
            if kind == "z":
                sends.append(self.chunk(i))
            elif kind == "xy":
                sends.append(self.blocks[i])
            else:
                by_x, by_y = self.sides[i]
                cut = self.cut(i, by_x.shape[1])
                sends.append((by_x[:, :cut], by_y[:, cut:]))
        if self.gate or also:
            sends, _ = lax.optimization_barrier((sends, (self.gate, also)))
        self.gate = ()
        for (kind, i), value in zip(moves, sends):
            if kind == "c":
                got = ()
                if value[0].shape[1]:
                    got += (grid.to_y(value[0]),)
                if value[1].shape[1]:
                    got += (grid.to_x(value[1]),)
                self.corners[i] = got
            elif kind == "xy":
                self.blocks[i] = value
                got = self.sides[i] = (grid.to_x(value), grid.to_y(value))
            else:
                got = tuple(grid.to_column(value, k) for k in range(1, columns))
                order = (value, *got)
                places = []
                for place in range(columns):
                    here = order[0]
                    for k in range(1, columns):
                        here = jnp.where((grid.column - place) % columns == k, order[k], here)
                    places.append(here)
                self.blocks[i] = jnp.stack(places)
            self.gate += got

    def full(self, i, gate=None):
        grid, bundle, parts = self.grid, self.bundles[i], self.parts
        corner = joined(self.corners[i] if gate is None else after(gate, self.corners[i]), 1)
        full, at = {}, 0
        for name in bundle.names:
            shape = parts[name].shape
            p, r, c = shape
            n = bundle.count(shape)
            cut = [bundle.unflat(b[:, at : at + n], shape) for b in (self.blocks[i], *self.sides[i], corner)]
            at += n
            if p == TEAM:
                cut = [b.reshape(2, grid.rest, 2, 2, r, c).transpose(0, 3, 1, 2, 4, 5) for b in cut]
                cut = [b[:, :, :, None, :, None] for b in cut]
                place = (3, 5)
            else:
                cut = [b.reshape(2, grid.rest, r, c).swapaxes(0, 1)[:, None, :, None] for b in cut]
                place = (1, 3)
            size = list(cut[0].shape)
            size[place[0]] = size[place[1]] = 2
            here_y = lax.broadcasted_iota(jnp.int32, size, place[0]) == grid.y
            here_x = lax.broadcasted_iota(jnp.int32, size, place[1]) == grid.x
            own, ox, oy, oxy = cut
            value = jnp.where(here_y, jnp.where(here_x, own, ox), jnp.where(here_x, oy, oxy))
            full[name] = lax.optimization_barrier(value).reshape(-1, c)
        return full


def plus(a, *more):
    total = a.astype(F32)
    for b in more:
        total = total + b.astype(F32)
    return total.astype(BF16)


def lay_kernel(core, mine, came, *outs, shapes):
    first = core[0] == 0
    at = 0
    for (r, c, groups, n), out in zip(shapes, outs):
        wide = n // groups // TEAM
        step = c // groups
        for near in range(2):
            a = mine[near, pl.ds(at, r), :].astype(F32)
            b = came[near, pl.ds(at, r), :].astype(F32)
            for k, value in enumerate((jnp.where(first, a, b), jnp.where(first, b, a))):
                for g in range(groups):
                    to = g * (n // groups) + (2 * k + near) * wide
                    out[:, to : to + wide] = value[:, g * step : g * step + wide]
        at += r


def lay_out(core, mine, came, shapes):
    if any(r % 8 for r, _, _, _ in shapes):
        lines, at, outs = paired(mine, came, core, 0), 0, []
        for r, c, groups, n in shapes:
            outs.append(from_quarters(lines[:, :, at : at + r, :c], groups, n).astype(F32))
            at += r
        return outs
    size = 4 * mine.size + sum(4 * r * n for r, _, _, n in shapes)
    return pl.pallas_call(
        partial(lay_kernel, shapes=shapes),
        out_shape=[jax.ShapeDtypeStruct((r, n), F32) for r, _, _, n in shapes],
        in_specs=[pl.BlockSpec(memory_space=pltpu.SMEM)] + [pl.BlockSpec(memory_space=pltpu.VMEM)] * 2,
        compiler_params=pltpu.CompilerParams(vmem_limit_bytes=2 * size + (8 << 20)),
        cost_estimate=pl.CostEstimate(flops=size, bytes_accessed=size, transcendentals=0),
    )(core.astype(jnp.int32).reshape(1), mine, came)


def after(gate, value):
    return lax.optimization_barrier((value, gate))[0]


class Give:
    def __init__(self, grid, bundle, grads):
        self.grid, self.bundle, self.step = grid, bundle, 0
        rest = grid.rest
        self.views, self.shapes = [], []
        for name in bundle.names:
            k, c = grads[name].shape
            if name in GROUPS:
                r = k // (rest * 32)
                self.views.append(grads[name].reshape(2, 2, rest, 2, 2, 2, r, c))
                self.shapes.append((TEAM, r, c))
            else:
                r = k // (rest * 8)
                self.views.append(grads[name].reshape(rest, 2, 2, 2, r, c))
                self.shapes.append((1, r, c))
        self.names = list(bundle.names)

    def block(self, y, x):
        pieces = []
        for view, (p, r, c) in zip(self.views, self.shapes):
            if p == TEAM:
                value = pick(pick(view, x, 5), y, 3).transpose(0, 2, 3, 1, 4, 5)
            else:
                value = pick(pick(view, x, 3), y, 1).swapaxes(0, 1)
            pieces.append(self.bundle.flat(value.reshape(2 * self.grid.rest, p, r, c)))
        return joined(pieces, 1)

    def next(self, gate):
        if self.step:
            self.got = after(gate, self.got)
        else:
            self.views = after(gate, self.views)
        step, self.step = self.step, self.step + 1
        (self.corner, self.side, self.column)[step]()

    def corner(self):
        grid = self.grid
        corner = self.block(1 - grid.y, 1 - grid.x)
        n = corner.shape[1]
        self.cut = {"both": n // 2, "x": 0, "y": n}[self.bundle.turn]
        self.got = ()
        if self.cut:
            self.got += (grid.to_y(corner[:, : self.cut]),)
        if self.cut < n:
            self.got += (grid.to_x(corner[:, self.cut :]),)

    def side(self):
        grid, cut, got = self.grid, self.cut, list(self.got)
        x = self.block(grid.y, 1 - grid.x)
        y = self.block(1 - grid.y, grid.x)
        n = x.shape[1]
        if cut == n:
            x = plus(x, got[0])
        elif cut == 0:
            y = plus(y, got[0])
        else:
            x = jnp.concatenate([plus(x[:, :cut], got[0]), x[:, cut:]], 1)
            y = jnp.concatenate([y[:, :cut], plus(y[:, cut:], got[1])], 1)
        self.got = grid.to_x(x), grid.to_y(y)

    def column(self):
        grid, columns = self.grid, 2 * self.grid.rest
        chunk = plus(self.block(grid.y, grid.x), *self.got)
        self.mine = pick(chunk, grid.column, 0)
        self.got = tuple(
            grid.to_column(pick(chunk, (grid.column + k) % columns, 0), k) for k in range(1, columns)
        )


class Deliver:
    def __init__(self, grid, gives, widths, gate=None):
        self.grid, self.widths = grid, widths
        self.quads, self.outs = [], []
        for give in gives:
            got = give.got if gate is None else after(gate, give.got)
            total, at = plus(give.mine, *got), 0
            for name, shape in zip(give.names, give.shapes):
                n = give.bundle.count(shape)
                part = give.bundle.unflat(total[at : at + n], shape)
                if name in GROUPS:
                    self.quads.append((name, part.reshape((2, 2) + part.shape[1:])))
                else:
                    self.outs.append((name, part[0]))
                at += n
        width = max(q.shape[3] for _, q in self.quads)
        lines = joined([widen(q, width) for _, q in self.quads], 2)
        self.mine, self.came = pick(lines, grid.near, 1), grid.to_near(pick(lines, 1 - grid.near, 1))
        width = max(o.shape[1] for _, o in self.outs)
        self.swapped = grid.swap_far(joined([widen(o, width) for _, o in self.outs], 0))
        self.got = self.came

    def core(self, gate=None):
        grid = self.grid
        came = self.came if gate is None else after(gate, self.came)
        lines = paired(self.mine, came, grid.near, 1)
        self.mine, self.came = pick(lines, grid.core, 0), grid.to_core(pick(lines, 1 - grid.core, 0))
        self.got = self.came

    def finish(self, gate=None):
        came, swapped = self.came, self.swapped
        if gate is not None:
            came, swapped = after(gate, (came, swapped))
        shapes = [(*quad.shape[2:], GROUPS[name], self.widths[name]) for name, quad in self.quads]
        done = dict(zip((n for n, _ in self.quads), lay_out(self.grid.core, self.mine, came, shapes)))
        at = 0
        for name, out in self.outs:
            r, c = out.shape
            done[name] = swapped[at : at + r, :c].astype(F32)
            at += r
        return done


class Sizes:
    def __init__(self, lt, kt, li, ki):
        self.lt, self.kt, self.li, self.ki = lt, kt, li, ki
        self.third, self.tall, self.left = kt // 3, lt * 3 // 4, lt // 4
        self.below = li + 2 * self.tall
        self.rows = self.below + li

    def text(self, ref, r):
        base = self.li + r * self.tall
        top = ref[pl.ds(base, self.tall), : self.kt]
        last = [ref[pl.ds(base + j * self.left, self.left), self.kt :] for j in range(3)]
        return jnp.concatenate([top, jnp.concatenate(last, 1)], 0)

    def put_text(self, ref, r, text):
        base = self.li + r * self.tall
        text = text.astype(ref.dtype)
        ref[pl.ds(base, self.tall), : self.kt] = text[: self.tall]
        for j in range(3):
            block = text[self.tall :, j * self.third : (j + 1) * self.third]
            ref[pl.ds(base + j * self.left, self.left), self.kt :] = block

    def image(self, ref, r=0):
        return ref[pl.ds(r * self.below, self.li), :]

    def put_image(self, ref, image, r=0):
        ref[pl.ds(r * self.below, self.li), :] = image.astype(ref.dtype)

    def pack_rows(self, text, image):
        last = text[self.tall :]
        last = [last[:, j * self.third : (j + 1) * self.third] for j in range(3)]
        return jnp.concatenate([image, jnp.concatenate([text[: self.tall], jnp.concatenate(last, 0)], 1)], 0)

    def unpack_text(self, rows):
        rows = rows[self.li : self.li + self.tall]
        last = [rows[j * self.left : (j + 1) * self.left, self.kt :] for j in range(3)]
        return jnp.concatenate([rows[:, : self.kt], jnp.concatenate(last, 1)], 0)

    def both(self, near, far):
        text = [self.text(ref, r) for ref in (near, far) for r in range(2)]
        image = [self.image(ref, r) for ref in (near, far) for r in range(2)]
        return jnp.concatenate(text, 0), jnp.concatenate(image, 0)

    def put_sums(self, home, away, text, image):
        for r in range(TEAM):
            ref = (home, away)[r // 2]
            self.put_text(ref, r % 2, text[r * self.lt : (r + 1) * self.lt])
            self.put_image(ref, image[r * self.li : (r + 1) * self.li], r % 2)

    def sums(self):
        shape = (self.rows, self.ki)
        return [(shape, F32), (shape, BF16)]


def kernel(body, outs, args, flops, scratch=()):
    outs = [jax.ShapeDtypeStruct(shape, kind) for shape, kind in outs]
    size = sum(a.size * a.dtype.itemsize for a in (*args, *outs))
    return pl.pallas_call(
        body,
        out_shape=outs,
        scratch_shapes=[pltpu.VMEM(shape, kind) for shape, kind in scratch],
        compiler_params=pltpu.CompilerParams(vmem_limit_bytes=int(1.25 * size) + (14 << 20)),
        cost_estimate=pl.CostEstimate(flops=flops, bytes_accessed=size, transcendentals=0),
    )(*args)


def mm(a, b):
    return jnp.dot(a, b, preferred_element_type=F32)


def mm_bt(a, b):
    return lax.dot_general(a, b, (((1,), (1,)), ((), ())), preferred_element_type=F32)


def mm_at(a, b):
    return lax.dot_general(a, b, (((0,), (0,)), ((), ())), preferred_element_type=F32)


def gelu(v):
    return 0.5 * v * (1.0 + lax.erf(v * (0.5**0.5)))


def gelu_slope(v):
    return 0.5 * (1.0 + lax.erf(v * (0.5**0.5))) + v * jnp.exp(-0.5 * v * v) * (0.5 / jnp.pi) ** 0.5


def ffn_kernel(near, far, ut, dt, ui, di, before_t, hidden_t, before_i, hidden_i, home, away, *, s):
    text, image = s.both(near, far)
    sums = []
    for low, up, down, before, hidden in (
        (text, ut, dt, before_t, hidden_t),
        (image, ui, di, before_i, hidden_i),
    ):
        pre = mm(low, up[...])
        before[...] = pre
        act = gelu(pre).astype(BF16)
        hidden[...] = act
        sums.append(mm(act, down[...]))
    s.put_sums(home, away, *sums)


def ffn(s, low, ut, dt, ui, di):
    ft, fi = ut.shape[1], ui.shape[1]
    outs = []
    for length, f in ((TEAM * s.lt, ft), (TEAM * s.li, fi)):
        outs += [((length, f), F32), ((length, f), BF16)]
    flops = 16 * (s.lt * s.kt * ft + s.li * s.ki * fi)
    return kernel(partial(ffn_kernel, s=s), outs + s.sums(), (*low, ut, dt, ui, di), flops)


def ffn_back_kernel(near, far, before_t, before_i, ut, dt, ui, di, bg_t, bg_i, home, away, *, s):
    text, image = s.both(near, far)
    sums = []
    for out, before, up, down, bg in (
        (text, before_t, ut, dt, bg_t),
        (image, before_i, ui, di, bg_i),
    ):
        grad = (mm_bt(out, down[...]) * gelu_slope(before[...])).astype(BF16)
        bg[...] = grad
        sums.append(mm_bt(grad, up[...]))
    s.put_sums(home, away, *sums)


def ffn_back(s, out, before_t, before_i, ut, dt, ui, di):
    ft, fi = ut.shape[1], ui.shape[1]
    outs = [((TEAM * s.lt, ft), BF16), ((TEAM * s.li, fi), BF16)] + s.sums()
    flops = 16 * (s.lt * s.kt * ft + s.li * s.ki * fi)
    args = (*out, before_t, before_i, ut, dt, ui, di)
    return kernel(partial(ffn_back_kernel, s=s), outs, args, flops)


def softmax_of(q, k, allowed, factor):
    scores = jnp.where(allowed, mm_bt(q, k) * factor, -1e30)
    exponent = jnp.exp(scores - jnp.max(scores, -1, keepdims=True))
    return exponent / jnp.sum(exponent, -1, keepdims=True)


def head_back(q, k, v, grad, allowed, factor):
    probs = softmax_of(q, k, allowed, factor)
    dv = mm_at(probs.astype(BF16), grad)
    dp = mm_bt(grad, v)
    ds = (probs * (dp - jnp.sum(dp * probs, -1, keepdims=True))).astype(BF16)
    return mm(ds, k) * factor, mm_at(ds, q) * factor, dv


LANES = 128


def lane_part(size, sub):
    lane = lax.broadcasted_iota(jnp.int32, (1, LANES), 1)
    return jnp.logical_and(lane >= sub * size, lane < (sub + 1) * size)


def half_ids(length):
    col = lax.broadcasted_iota(jnp.int32, (length, 1), 0) >= length // 2
    row = lax.broadcasted_iota(jnp.int32, (1, length), 1) >= length // 2
    return col, row


def thirds(tile, wide):
    return [pl.ds(i * wide + tile * LANES, LANES) for i in range(3)]


def image_places(s):
    for r in range(TEAM):
        yield pl.ds(r * s.li, s.li)


def self_kernel(near, far, wt, wot, wi, woi, col, row, qkv_t, ctx_t, qkv_i, ctx_i, home, away, *, s, size, heads):
    text, image = s.both(near, far)
    qkv_t[...] = mm(text, wt[...]).astype(BF16)
    qkv_i[...] = mm(image, wi[...]).astype(BF16)
    wide = ctx_t.shape[1]
    allowed = col[...] == row[...]
    for tile in range(wide // LANES):
        q, k, v = (qkv_t[:, at] for at in thirds(tile, wide))
        total = jnp.zeros(q.shape, F32)
        for sub in range(min(LANES // size, heads - tile * (LANES // size))):
            lanes = lane_part(size, sub)
            probs = softmax_of(jnp.where(lanes, q, 0), k, allowed, size**-0.5)
            total = total + jnp.where(lanes, mm(probs.astype(BF16), v), 0.0)
        ctx_t[:, pl.ds(tile * LANES, LANES)] = total.astype(BF16)
    wide = ctx_i.shape[1]
    own, other = half_ids(s.li)
    for at in image_places(s):
        for tile in range(wide // LANES):
            q, k, v = (qkv_i[at, lanes] for lanes in thirds(tile, wide))
            probs = softmax_of(q, k, own == other, LANES**-0.5)
            ctx_i[at, pl.ds(tile * LANES, LANES)] = mm(probs.astype(BF16), v).astype(BF16)
    s.put_sums(home, away, mm(ctx_t[...], wot[...]), mm(ctx_i[...], woi[...]))


def attention_outs(s, wt, wi):
    outs = []
    for length, n in ((s.lt, wt.shape[1]), (s.li, wi.shape[1])):
        outs += [((TEAM * length, n), BF16), ((TEAM * length, n // 3), BF16)]
    return outs


def attention_flops(s, wt, wi):
    return 12 * (s.lt * s.kt * wt.shape[1] + s.li * s.ki * wi.shape[1])


def self_attention(s, low, wt, wot, wi, woi, col, row, size, heads):
    outs = attention_outs(s, wt, wi) + s.sums()
    args = (*low, wt, wot, wi, woi, col, row)
    return kernel(partial(self_kernel, s=s, size=size, heads=heads), outs, args, attention_flops(s, wt, wi))


def self_back_kernel(
    near, far, wt, wot, wi, woi, col, row, qkv_t, qkv_i, dqkv_t, dqkv_i, home, away, dctx_t, dctx_i, *, s, size, heads
):
    text, image = s.both(near, far)
    dctx_t[...] = mm_bt(text, wot[...]).astype(BF16)
    dctx_i[...] = mm_bt(image, woi[...]).astype(BF16)
    wide = dctx_t.shape[1]
    allowed = col[...] == row[...]
    for tile in range(wide // LANES):
        q, k, v = (qkv_t[:, at] for at in thirds(tile, wide))
        grad = dctx_t[:, pl.ds(tile * LANES, LANES)]
        totals = [jnp.zeros(q.shape, F32) for _ in range(3)]
        for sub in range(min(LANES // size, heads - tile * (LANES // size))):
            lanes = lane_part(size, sub)
            dq, dk, dv = head_back(
                jnp.where(lanes, q, 0), k, v, jnp.where(lanes, grad, 0), allowed, size**-0.5
            )
            totals = [totals[0] + jnp.where(lanes, dq, 0.0), totals[1] + dk, totals[2] + dv]
        for at, total in zip(thirds(tile, wide), totals):
            dqkv_t[:, at] = total.astype(BF16)
    wide = dctx_i.shape[1]
    own, other = half_ids(s.li)
    for at in image_places(s):
        for tile in range(wide // LANES):
            columns = thirds(tile, wide)
            q, k, v = (qkv_i[at, lanes] for lanes in columns)
            grad = dctx_i[at, pl.ds(tile * LANES, LANES)]
            grads = head_back(q, k, v, grad, own == other, LANES**-0.5)
            for lanes, value in zip(columns, grads):
                dqkv_i[at, lanes] = value.astype(BF16)
    s.put_sums(home, away, mm_bt(dqkv_t[...], wt[...]), mm_bt(dqkv_i[...], wi[...]))


def back_outs(s, wt, wi):
    outs = [((TEAM * s.lt, wt.shape[1]), BF16), ((TEAM * s.li, wi.shape[1]), BF16)] + s.sums()
    scratch = [((TEAM * s.lt, wt.shape[1] // 3), BF16), ((TEAM * s.li, wi.shape[1] // 3), BF16)]
    return outs, scratch


def self_back(s, out, wt, wot, wi, woi, col, row, qkv_t, qkv_i, size, heads):
    outs, scratch = back_outs(s, wt, wi)
    args = (*out, wt, wot, wi, woi, col, row, qkv_t, qkv_i)
    body = partial(self_back_kernel, s=s, size=size, heads=heads)
    return kernel(body, outs, args, attention_flops(s, wt, wi), scratch)


def co_places(s, seg_col, seg_row):
    col, row = half_ids(s.li)
    for r in range(TEAM):
        text, image = pl.ds(r * s.lt, s.lt), pl.ds(r * s.li, s.li)
        text_col = seg_col[text, :] > 0.5
        text_row = seg_row[pl.ds(r, 1), :] > 0.5
        yield text, image, text_col == row, col == text_row


def co_kernel(
    near, far, wt, wot, wi, woi, seg_col, seg_row, qkv_t, ctx_t, qkv_i, ctx_i, home, away, *, s
):
    text, image = s.both(near, far)
    qkv_t[...] = mm(text, wt[...]).astype(BF16)
    qkv_i[...] = mm(image, wi[...]).astype(BF16)
    wide = ctx_t.shape[1]
    for text, image, cross, back in co_places(s, seg_col, seg_row):
        for tile in range(wide // LANES):
            q, k, v = thirds(tile, wide)
            probs = softmax_of(qkv_t[text, q], qkv_i[image, k], cross, LANES**-0.5)
            ctx_t[text, q] = mm(probs.astype(BF16), qkv_i[image, v]).astype(BF16)
            probs = softmax_of(qkv_i[image, q], qkv_t[text, k], back, LANES**-0.5)
            ctx_i[image, q] = mm(probs.astype(BF16), qkv_t[text, v]).astype(BF16)
    s.put_sums(home, away, mm(ctx_t[...], wot[...]), mm(ctx_i[...], woi[...]))


def co_attention(s, low, wt, wot, wi, woi, seg_col, seg_row):
    outs = attention_outs(s, wt, wi) + s.sums()
    args = (*low, wt, wot, wi, woi, seg_col, seg_row)
    return kernel(partial(co_kernel, s=s), outs, args, attention_flops(s, wt, wi))


def co_back_kernel(
    near, far, wt, wot, wi, woi, seg_col, seg_row, qkv_t, qkv_i, dqkv_t, dqkv_i, home, away, dctx_t, dctx_i, *, s
):
    text, image = s.both(near, far)
    dctx_t[...] = mm_bt(text, wot[...]).astype(BF16)
    dctx_i[...] = mm_bt(image, woi[...]).astype(BF16)
    wide = dctx_t.shape[1]
    for text, image, cross, back in co_places(s, seg_col, seg_row):
        for tile in range(wide // LANES):
            q, k, v = thirds(tile, wide)
            dq, dk, dv = head_back(
                qkv_t[text, q], qkv_i[image, k], qkv_i[image, v], dctx_t[text, q], cross, LANES**-0.5
            )
            dqkv_t[text, q] = dq.astype(BF16)
            dqkv_i[image, k] = dk.astype(BF16)
            dqkv_i[image, v] = dv.astype(BF16)
            dq, dk, dv = head_back(
                qkv_i[image, q], qkv_t[text, k], qkv_t[text, v], dctx_i[image, q], back, LANES**-0.5
            )
            dqkv_i[image, q] = dq.astype(BF16)
            dqkv_t[text, k] = dk.astype(BF16)
            dqkv_t[text, v] = dv.astype(BF16)
    s.put_sums(home, away, mm_bt(dqkv_t[...], wt[...]), mm_bt(dqkv_i[...], wi[...]))


def co_back(s, out, wt, wot, wi, woi, seg_col, seg_row, qkv_t, qkv_i):
    outs, scratch = back_outs(s, wt, wi)
    args = (*out, wt, wot, wi, woi, seg_col, seg_row, qkv_t, qkv_i)
    return kernel(partial(co_back_kernel, s=s), outs, args, attention_flops(s, wt, wi), scratch)


def weight_kernel(near, far, out_near, out_far, mid_t, grad_t, mid_i, grad_i, in_t, out_t, in_i, out_i, *, s):
    text, image = s.both(near, far)
    in_t[...] = mm_at(text, grad_t[...]).astype(BF16)
    in_i[...] = mm_at(image, grad_i[...]).astype(BF16)
    text, image = s.both(out_near, out_far)
    out_t[...] = mm_at(mid_t[...], text).astype(BF16)
    out_i[...] = mm_at(mid_i[...], image).astype(BF16)


def weight_grads(s, low, out, mid_t, grad_t, mid_i, grad_i):
    outs = []
    for k, mid, grad in ((s.kt, mid_t, grad_t), (s.ki, mid_i, grad_i)):
        outs += [((k, grad.shape[1]), BF16), ((mid.shape[1], k), BF16)]
    flops = sum(8 * s.lt * shape[0] * shape[1] for shape, _ in outs)
    args = (*low, *out, mid_t, grad_t, mid_i, grad_i)
    return kernel(partial(weight_kernel, s=s), outs, args, flops)


def fold_kernel(home, got, out):
    out[...] = (home[...] + got[...].astype(F32)).astype(BF16)


def fold(s, home, got):
    return kernel(fold_kernel, [((s.rows, s.ki), BF16)], (home, got), home.size)[0]


def settled(read, base, home, got, other, r):
    return read(base, r).astype(F32) + read(home, r) + read(got, r).astype(F32) + read(other, 1 - r).astype(F32)


def streams(s, params, i, k):
    return (
        (s.text, lambda ref, r, v: s.put_text(ref, r, v), params[pl.ds(4 * k + i, 1), : s.kt], 2 * s.li, s.lt),
        (s.image, lambda ref, r, v: s.put_image(ref, v, r), params[pl.ds(8 + 4 * k + i, 1), :], 0, s.li),
    )


def norm_kernel(values, home, got, other, params, out, low, normed, inverse, *, s, i):
    for (read, put, gain, start, length), (_, _, shift, _, _) in zip(streams(s, params, i, 0), streams(s, params, i, 1)):
        for r in range(2):
            v = settled(read, values, home, got, other, r)
            centred = v - jnp.mean(v, -1, keepdims=True)
            inv = lax.rsqrt(jnp.mean(centred * centred, -1, keepdims=True) + EPS)
            n = centred * inv
            inverse[pl.ds(start + r * length, length), :] = inv
            y = n * gain + shift
            for ref, value in ((normed, n), (out, y), (low, y)):
                put(ref, r, value)


def norm(s, values, sums, params, i):
    pack = (s.rows, s.ki)
    outs = [(pack, F32), (pack, BF16), (pack, F32), ((2 * s.li + 2 * s.lt, 1), F32)]
    y, low, *stored = kernel(partial(norm_kernel, s=s, i=i), outs, (values, *sums, params), 32 * s.rows * s.ki)
    return y, low, stored


def norm_back_kernel(*refs, s, i, first):
    if first:
        up, normed, inverse, params, grad, low, sums = refs
    else:
        up, home, got, other, normed, inverse, params, grad, low, sums = refs
    sums[...] = jnp.zeros(sums.shape, F32)
    for stream, (read, put, gain, start, length) in enumerate(streams(s, params, i, 0)):
        for r in range(2):
            u = read(up, r).astype(F32) if first else settled(read, up, home, got, other, r)
            n = read(normed, r)
            scaled = u * gain
            value = inverse[pl.ds(start + r * length, length), :] * (
                scaled - jnp.mean(scaled, -1, keepdims=True) - n * jnp.mean(scaled * n, -1, keepdims=True)
            )
            put(grad, r, value)
            put(low, r, value)
            if r == 0:
                width = u.shape[1]
                sums[pl.ds(2 * stream, 1), :width] = jnp.sum(u * n, axis=0, keepdims=True)
                sums[pl.ds(2 * stream + 1, 1), :width] = jnp.sum(u, axis=0, keepdims=True)


def norm_back(s, upstream, sums, stored, params, i):
    pack = (s.rows, s.ki)
    outs = [(pack, F32), (pack, BF16), ((4, s.ki), F32)]
    body = partial(norm_back_kernel, s=s, i=i, first=sums is None)
    return kernel(body, outs, (upstream, *(sums or ()), *stored, params), 32 * s.rows * s.ki)


FETCH = (
    Bundle(["tci", "ici", "tco", "icoa", "icob"], 768),
    Bundle(["id0", "iu0", "iso"], 1024, "x"),
    Bundle(["tu0", "td0"], 768),
    Bundle(["tsi", "isi", "tso"], 768, "x"),
    Bundle(["id1", "iu1"], 1024, "y"),
    Bundle(["tu1", "td1"], 768, "y"),
)


def shards(
    text_in,
    image_in,
    text_segments,
    text_co_in,
    text_co_out,
    image_co_in,
    image_co_out,
    text_self_in,
    text_self_out,
    image_self_in,
    image_self_out,
    text_up,
    text_down,
    image_up,
    image_down,
    text_gains,
    text_shifts,
    image_gains,
    image_shifts,
    grad_text_out,
    grad_image_out,
    rest,
):
    grid = Grid(rest)
    tw, iw = text_gains.shape[2], image_gains.shape[2]
    s = Sizes(*text_in.shape[1:], *image_in.shape[1:])
    weights = {
        "tci": text_co_in[0],
        "tco": text_co_out[0],
        "ici": image_co_in[0],
        "ico": image_co_out[0],
        "tsi": text_self_in[0],
        "tso": text_self_out[0],
        "isi": image_self_in[0],
        "iso": image_self_out[0],
        "tu0": text_up[0, 0],
        "tu1": text_up[0, 1],
        "td0": text_down[0, 0],
        "td1": text_down[0, 1],
        "iu0": image_up[0, 0],
        "iu1": image_up[0, 1],
        "id0": image_down[0, 0],
        "id1": image_down[0, 1],
    }

    weights["icoa"] = image_co_out[0][:, : FETCH[0].width]
    weights["icob"] = widen(image_co_out[0][:, FETCH[0].width :], FETCH[0].width)
    place = ((((grid.far * 2 + grid.near) * rest + grid.low) * 2 + grid.y) * 2 + grid.core) * 2 + grid.x
    params = jnp.zeros((16, s.ki), BF16)
    for at, k, kinds in ((0, tw, (text_gains, text_shifts)), (8, iw, (image_gains, image_shifts))):
        own = jnp.concatenate([a[0] for a in kinds])
        params = lax.dynamic_update_slice(params, own, (at, place * k))
    width = FETCH[0].width
    widths = {name: weights[name].shape[1] for name in GROUPS}
    quads = {name: quarters(weights[name], groups) for name, groups in GROUPS.items()}
    parts = {}

    def trade(names):
        got, _ = trade_ins(grid, [quads[n] for n in names])
        for n, q in zip(names, got):
            parts[n] = q.reshape((TEAM,) + q.shape[2:])

    def swap(names):
        swapped, at = grid.swap_far(joined([weights[n] for n in names], 0)), 0
        for n in names:
            r = weights[n].shape[0]
            parts[n] = swapped[at : at + r][None]
            at += r

    def pair(own):
        return own, grid.to_core(own)

    trade(("tci", "ici"))
    swap(("tco", "icoa", "icob"))
    segments = text_segments.astype(F32)
    segments = jnp.concatenate(pair(jnp.concatenate([segments, grid.to_near(segments)])))
    params = params + grid.to_x(params)
    params = params + grid.to_y(params)
    params = params + grid.to_core(params)

    def more(move):
        nonlocal params, moved
        params = params + after(fetch.gate, moved)
        moved = move(params)

    fetch = Gather(grid, FETCH, parts)
    moved = grid.to_near(params)
    fetch.round([("z", 0)])

    def later(ins, outs, *inputs):
        new = {n: quads[n] for n in ins}, {n: weights[n] for n in sum(outs, ())}, inputs
        new_quads, new_weights, inputs = after(fetch.gate, new)
        quads.update(new_quads)
        weights.update(new_weights)
        trade(ins)
        for names in outs:
            swap(names)
        return inputs

    text_in, image_in = later(
        ("iu0", "tu0", "tsi", "isi", "iu1", "tu1"), (("id0", "iso", "id1"), ("td0", "tso", "td1")), text_in, image_in
    )
    own = s.pack_rows(text_in[0], image_in[0])
    got = grid.to_near(own)
    values = jnp.concatenate([own, got[s.li :], got[: s.li]])
    low0 = pair(values)
    fetch.round([("xy", 0)])

    seg_col = segments.reshape(-1, 1)
    ids = segments + 2.0 * jnp.arange(TEAM, dtype=F32)[:, None]
    id_col, id_row = ids.reshape(-1, 1), ids.reshape(1, -1)
    size, heads = s.kt // HT, HT // TEAM

    def settle(home, away):
        got = grid.to_core(away)
        return home, got, grid.to_near(fold(s, home, got))

    def normal(values, sums, i):
        return norm(s, values, sums, params, i)

    more(lambda value: sum((grid.to_column(value, k) for k in range(2, 2 * rest)), grid.to_column(value, 1)))
    fetch.round([("c", 0), ("z", 1)])
    params = (params + after(fetch.gate, moved)).astype(F32)
    grad_text_out, grad_image_out = after(fetch.gate, (grad_text_out, grad_image_out))
    own = s.pack_rows(grad_text_out[0], grad_image_out[0])
    got = grid.to_near(own)
    upstream = jnp.concatenate([own, got[s.li :], got[: s.li]])
    full = fetch.full(0)
    full["ico"] = jnp.concatenate([full["icoa"], full["icob"][:, : s.ki - width]], 1)
    co_w = [full[n] for n in ("tci", "tco", "ici", "ico")]
    fetch.round([("xy", 1), ("z", 2)])
    qkv_t, ctx_t, qkv_i, ctx_i, home, away = co_attention(s, low0, *co_w, seg_col, segments)
    fetch.round([("c", 1), ("xy", 2), ("z", 3)], away)
    sums = settle(home, away)
    full.update(fetch.full(1, sums[1]))
    y, low, stored0 = normal(values, sums, 0)
    low1 = pair(low)
    fetch.round([("c", 2), ("xy", 3), ("z", 4)], sums[1])
    full.update(fetch.full(2, low))
    ffn_w = [[full["tu0"], full["td0"], full["iu0"], full["id0"]]]
    before_t0, hidden_t0, before_i0, hidden_i0, home, away = ffn(s, low1, *ffn_w[0])
    fetch.round([("c", 3), ("xy", 4), ("z", 5)], low)
    full.update(fetch.full(3, away))
    full["tso"] = jnp.pad(full["tso"], ((0, full["tsi"].shape[1] // 3 - full["tso"].shape[0]), (0, 0)))
    self_w = [full[n] for n in ("tsi", "tso", "isi", "iso")]
    fetch.round([("c", 4), ("xy", 5)], away)
    y, low, stored1 = normal(y, settle(home, away), 1)
    low2 = pair(low)
    sqkv_t, sctx_t, sqkv_i, sctx_i, home, away = self_attention(s, low2, *self_w, id_col, id_row, size, heads)
    fetch.round([("c", 5)], low)
    full.update(fetch.full(4, away))
    sums = settle(home, away)
    full.update(fetch.full(5, sums[1]))
    ffn_w.append([full["tu1"], full["td1"], full["iu1"], full["id1"]])
    y, low, stored2 = normal(y, sums, 2)
    low3 = pair(low)
    before_t1, hidden_t1, before_i1, hidden_i1, home, away = ffn(s, low3, *ffn_w[1])
    _, last, stored3 = normal(y, settle(home, away), 3)

    grads, norm_grads = {}, [None] * 4

    def normal_back(upstream, sums, stored, i, due=None):
        grad, low, norm_grads[i] = norm_back(s, upstream, sums, stored, params, i)
        return grad, low if due is None else after(due, low)

    def weigh(names, home, away, low, out, *mids, due=None):
        got = grid.to_core(away)
        if due is not None:
            got = after(due, got)
        folded = fold(s, home, got)
        low, out, mids = after(folded, (low, out, mids))
        values = weight_grads(s, low, out, *mids)
        grads.update(zip(names, values))
        return home, got, folded, values[0]

    def give(names, wide, turn="both"):
        return Give(grid, Bundle(names, wide, turn), grads)

    arrived = ()

    def steps(*gives, also=()):
        nonlocal arrived
        gate = arrived, also
        for each in gives:
            each.next(gate)
        arrived = tuple(each.got for each in gives)

    g, low = normal_back(upstream, None, stored3, 3)
    out = pair(low)
    bg_t, bg_i, home, away = ffn_back(s, out, before_t1, before_i1, *ffn_w[1])
    home, got, folded, weighed = weigh(
        ("tu1", "td1", "iu1", "id1"), home, away, low3, out, hidden_t1, bg_t, hidden_i1, bg_i
    )
    other = grid.to_near(folded)

    text3 = give(["tu1", "td1"], width, "y")
    steps(text3, also=weighed)

    g, low = normal_back(g, (home, got, other), stored2, 2, (weighed, text3.got))
    out = pair(low)
    dqkv_t, dqkv_i, home, away = self_back(s, out, *self_w, id_col, id_row, sqkv_t, sqkv_i, size, heads)
    home, got, folded, weighed = weigh(
        ("tsi", "tso", "isi", "iso"), home, away, low2, out, sctx_t, dqkv_t, sctx_i, dqkv_i
    )
    other = grid.to_near(folded)
    grads["tso"] = grads["tso"][: size * heads]
    text2 = give(["tsi", "isi", "tso"], width, "x")
    text3.next(folded)
    text2.next(weighed)

    g, low = normal_back(g, (home, got, other), stored1, 1, (weighed, text3.got))
    image3 = give(["id1", "iu1", "iso"], s.ki, "y")
    text3.next(low)
    image3.next(low)
    out = pair(low)
    bg_t, bg_i, home, away = ffn_back(s, out, before_t0, before_i0, *ffn_w[0])
    home, got, folded, weighed = weigh(
        ("tu0", "td0", "iu0", "id0"), home, away, low1, out, hidden_t0, bg_t, hidden_i0, bg_i
    )
    other = grid.to_near(folded)
    text1 = give(["tu0", "td0"], width, "y")
    text1.next(weighed)

    g, low = normal_back(g, (home, got, other), stored0, 0, (weighed, text3.got, text2.got, image3.got, text1.got))
    steps(text2, image3, also=low)
    out = pair(low)
    norm_sums = jnp.concatenate(norm_grads)
    moved = grid.to_core(norm_sums)
    dqkv_t, dqkv_i, home, away = co_back(s, out, *co_w, seg_col, segments, qkv_t, qkv_i)
    norm_sums = norm_sums + after(away, moved)
    moved = grid.to_x(norm_sums)
    home, got, folded, weighed = weigh(
        ("tci", "tco", "ici", "ico"), home, away, low0, out, ctx_t, dqkv_t, ctx_i, dqkv_i
    )
    text0 = give(["tci", "ici", "tco"], width)
    image1 = give(["id0", "iu0", "ico"], s.ki, "y")

    other = grid.to_near(after(weighed, folded))
    steps(text0, text2, text1, image1, also=weighed)
    arrived = arrived, other
    norm_sums = norm_sums + after(arrived, moved)
    steps(text0, image1, image3, text1)
    moved = grid.to_y(after(arrived, norm_sums))
    first = Deliver(grid, [text3, text2, image3], widths, arrived)
    steps(text0, image1)
    first.core(arrived)
    norm_sums = norm_sums + after(arrived, moved)
    moved = grid.to_near(norm_sums)
    second = Deliver(grid, [text0, text1, image1], widths, arrived)
    done = first.finish(second.got)
    norm_sums = norm_sums + after(second.got, moved)
    moved = [grid.to_column(norm_sums, k) for k in range(1, 2 * rest)]
    other = after(second.got, other)
    mine = slice(0, s.li + s.tall)
    sums = g[mine] + home[mine] + got[mine].astype(F32)
    sums = sums + jnp.concatenate([other[s.below :], other[s.li + s.tall : s.below]]).astype(F32)
    second.core()
    norm_sums = sum(after(second.got, moved), norm_sums).reshape(4, 4, s.ki)
    done.update(second.finish())
    norm_outs = [
        lax.dynamic_slice(norm_sums[:, i], (0, place * k), (4, k))[None]
        for i, k in enumerate((tw, tw, iw, iw))
    ]

    def both(first, second):
        return jnp.stack([done[first], done[second]])[None]

    return (
        s.unpack_text(last)[None],
        last[: s.li][None],
        s.unpack_text(sums)[None],
        sums[: s.li][None],
        *(done[n][None] for n in ("tci", "tco", "ici", "ico", "tsi", "tso", "isi", "iso")),
        both("tu0", "tu1"),
        both("td0", "td1"),
        both("iu0", "iu1"),
        both("id0", "id1"),
        *norm_outs,
    )


def solution(mesh):
    rest = mesh.shape["wide"] // 16
    fine = Mesh(mesh.devices.reshape(2, 2, rest, 2, 2, mesh.shape["narrow"]), ALL)
    rows = P(ALL, None, None)
    weight = P(None, ALL, None)
    pair = P(None, None, ALL, None)
    norm = P(None, None, ALL)
    return jax.shard_map(
        partial(shards, rest=rest),
        mesh=fine,
        in_specs=(rows, rows, P(ALL, None), *[weight] * 8, *[pair] * 4, *[norm] * 4, rows, rows),
        out_specs=(rows, rows, rows, rows, *[weight] * 8, *[pair] * 4, *[norm] * 4),
        check_vma=False,
    )
```
